32 devices in a mesh: gx: 8 (over y, x, core), col: 4 (over z).
Axes of the slice: x: 2, y: 2, z: 4, core: 2. Of those that a mesh axis runs over, the one named last changes fastest.
Arguments:
- resid: float32 [8, 4, 32, 1024], P('gx', 'col'), may hold values from -6 to 6
- direction: float32 [8, 4, 32, 1024], P('gx', 'col'), may hold values from -6 to 6
- rz_prev: float32 [32], replicated, may hold values from 10922 to 49152
- schur: bfloat16 [8, 4, 1024, 1024], P('gx', 'col'), may hold values from -1 to 4
- neumann: bfloat16 [8, 4, 1024, 1024], P('gx', 'col'), may hold values from -1 to 4
- basis: bfloat16 [8, 4, 1024, 20], P('gx', 'col'), may hold values from -0.375 to 0.375
- coarse_inv: bfloat16 [4, 8, 20, 8, 4, 20], P('col', None, None, 'gx'), may hold values from -1 to 4
- conduct: float32 [8, 4], replicated, may hold values from 0.01 to 100
- face_perm: int32 [8, 4, 8], P('gx', 'col'), may hold values from 0 to 7, each once within a row
Outputs:
- resid_next: float32 [8, 4, 32, 1024], P('gx', 'col')
- direction_next: float32 [8, 4, 32, 1024], P('gx', 'col')
- rz_next: float32 [32], replicated
The draws below stay inside these ranges and needn't reach their ends.
All inputs are finite; a program needn't handle non-finite values.
Results may differ from the reference program's by a relative error of at most 0.018.
Values may be sent and summed in bfloat16 or wider, within the bound.
No kernel may reach another device: no remote copies, remote signals or barrier semaphores. Data moves between devices by JAX's collectives and lax.ppermute only.
A program may use at most 64 MiB of HBM per device.

```python
import math
import jax
import jax.numpy as jnp
from jax import lax

NG = 1024
BLK = 128
NBLK = 8
PRIM = 20
RHS = 32
SLABS = 8
SECTORS = 4


def add_diagonal(off_part, diag_mask, diag_key, diag_shape, low_end, high_end):
    diag_values = jax.random.uniform(diag_key, diag_shape, jnp.float32, low_end, high_end)
    return off_part + jnp.where(diag_mask, diag_values, 0.0)


def rough_field(sub_key, full_shape):
    return jnp.clip(jax.random.normal(sub_key, full_shape, jnp.float32), -6.0, 6.0)


def draw_schur(key, part):
    key = jax.random.fold_in(key, 11)
    key_off, key_diag = jax.random.split(key)
    full_shape = (SLABS, SECTORS, NG, NG)
    spread_scale = 0.3 / math.sqrt(NG)
    rough = rough_field(key_off, full_shape)
    diag_mask = jnp.arange(NG)[:, None] == jnp.arange(NG)[None, :]
    return add_diagonal(rough * spread_scale, diag_mask, key_diag, (SLABS, SECTORS, 1, NG), 1.0, 3.0).astype(jnp.bfloat16)


def draw_neumann(key, part):
    key = jax.random.fold_in(key, 12)
    key_off, key_diag = jax.random.split(key)
    full_shape = (SLABS, SECTORS, NG, NG)
    spread_scale = 0.3 / math.sqrt(NG)
    rough = rough_field(key_off, full_shape)
    diag_mask = jnp.arange(NG)[:, None] == jnp.arange(NG)[None, :]
    return add_diagonal(rough * spread_scale, diag_mask, key_diag, (SLABS, SECTORS, 1, NG), 0.5, 2.0).astype(jnp.bfloat16)


def draw_coarse_inv(key, part):
    key = jax.random.fold_in(key, 13)
    key_off, key_diag, key_band = jax.random.split(key, 3)
    full_shape = (SECTORS, SLABS, PRIM, SLABS, SECTORS, PRIM)
    spread_scale = 0.3 / math.sqrt(PRIM * SLABS * SECTORS)
    band_scale = 1.0 / math.sqrt(PRIM * SLABS)
    rough = rough_field(key_off, full_shape)
    band = rough_field(key_band, full_shape)
    sector_a = jnp.arange(SECTORS).reshape(SECTORS, 1, 1, 1, 1, 1)
    sector_b = jnp.arange(SECTORS).reshape(1, 1, 1, 1, SECTORS, 1)
    slab_a = jnp.arange(SLABS).reshape(1, SLABS, 1, 1, 1, 1)
    slab_b = jnp.arange(SLABS).reshape(1, 1, 1, SLABS, 1, 1)
    prim_a = jnp.arange(PRIM).reshape(1, 1, PRIM, 1, 1, 1)
    prim_b = jnp.arange(PRIM).reshape(1, 1, 1, 1, 1, PRIM)
    diag_mask = (sector_a == sector_b) & (slab_a == slab_b) & (prim_a == prim_b)
    opposite = sector_b == (sector_a + SECTORS // 2) % SECTORS
    off_part = rough * spread_scale + jnp.where(opposite, band * band_scale, 0.0)
    return add_diagonal(off_part, diag_mask, key_diag, (SECTORS, SLABS, PRIM, 1, 1, 1), 1.0, 2.0).astype(jnp.bfloat16)


def level_of(own_key, extent, cuts, least, top_value):
    gain = 1.0
    for dim, parts in cuts:
        draws = jax.random.uniform(jax.random.fold_in(jax.random.fold_in(own_key, 6), dim), (parts,), jnp.float32, least / len(cuts), top_value / len(cuts))
        gain = gain * jnp.repeat(jnp.exp(draws), extent[dim] // parts).reshape((-1,) + (1,) * (len(extent) - 1 - dim))
    return gain


def scatter_about(stream_key, shape, deviation, reach, shards=(), kind=jnp.bfloat16):
    drawn = jax.random.normal(stream_key, shape, jnp.float32) * deviation
    if len(shards) > 0:
        drawn = level_of(stream_key, shape, shards, -0.22, 0.18) * drawn
    return jnp.clip(drawn, min=-reach, max=reach).astype(kind)


def setup_inputs(seed: int = 0) -> dict:
    keys = jax.random.split(jax.random.key(seed), 10)
    resid = scatter_about(keys[0], (SLABS, SECTORS, RHS, NG), 1.0, 6.0, ((0, 8), (1, 4)), jnp.float32)
    direction = scatter_about(keys[1], (SLABS, SECTORS, RHS, NG), 1.0, 6.0, ((0, 8), (1, 4)), jnp.float32)
    rz_prev = jnp.clip(jnp.exp(jax.random.uniform(keys[2], (RHS,), jnp.float32, math.log(10922.0), math.log(49152.0))), 10922.0, 49152.0)
    schur = draw_schur(jax.random.fold_in(keys[9], 71), 0)
    neumann = draw_neumann(jax.random.fold_in(keys[9], 71), 0)
    basis = scatter_about(keys[5], (SLABS, SECTORS, NG, PRIM), (NG // 4) ** -0.5, 0.375, ((0, 8), (1, 4)))
    coarse_inv = draw_coarse_inv(jax.random.fold_in(keys[9], 71), 0)
    conduct = jnp.clip(jnp.exp(jax.random.uniform(keys[7], (SLABS, SECTORS), jnp.float32, math.log(0.01), math.log(100.0))), 0.01, 100.0)
    face_perm = jax.vmap(lambda own: jax.random.permutation(own, NBLK))(jax.random.split(keys[8], SLABS * SECTORS)).reshape((SLABS, SECTORS, NBLK)).astype(jnp.int32)
    return {"resid": resid, "direction": direction, "rz_prev": rz_prev, "schur": schur, "neumann": neumann, "basis": basis, "coarse_inv": coarse_inv, "conduct": conduct, "face_perm": face_perm}


def inverse_perm(face_perm):
    return jnp.argsort(face_perm, axis=-1).astype(jnp.int32)


def to_slots(values, face_perm):
    blocks = values.reshape(values.shape[0], values.shape[1], values.shape[2], NBLK, BLK)
    return jnp.take_along_axis(blocks, face_perm[:, :, None, :, None], axis=3)


def from_slots(slotted, face_perm):
    blocks = jnp.take_along_axis(slotted, inverse_perm(face_perm)[:, :, None, :, None], axis=3)
    return blocks.reshape(blocks.shape[0], blocks.shape[1], blocks.shape[2], NBLK * BLK)


def face_sum(values, face_perm):
    slotted = to_slots(values, face_perm)
    per_face = NBLK // 4
    lower_face = slotted[:, :, :, 0:per_face]
    upper_face = slotted[:, :, :, per_face:2 * per_face]
    prev_face = slotted[:, :, :, 2 * per_face:3 * per_face]
    next_face = slotted[:, :, :, 3 * per_face:]
    from_below = jnp.concatenate([jnp.zeros_like(upper_face[:1]), upper_face[:-1]], axis=0)
    from_above = jnp.concatenate([lower_face[1:], jnp.zeros_like(lower_face[:1])], axis=0)
    from_left = jnp.roll(next_face, 1, axis=1)
    from_right = jnp.roll(prev_face, -1, axis=1)
    received = jnp.concatenate([from_below, from_above, from_left, from_right], axis=3)
    return values + from_slots(received, face_perm)


def block_weights(conduct, face_perm):
    zero_row = jnp.zeros_like(conduct[:1])
    below_side = jnp.concatenate([zero_row, conduct[:-1]], axis=0)
    above_side = jnp.concatenate([conduct[1:], zero_row], axis=0)
    left_side = jnp.roll(conduct, 1, axis=1)
    right_side = jnp.roll(conduct, -1, axis=1)
    others = jnp.stack([below_side, above_side, left_side, right_side], axis=2)
    face_weight = conduct[:, :, None] / (conduct[:, :, None] + others)
    slot_weight = jnp.repeat(face_weight, NBLK // 4, axis=2)
    per_block = jnp.take_along_axis(slot_weight, inverse_perm(face_perm), axis=2)
    return jnp.repeat(per_block, BLK, axis=2)[:, :, None, :]


def batched_dot(left_side, right_side):
    count = left_side.shape[0] * left_side.shape[1]
    flat_left = left_side.reshape((count,) + left_side.shape[2:])
    flat_right = right_side.reshape((count,) + right_side.shape[2:])

    def one_pair(pair):
        return jnp.dot(pair[0], pair[1], preferred_element_type=jnp.float32)

    result = lax.map(one_pair, (flat_left, flat_right))
    return result.reshape(left_side.shape[:2] + result.shape[1:])


def reference(resid, direction, rz_prev, schur, neumann, basis, coarse_inv, conduct, face_perm):
    highest = lax.Precision.HIGHEST
    weight = block_weights(conduct, face_perm)
    image_part = batched_dot(direction.astype(jnp.bfloat16), schur)
    curvature = jnp.sum(direction * image_part, axis=(0, 1, 3))
    step_len = rz_prev / curvature
    resid_next = resid - step_len[None, None, :, None] * face_sum(image_part, face_perm)
    scaled = weight * resid_next
    scaled_b = scaled.astype(jnp.bfloat16)
    coarse_rhs = batched_dot(scaled_b, basis).astype(jnp.bfloat16)
    coarse_sol = jnp.einsum('cgkhdl,hdrl->gcrk', coarse_inv.astype(jnp.float32), coarse_rhs.astype(jnp.float32), precision=highest).astype(jnp.bfloat16)
    correction = jnp.einsum('gcrk,gcnk->gcrn', coarse_sol.astype(jnp.float32), basis.astype(jnp.float32), precision=highest)
    local_sol = batched_dot(scaled_b, neumann) + correction
    rz_next = jnp.sum(scaled * local_sol, axis=(0, 1, 3))
    precond = face_sum(weight * local_sol, face_perm)
    direction_next = precond + (rz_next / rz_prev)[None, None, :, None] * direction
    return resid_next, direction_next, rz_next
```

```python
import functools

import jax
import jax.numpy as jnp
from jax import lax
from jax.experimental import pallas as pl
from jax.experimental.pallas import tpu as pltpu
from jax.sharding import PartitionSpec as P

F32 = jnp.float32
BF16 = jnp.bfloat16
BLK = 128
EXACT = lax.Precision.HIGHEST
SMEM = pltpu.SMEM
VMEM = pltpu.VMEM


def params():
    return pltpu.CompilerParams(vmem_limit_bytes=16 * 1024 * 1024)


def cost(flops, nbytes):
    return pl.CostEstimate(flops=flops, bytes_accessed=nbytes, transcendentals=0)


def swap(value, axis, offset):
    count = lax.axis_size(axis)
    pairs = []
    for low in range(offset, count, 2):
        high = (low + 1) % count
        pairs += [(low, high), (high, low)]
    return lax.ppermute(value, axis, pairs)


def swap_faces(faces):
    return (
        swap(faces[0], "gx", 0),
        swap(faces[1], "gx", 1),
        swap(faces[2], "col", 0),
        swap(faces[3], "col", 1),
    )


def swapped_faces():
    slab = lax.axis_index("gx") % 2
    sector = lax.axis_index("col") % 2
    return (1 - slab, slab, 3 - sector, 2 + sector)


def swap_counts():
    slab = lax.axis_index("gx")
    inside = jnp.logical_and(slab > 0, slab < lax.axis_size("gx") - 1)
    return (None, inside, None, None)


def block_at(perm_ref, slot):
    return pl.ds(pl.multiple_of(perm_ref[slot] * BLK, BLK), BLK)


def put_faces(perm_ref, source, outs):
    for face, out in zip(swapped_faces(), outs):
        for j in range(2):
            out[:, j * BLK : (j + 1) * BLK] = source[:, block_at(perm_ref, 2 * face + j)].astype(BF16)


def add_faces(perm_ref, target, received):
    for face, counts, got in zip(swapped_faces(), swap_counts(), received):
        for j in range(2):
            part = got[:, j * BLK : (j + 1) * BLK].astype(F32)
            if counts is not None:
                part = jnp.where(counts, part, 0.0)
            at = block_at(perm_ref, 2 * face + j)
            target[:, at] = target[:, at] + part


def to_column(row):
    n = row.shape[1]
    at = lax.broadcasted_iota(jnp.int32, (n, n), 0) == lax.broadcasted_iota(jnp.int32, (n, n), 1)
    return jnp.sum(jnp.where(at, row, 0.0), axis=1, keepdims=True)


def to_row(column):
    n = column.shape[0]
    at = lax.broadcasted_iota(jnp.int32, (n, n), 0) == lax.broadcasted_iota(jnp.int32, (n, n), 1)
    return jnp.sum(jnp.where(at, column, 0.0), axis=0, keepdims=True)


def image_kernel(perm_ref, dir_ref, schur_ref, image_ref, *faces):
    image_ref[...] = jnp.dot(dir_ref[...].astype(BF16), schur_ref[...], preferred_element_type=F32)
    put_faces(perm_ref, image_ref, faces)


def early_kernel(perm_ref, conduct_ref, dir_ref, image_ref, resid_ref, basis_ref, neumann_ref,
                 weight_ref, rhs_ref, curv_ref, sol_ref):
    slab, sector = lax.axis_index("gx"), lax.axis_index("col")
    slabs, sectors = lax.axis_size("gx"), lax.axis_size("col")
    own = conduct_ref[slab, sector]
    below = jnp.where(slab > 0, conduct_ref[jnp.maximum(slab - 1, 0), sector], 0.0)
    above = jnp.where(slab < slabs - 1, conduct_ref[jnp.minimum(slab + 1, slabs - 1), sector], 0.0)
    left = conduct_ref[slab, (sector + sectors - 1) % sectors]
    right = conduct_ref[slab, (sector + 1) % sectors]
    for face, other in enumerate((below, above, left, right)):
        across = jnp.full((8, BLK), own, F32) / jnp.full((8, BLK), own + other, F32)
        for j in range(2):
            weight_ref[:, block_at(perm_ref, 2 * face + j)] = across
    scaled = (weight_ref[0:1, :] * resid_ref[...]).astype(BF16)
    rhs_ref[...] = lax.dot_general(
        basis_ref[...], scaled, (((1,), (1,)), ((), ())), preferred_element_type=F32
    )
    curv = to_row(jnp.sum(dir_ref[...] * image_ref[...], axis=1, keepdims=True))
    high = curv.astype(BF16)
    low = (curv - high.astype(F32)).astype(BF16)
    curv_ref[...] = jnp.zeros_like(curv_ref)
    n = curv.shape[1]
    curv_ref[0:1, 0:n] = high.astype(F32)
    curv_ref[0:1, n : 2 * n] = low.astype(F32)
    sol_ref[...] = jnp.dot(scaled, neumann_ref[...], preferred_element_type=F32)


def coarse_rhs_kernel(perm_ref, image_ref, r0, r1, r2, r3, weight_ref, basis_ref, rhs_ref, curv_ref,
                      assembled_ref, scaled_ref, out_ref):
    assembled_ref[...] = image_ref[...]
    add_faces(perm_ref, assembled_ref, (r0, r1, r2, r3))
    scaled = (weight_ref[0:1, :] * assembled_ref[...]).astype(BF16)
    scaled_ref[...] = scaled
    rhs_q = lax.dot_general(
        basis_ref[...], scaled, (((1,), (1,)), ((), ())), preferred_element_type=F32
    )
    rhs_r = rhs_ref[...]
    half = rhs_r.shape[0] // 2
    rows = out_ref.shape[1]
    packed = jnp.concatenate([rhs_r[:half], rhs_q[:half], rhs_r[half:], rhs_q[half:]], axis=1)
    packed = jnp.concatenate(
        [packed, curv_ref[0:1, :], jnp.zeros((rows - half - 1, BLK), F32)], axis=0
    ).astype(BF16)
    for i in range(out_ref.shape[0]):
        out_ref[i] = packed


def neumann_kernel(scaled_ref, neumann_ref, out_ref):
    out_ref[...] = jnp.dot(scaled_ref[...], neumann_ref[...], preferred_element_type=F32)


def solve_kernel(prim, perm_ref, gathered_ref, coarse_ref, rz_ref, resid_ref, assembled_ref,
                 weight_ref, basis_ref, sol_r_ref, sol_q_ref,
                 resid_out, weighted_out, rz_out, *faces):
    blocks, rows, depth = coarse_ref.shape
    total = jnp.zeros((rows, BLK), F32)
    per = gathered_ref.shape[0] // blocks
    for h in range(blocks):
        part = gathered_ref[h * per : (h + 1) * per].reshape(depth, BLK)
        total = total + jnp.dot(coarse_ref[h], part, preferred_element_type=F32)
    n = rz_ref.shape[1]
    second = (rows - 8) // 2
    curvature = total[2 * second : 2 * second + 1, 0:n] + total[2 * second : 2 * second + 1, n : 2 * n]
    step = rz_ref[...] / curvature
    sol_r = total[0:prim, 0:n] + total[second : second + prim, 2 * n : 3 * n]
    sol_q = total[0:prim, n : 2 * n] + total[second : second + prim, 3 * n : 4 * n]
    coarse_sol = (sol_r - step * sol_q).astype(BF16)
    correction = lax.dot_general(
        coarse_sol, basis_ref[...], (((0,), (0,)), ((), ())), preferred_element_type=F32
    )
    step_col = to_column(step)
    weight = weight_ref[0:1, :]
    resid_new = resid_ref[...] - step_col * assembled_ref[...]
    resid_out[...] = resid_new
    local = sol_r_ref[...] - step_col * sol_q_ref[...] + correction
    weighted = weight * local
    weighted_out[...] = weighted
    put_faces(perm_ref, weighted_out, faces)
    partial = to_row(jnp.sum(resid_new * weighted, axis=1, keepdims=True))
    partial = jnp.concatenate([partial, jnp.zeros((1, BLK - n), F32)], axis=1)
    for i in range(rz_out.shape[0]):
        rz_out[i] = partial


def direction_kernel(perm_ref, partials_ref, rz_ref, dir_ref, weighted_ref, r0, r1, r2, r3,
                     out_ref, rz_out):
    n = rz_ref.shape[1]
    rz_next = jnp.sum(partials_ref[...], axis=0)[:, 0:n]
    rz_out[...] = rz_next
    out_ref[...] = weighted_ref[...] + to_column(rz_next / rz_ref[...]) * dir_ref[...]
    add_faces(perm_ref, out_ref, (r0, r1, r2, r3))


def coarse_blocks(coarse_inv, rows):
    slabs, prim, _, sectors, _ = coarse_inv.shape
    half = prim // 2
    up = -(-prim // 8) * 8
    own = coarse_inv[:, :, 0]
    first = jnp.pad(own[..., :half], ((0, 0), (0, up - prim), (0, 0), (0, rows - half)))
    second = jnp.pad(own[..., half:], ((0, 0), (0, up - prim), (0, 0), (0, rows - half)))
    last = jnp.zeros((slabs, 8, sectors, rows), coarse_inv.dtype).at[:, 0, :, half].set(1)
    return jnp.concatenate([first, second, last], axis=1).reshape(slabs, 2 * up + 8, sectors * rows)


def body(resid, direction, rz_prev, schur, neumann, basis, coarse_inv, conduct, face_perm):
    resid, direction, schur, neumann = resid[0, 0], direction[0, 0], schur[0, 0], neumann[0, 0]
    basis_t = basis[0, 0].T
    perm = face_perm[0, 0]
    rhs, width = resid.shape
    prim = basis_t.shape[0]
    count = lax.axis_size("gx") * lax.axis_size("col")
    rows = -(-(prim // 2 + 1) // 16) * 16
    face = jax.ShapeDtypeStruct((rhs, 2 * BLK), BF16)
    full = jax.ShapeDtypeStruct((rhs, width), F32)
    rz_row = rz_prev[None, :]
    smem = pl.BlockSpec(memory_space=SMEM)
    vmem = pl.BlockSpec(memory_space=VMEM)
    flops = 2 * rhs * width * width

    coarse = lax.all_to_all(coarse_blocks(coarse_inv[0], rows), "gx", 0, 0)

    image, *faces = pl.pallas_call(
        image_kernel, out_shape=(full,) + (face,) * 4, in_specs=[smem, vmem, vmem],
        out_specs=(vmem,) * 5, compiler_params=params(), cost_estimate=cost(flops, 2 * width * width),
    )(perm, direction, schur)
    received = swap_faces(faces)
    weight, rhs_r, curv, sol_r = pl.pallas_call(
        early_kernel,
        out_shape=(
            jax.ShapeDtypeStruct((8, width), F32),
            jax.ShapeDtypeStruct((prim, rhs), F32),
            jax.ShapeDtypeStruct((8, BLK), F32),
            full,
        ),
        in_specs=[smem, smem] + [vmem] * 5, out_specs=(vmem,) * 4, compiler_params=params(),
        cost_estimate=cost(flops, 2 * width * width),
    )(perm, conduct, direction, image, resid, basis_t, neumann)
    assembled, scaled_q, packed = pl.pallas_call(
        coarse_rhs_kernel,
        out_shape=(
            full,
            jax.ShapeDtypeStruct((rhs, width), BF16),
            jax.ShapeDtypeStruct((count, rows, BLK), BF16),
        ),
        in_specs=[smem] + [vmem] * 9, out_specs=(vmem,) * 3, compiler_params=params(),
        cost_estimate=cost(2 * rhs * width * prim, 8 * rhs * width),
    )(perm, image, *received, weight, basis_t, rhs_r, curv)
    gathered = lax.all_to_all(packed, ("gx", "col"), 0, 0)
    sol_q = pl.pallas_call(
        neumann_kernel, out_shape=full, in_specs=[vmem] * 2, out_specs=vmem,
        compiler_params=params(), cost_estimate=cost(flops, 2 * width * width),
    )(scaled_q, neumann)
    resid_new, weighted, partial, *faces = pl.pallas_call(
        functools.partial(solve_kernel, prim),
        out_shape=(full, full, jax.ShapeDtypeStruct((count, 1, BLK), F32)) + (face,) * 4,
        in_specs=[smem] + [vmem] * 9, out_specs=(vmem,) * 7, compiler_params=params(),
        cost_estimate=cost(2 * rhs * width * prim, 8 * rhs * width),
    )(perm, gathered, coarse, rz_row, resid, assembled, weight, basis_t, sol_r, sol_q)
    partials = lax.all_to_all(partial, ("gx", "col"), 0, 0)
    received = swap_faces(faces)
    direction_new, rz_next = pl.pallas_call(
        direction_kernel, out_shape=(full, jax.ShapeDtypeStruct((1, rhs), F32)),
        in_specs=[smem] + [vmem] * 8, out_specs=(vmem,) * 2, compiler_params=params(),
        cost_estimate=cost(2 * rhs * width, 8 * rhs * width),
    )(perm, partials, rz_row, direction, weighted, *received)
    return (resid_new[None, None], direction_new[None, None], rz_next[0])


def solution(mesh):
    placed = (
        P("gx", "col", None, None),
        P("gx", "col", None, None),
        P(),
        P("gx", "col", None, None),
        P("gx", "col", None, None),
        P("gx", "col", None, None),
        P("col", None, None, "gx", None, None),
        P(),
        P("gx", "col", None),
    )
    return jax.shard_map(
        body,
        mesh=mesh,
        in_specs=placed,
        out_specs=(P("gx", "col", None, None), P("gx", "col", None, None), P()),
        check_vma=False,
    )
```

```python
import functools

import jax
import jax.numpy as jnp
from jax import lax
from jax.experimental import pallas as pl
from jax.experimental.pallas import tpu as pltpu
from jax.sharding import PartitionSpec as P

F32 = jnp.float32
BF16 = jnp.bfloat16
BLK = 128
EXACT = lax.Precision.HIGHEST
VMEM = pltpu.VMEM


def params(limit=16 * 1024 * 1024):
    return pltpu.CompilerParams(vmem_limit_bytes=limit)


def cost(flops, nbytes):
    return pl.CostEstimate(flops=flops, bytes_accessed=nbytes, transcendentals=0)


def swap(value, axis, offset):
    count = lax.axis_size(axis)
    pairs = []
    for low in range(offset, count, 2):
        high = (low + 1) % count
        pairs += [(low, high), (high, low)]
    return lax.ppermute(value, axis, pairs)


def swap_faces(faces):
    return (
        swap(faces[0], "col", 1),
        swap(faces[1], "col", 0),
        swap(faces[2], "gx", 1),
        swap(faces[3], "gx", 0),
    )


def swap_counts():
    slab = lax.axis_index("gx")
    inside = jnp.logical_and(slab > 0, slab < lax.axis_size("gx") - 1)
    return (None, None, inside, None)


def slot_place(perm_ref, slot):
    return jnp.broadcast_to(perm_ref[0:1, slot : slot + 1], (1, BLK))


def swapped_places(perm_ref):
    slab = lax.axis_index("gx") % 2
    sector = lax.axis_index("col") % 2
    places = []
    for parity, even, odd in ((sector, 2, 3), (sector, 3, 2), (slab, 0, 1), (slab, 1, 0)):
        for j in range(2):
            at_even, at_odd = (slot_place(perm_ref, 2 * face + j) for face in (even, odd))
            places.append(jnp.where(parity == 0, at_even, at_odd))
    return places


def put_faces(perm_ref, source, outs):
    blocks = [source[:, b * BLK : (b + 1) * BLK] for b in range(source.shape[1] // BLK)]
    for i, place in enumerate(swapped_places(perm_ref)):
        chosen = blocks[0]
        for b in range(1, len(blocks)):
            chosen = jnp.where(place == b, blocks[b], chosen)
        j = i % 2
        outs[i // 2][:, j * BLK : (j + 1) * BLK] = chosen.astype(BF16)


def received_blocks(perm_ref, received, blocks):
    places = swapped_places(perm_ref)
    parts = []
    for i in range(len(places)):
        j = i % 2
        part = received[i // 2][:, j * BLK : (j + 1) * BLK].astype(F32)
        counts = swap_counts()[i // 2]
        parts.append(part if counts is None else jnp.where(counts, part, 0.0))
    for b in range(blocks):
        chosen = parts[0]
        for place, part in zip(places[1:], parts[1:]):
            chosen = jnp.where(place == b, part, chosen)
        yield slice(b * BLK, (b + 1) * BLK), chosen


def to_column(row):
    n = row.shape[1]
    at = lax.broadcasted_iota(jnp.int32, (n, n), 0) == lax.broadcasted_iota(jnp.int32, (n, n), 1)
    return jnp.sum(jnp.where(at, row, 0.0), axis=1, keepdims=True)


def to_row(column):
    n = column.shape[0]
    at = lax.broadcasted_iota(jnp.int32, (n, n), 0) == lax.broadcasted_iota(jnp.int32, (n, n), 1)
    return jnp.sum(jnp.where(at, column, 0.0), axis=0, keepdims=True)


CHUNKS = 4


def other_block(i, k):
    mine = (lax.axis_index("gx") >> k) % 2
    return ((i >> k) << (k + 1)) + (i & ((1 << k) - 1)) + ((1 - mine) << k)


def swap_bit(value, k):
    count = lax.axis_size("gx")
    return lax.ppermute(value, "gx", [(i, i ^ (1 << k)) for i in range(count)])


def image_kernel(perm_hbm, dir_hbm, schur_hbm, resid_hbm, basis_hbm, coarse_hbm,
                 image_ref, f0, f1, f2, f3, send_ref, dir_ref, resid_ref, basis_ref, coarse_ref, perm_ref,
                 schur_ref, sems):
    rows = schur_ref.shape[0] // CHUNKS
    parts = [pl.ds(i * rows, rows) for i in range(CHUNKS)]
    pairs = [(dir_hbm, dir_ref), (perm_hbm, perm_ref)]
    pairs += [(schur_hbm.at[part], schur_ref.at[part]) for part in parts]
    pairs += [(coarse_hbm.at[other_block(i, 0)], send_ref.at[i]) for i in range(send_ref.shape[0])]
    pairs += [(resid_hbm, resid_ref), (basis_hbm, basis_ref), (coarse_hbm, coarse_ref)]
    copies = [pltpu.make_async_copy(source, target, sems.at[i]) for i, (source, target) in enumerate(pairs)]
    for copy in copies:
        copy.start()
    copies[0].wait()
    total = None
    for i, part in enumerate(parts):
        copies[2 + i].wait()
        term = jnp.dot(dir_ref[:, part].astype(BF16), schur_ref[part], preferred_element_type=F32)
        total = term if total is None else total + term
    image_ref[...] = total
    copies[1].wait()
    put_faces(perm_ref, total, (f0, f1, f2, f3))
    for copy in copies[2 + CHUNKS :]:
        copy.wait()


def merge_kernel(k, last, blocks_ref, got_ref, out_ref, *send_ref):
    out_ref[...] = blocks_ref[...]
    for i in range(got_ref.shape[0]):
        out_ref[other_block(i, k)] = got_ref[i]
    if not last:
        for i in range(got_ref.shape[0]):
            send_ref[0][i] = out_ref[other_block(i, k + 1)]


def spread_kernel(matrix_ref, blocks_ref):
    slabs, rows, _ = blocks_ref.shape
    prim = matrix_ref.shape[0] // slabs
    half = prim // 2
    sectors = matrix_ref.shape[1] // prim
    width = blocks_ref.shape[2] // 2
    depth = width // sectors
    source = lax.broadcasted_iota(jnp.int32, (sectors * prim, 2 * width), 0)
    place = lax.broadcasted_iota(jnp.int32, (sectors * prim, 2 * width), 1)
    later = place // width
    within = place % width
    sector, at = within // depth, within % depth
    chosen = jnp.logical_and(at < half, source == sector * prim + later * half + at)
    spread = jnp.dot(matrix_ref[...], jnp.where(chosen, 1.0, 0.0).astype(BF16), preferred_element_type=F32)
    empty = jnp.zeros((rows - prim, 2 * width), F32)
    for g in range(slabs):
        own = jnp.concatenate([spread[g * prim : (g + 1) * prim], empty], axis=0)
        blocks_ref[g] = own.astype(BF16)


def conduct_at(row, sector):
    lane = lax.broadcasted_iota(jnp.int32, row.shape, 1)
    return jnp.sum(jnp.where(lane == sector, row, 0.0), axis=1, keepdims=True)


def early_kernel(perm_ref, conduct_ref, dir_ref, image_ref, resid_ref, basis_ref,
                 weight_ref, rhs_ref, curv_ref, scaled_ref):
    slab, sector = lax.axis_index("gx"), lax.axis_index("col")
    slabs, sectors = lax.axis_size("gx"), lax.axis_size("col")
    row = conduct_ref[pl.ds(slab, 1), :]
    own = conduct_at(row, sector)
    below = conduct_at(conduct_ref[pl.ds(jnp.maximum(slab - 1, 0), 1), :], sector)
    above = conduct_at(conduct_ref[pl.ds(jnp.minimum(slab + 1, slabs - 1), 1), :], sector)
    below = jnp.where(slab > 0, below, 0.0)
    above = jnp.where(slab < slabs - 1, above, 0.0)
    left = conduct_at(row, (sector + sectors - 1) % sectors)
    right = conduct_at(row, (sector + 1) % sectors)
    across = [jnp.broadcast_to(own / (own + other), (1, BLK)) for other in (below, above, left, right)]
    places = [slot_place(perm_ref, slot) for slot in range(8)]
    for b in range(weight_ref.shape[1] // BLK):
        weight = across[0]
        for slot in range(2, 8):
            weight = jnp.where(places[slot] == b, across[slot // 2], weight)
        weight_ref[:, b * BLK : (b + 1) * BLK] = jnp.broadcast_to(weight, (8, BLK))
    scaled = (weight_ref[0:1, :] * resid_ref[...]).astype(BF16)
    scaled_ref[...] = scaled
    rhs_ref[...] = lax.dot_general(
        basis_ref[...], scaled, (((1,), (1,)), ((), ())), preferred_element_type=F32
    )
    curv = to_row(jnp.sum(dir_ref[...] * image_ref[...], axis=1, keepdims=True))
    high = curv.astype(BF16).astype(F32)
    n = curv.shape[1]
    curv_ref[...] = jnp.zeros_like(curv_ref)
    curv_ref[0:1, 0:n] = high
    curv_ref[0:1, n : 2 * n] = curv - high


def coarse_rhs_kernel(perm_ref, image_ref, r0, r1, r2, r3, weight_ref, basis_ref, rhs_ref, curv_ref,
                      assembled_ref, scaled_ref, out_ref):
    for at, part in received_blocks(perm_ref, (r0, r1, r2, r3), image_ref.shape[1] // BLK):
        assembled_ref[:, at] = image_ref[:, at] + part
    scaled = (weight_ref[0:1, :] * assembled_ref[...]).astype(BF16)
    scaled_ref[...] = scaled
    rhs_q = lax.dot_general(
        basis_ref[...], scaled, (((1,), (1,)), ((), ())), preferred_element_type=F32
    )
    rhs_r = rhs_ref[...]
    half = rhs_r.shape[0] // 2
    rows = out_ref.shape[1]
    packed = jnp.concatenate([rhs_r[:half], rhs_q[:half], rhs_r[half:], rhs_q[half:]], axis=1)
    packed = jnp.concatenate(
        [packed, curv_ref[0:1, :], jnp.zeros((rows - half - 1, BLK), F32)], axis=0
    ).astype(BF16)
    for i in range(out_ref.shape[0]):
        out_ref[i] = packed


def neumann_kernel(scaled_r_ref, scaled_q_ref, neumann_ref, sol_r_ref, sol_q_ref):
    sol_r_ref[...] = jnp.dot(scaled_r_ref[...], neumann_ref[...], preferred_element_type=F32)
    sol_q_ref[...] = jnp.dot(scaled_q_ref[...], neumann_ref[...], preferred_element_type=F32)


def solve_kernel(perm_ref, gathered_ref, blocks_ref, rz_ref, resid_ref, assembled_ref, weight_ref,
                 basis_ref, sol_r_ref, sol_q_ref, step_out, weighted_out, rz_out, *faces):
    n = rz_ref.shape[1]
    prim = basis_ref.shape[0]
    slabs, _, width = blocks_ref.shape
    width = width // 2
    sectors = gathered_ref.shape[0] // slabs
    depth = gathered_ref.shape[1]
    total = None
    for h in range(slabs):
        part = gathered_ref[h * sectors : (h + 1) * sectors].reshape(width, 4 * n)
        halves = jnp.concatenate([part[:, : 2 * n], part[:, 2 * n :]], axis=0)
        term = jnp.dot(blocks_ref[h], halves, preferred_element_type=F32)
        total = term if total is None else total + term
    everything = gathered_ref[...].reshape(slabs * width, 4 * n)
    at = lax.broadcasted_iota(jnp.int32, (16, slabs * width), 1) % depth
    picks = jnp.where(at == prim // 2, 1.0, 0.0).astype(BF16)
    sums = jnp.dot(picks, everything, preferred_element_type=F32)
    step = rz_ref[...] / (sums[0:1, 0:n] + sums[0:1, n : 2 * n])
    coarse_sol = (total[0:prim, 0:n] - step * total[0:prim, n : 2 * n]).astype(BF16)
    correction = lax.dot_general(
        coarse_sol, basis_ref[...], (((0,), (0,)), ((), ())), preferred_element_type=F32
    )
    step_col = to_column(step)
    step_out[...] = jnp.broadcast_to(step_col, step_out.shape)
    resid_new = resid_ref[...] - step_col * assembled_ref[...]
    local = sol_r_ref[...] - step_col * sol_q_ref[...] + correction
    weighted = weight_ref[0:1, :] * local
    weighted_out[...] = weighted
    put_faces(perm_ref, weighted, faces)
    partial = to_row(jnp.sum(resid_new * weighted, axis=1, keepdims=True))
    partial = jnp.concatenate([partial, jnp.zeros((1, BLK - n), F32)], axis=1)
    for i in range(rz_out.shape[0]):
        rz_out[i] = partial


def resid_kernel(step_ref, resid_ref, assembled_ref, out_ref):
    out_ref[...] = resid_ref[...] - step_ref[:, 0:1] * assembled_ref[...]


def direction_kernel(perm_ref, partials_ref, rz_ref, dir_ref, weighted_ref, r0, r1, r2, r3,
                     out_ref, rz_out):
    n = rz_ref.shape[1]
    rz_next = jnp.sum(partials_ref[...], axis=0)[:, 0:n]
    rz_out[...] = rz_next
    factor = to_column(rz_next / rz_ref[...])
    for at, part in received_blocks(perm_ref, (r0, r1, r2, r3), dir_ref.shape[1] // BLK):
        out_ref[:, at] = weighted_ref[:, at] + factor * dir_ref[:, at] + part


def body(resid, direction, rz_prev, schur, neumann, basis, coarse_inv, conduct, face_perm):
    resid, direction, schur, neumann = resid[0, 0], direction[0, 0], schur[0, 0], neumann[0, 0]
    basis_t = basis[0, 0].T
    perm = face_perm[0]
    rhs, width = resid.shape
    prim = basis_t.shape[0]
    slabs, sectors = lax.axis_size("gx"), lax.axis_size("col")
    rows = -(-(prim // 2 + 1) // 16) * 16
    block_rows = -(-prim // 16) * 16
    rounds = slabs.bit_length() - 1
    face = jax.ShapeDtypeStruct((rhs, 2 * BLK), BF16)
    full = jax.ShapeDtypeStruct((rhs, width), F32)
    rz_row = rz_prev[None, :]
    vmem = pl.BlockSpec(memory_space=VMEM)
    hbm = pl.BlockSpec(memory_space=pltpu.HBM)
    flops = 2 * rhs * width * width
    coarse = coarse_inv[0, :, :, 0]
    coarse_type = jax.ShapeDtypeStruct(coarse.shape, BF16)
    send_type = jax.ShapeDtypeStruct((slabs // 2,) + coarse.shape[1:], BF16)
    blocks_type = jax.ShapeDtypeStruct((slabs, block_rows, 2 * sectors * rows), BF16)

    fetched = [pltpu.with_memory_space_constraint(x, pltpu.HBM) for x in (perm, direction, schur, resid, basis_t, coarse)]
    image, f0, f1, f2, f3, send, direction, resid, basis_t, coarse = pl.pallas_call(
        image_kernel,
        out_shape=(full,) + (face,) * 4
        + (send_type, full, full, jax.ShapeDtypeStruct((prim, width), BF16), coarse_type),
        in_specs=[hbm] * 6, out_specs=(vmem,) * 10,
        scratch_shapes=[
            pltpu.VMEM(perm.shape, jnp.int32),
            pltpu.VMEM((width, width), BF16),
            pltpu.SemaphoreType.DMA((CHUNKS + 5 + slabs // 2,)),
        ],
        compiler_params=params(), cost_estimate=cost(flops, 2 * width * width),
    )(*fetched)
    received = swap_faces((f0, f1, f2, f3))
    weight, rhs_r, curv, scaled_r = pl.pallas_call(
        early_kernel,
        out_shape=(
            jax.ShapeDtypeStruct((8, width), F32),
            jax.ShapeDtypeStruct((prim, rhs), F32),
            jax.ShapeDtypeStruct((8, BLK), F32),
            jax.ShapeDtypeStruct((rhs, width), BF16),
        ),
        in_specs=[vmem] * 6, out_specs=(vmem,) * 4, compiler_params=params(),
        cost_estimate=cost(2 * rhs * width * prim, 8 * rhs * width),
    )(perm, conduct, direction, image, resid, basis_t)
    for k in range(rounds):
        got = swap_bit(send, k)
        last = k + 1 == rounds
        coarse, *send = pl.pallas_call(
            functools.partial(merge_kernel, k, last),
            out_shape=(coarse_type,) if last else (coarse_type, send_type),
            in_specs=[vmem] * 2, out_specs=(vmem,) if last else (vmem,) * 2,
            compiler_params=params(), cost_estimate=cost(1 << 10, 1 << 16),
        )(coarse, got)
        send = send[0] if send else None
    blocks = pl.pallas_call(
        spread_kernel, out_shape=blocks_type, in_specs=[vmem], out_specs=vmem,
        compiler_params=params(), cost_estimate=cost(1 << 20, 1 << 16),
    )(coarse.reshape(slabs * prim, sectors * prim))
    assembled, scaled_q, packed = pl.pallas_call(
        coarse_rhs_kernel,
        out_shape=(
            full,
            jax.ShapeDtypeStruct((rhs, width), BF16),
            jax.ShapeDtypeStruct((slabs * sectors, rows, BLK), BF16),
        ),
        in_specs=[vmem] + [vmem] * 9, out_specs=(vmem,) * 3, compiler_params=params(),
        cost_estimate=cost(2 * rhs * width * prim, 8 * rhs * width),
    )(perm, image, *received, weight, basis_t, rhs_r, curv)
    gathered = lax.all_to_all(packed, ("gx", "col"), 0, 0)
    sol_r, sol_q = pl.pallas_call(
        neumann_kernel, out_shape=(full, full), in_specs=[vmem] * 3, out_specs=(vmem,) * 2,
        compiler_params=params(), cost_estimate=cost(1000 * flops, 2 * width * width),
    )(scaled_r, scaled_q, neumann)
    step, weighted, partial, *faces = pl.pallas_call(
        solve_kernel,
        out_shape=(
            jax.ShapeDtypeStruct((rhs, BLK), F32),
            full,
            jax.ShapeDtypeStruct((slabs * sectors, 1, BLK), F32),
        )
        + (face,) * 4,
        in_specs=[vmem] + [vmem] * 9, out_specs=(vmem,) * 7, compiler_params=params(),
        cost_estimate=cost(2 * rhs * width * prim, 8 * rhs * width),
    )(perm, gathered, blocks, rz_row, resid, assembled, weight, basis_t, sol_r, sol_q)
    partials = lax.all_to_all(partial, ("gx", "col"), 0, 0)
    received = swap_faces(faces)
    resid_new = pl.pallas_call(
        resid_kernel, out_shape=full, in_specs=[vmem] * 3, out_specs=vmem,
        compiler_params=params(), cost_estimate=cost(2 * rhs * width, 12 * rhs * width),
    )(step, resid, assembled)
    direction_new, rz_next = pl.pallas_call(
        direction_kernel, out_shape=(full, jax.ShapeDtypeStruct((1, rhs), F32)),
        in_specs=[vmem] + [vmem] * 8, out_specs=(vmem,) * 2, compiler_params=params(),
        cost_estimate=cost(2 * rhs * width, 8 * rhs * width),
    )(perm, partials, rz_row, direction, weighted, *received)
    return (resid_new[None, None], direction_new[None, None], rz_next[0])


def solution(mesh):
    placed = (
        P("gx", "col", None, None),
        P("gx", "col", None, None),
        P(),
        P("gx", "col", None, None),
        P("gx", "col", None, None),
        P("gx", "col", None, None),
        P("col", None, None, "gx", None, None),
        P(),
        P("gx", "col", None),
    )
    return jax.shard_map(
        body,
        mesh=mesh,
        in_specs=placed,
        out_specs=(P("gx", "col", None, None), P("gx", "col", None, None), P()),
        check_vma=False,
    )
```

```python
import functools

import jax
import jax.numpy as jnp
from jax import lax
from jax.experimental import pallas as pl
from jax.experimental.pallas import tpu as pltpu
from jax.sharding import PartitionSpec as P

F32 = jnp.float32
BF16 = jnp.bfloat16
BLK = 128
EXACT = lax.Precision.HIGHEST
VMEM = pltpu.VMEM


def params(limit=16 * 1024 * 1024):
    return pltpu.CompilerParams(vmem_limit_bytes=limit)


def cost(flops, nbytes):
    return pl.CostEstimate(flops=flops, bytes_accessed=nbytes, transcendentals=0)


def swap(value, axis, offset):
    count = lax.axis_size(axis)
    pairs = []
    for low in range(offset, count, 2):
        high = (low + 1) % count
        pairs += [(low, high), (high, low)]
    return lax.ppermute(value, axis, pairs)


def swap_faces(faces):
    return (
        swap(faces[0], "col", 1),
        swap(faces[1], "col", 0),
        swap(faces[2], "gx", 1),
        swap(faces[3], "gx", 0),
    )


def swap_counts():
    slab = lax.axis_index("gx")
    inside = jnp.logical_and(slab > 0, slab < lax.axis_size("gx") - 1)
    return (None, None, inside, None)


def slot_place(perm_ref, slot):
    return jnp.broadcast_to(perm_ref[0:1, slot : slot + 1], (1, BLK))


def swapped_places(perm_ref):
    slab = lax.axis_index("gx") % 2
    sector = lax.axis_index("col") % 2
    places = []
    for parity, even, odd in ((sector, 2, 3), (sector, 3, 2), (slab, 0, 1), (slab, 1, 0)):
        for j in range(2):
            at_even, at_odd = (slot_place(perm_ref, 2 * face + j) for face in (even, odd))
            places.append(jnp.where(parity == 0, at_even, at_odd))
    return places


def put_faces(perm_ref, source, outs):
    blocks = [source[:, b * BLK : (b + 1) * BLK] for b in range(source.shape[1] // BLK)]
    for i, place in enumerate(swapped_places(perm_ref)):
        chosen = blocks[0]
        for b in range(1, len(blocks)):
            chosen = jnp.where(place == b, blocks[b], chosen)
        j = i % 2
        outs[i // 2][:, j * BLK : (j + 1) * BLK] = chosen.astype(BF16)


def received_blocks(perm_ref, received, blocks):
    places = swapped_places(perm_ref)
    parts = []
    for i in range(len(places)):
        j = i % 2
        part = received[i // 2][:, j * BLK : (j + 1) * BLK].astype(F32)
        counts = swap_counts()[i // 2]
        parts.append(part if counts is None else jnp.where(counts, part, 0.0))
    for b in range(blocks):
        chosen = parts[0]
        for place, part in zip(places[1:], parts[1:]):
            chosen = jnp.where(place == b, part, chosen)
        yield slice(b * BLK, (b + 1) * BLK), chosen


def to_column(row):
    n = row.shape[1]
    at = lax.broadcasted_iota(jnp.int32, (n, n), 0) == lax.broadcasted_iota(jnp.int32, (n, n), 1)
    return jnp.sum(jnp.where(at, row, 0.0), axis=1, keepdims=True)


def to_row(column):
    n = column.shape[0]
    at = lax.broadcasted_iota(jnp.int32, (n, n), 0) == lax.broadcasted_iota(jnp.int32, (n, n), 1)
    return jnp.sum(jnp.where(at, column, 0.0), axis=0, keepdims=True)


CHUNKS = 4


def other_block(i, k):
    mine = (lax.axis_index("gx") >> k) % 2
    return ((i >> k) << (k + 1)) + (i & ((1 << k) - 1)) + ((1 - mine) << k)


def swap_bit(value, k):
    count = lax.axis_size("gx")
    return lax.ppermute(value, "gx", [(i, i ^ (1 << k)) for i in range(count)])


def image_kernel(perm_hbm, dir_hbm, schur_hbm, resid_hbm, basis_hbm, coarse_hbm,
                 image_ref, f0, f1, f2, f3, send_ref, dir_ref, resid_ref, basis_ref, coarse_ref, perm_ref,
                 schur_ref, sems):
    rows = schur_ref.shape[0] // CHUNKS
    parts = [pl.ds(i * rows, rows) for i in range(CHUNKS)]
    pairs = [(dir_hbm, dir_ref), (perm_hbm, perm_ref)]
    pairs += [(schur_hbm.at[part], schur_ref.at[part]) for part in parts]
    pairs += [(coarse_hbm.at[other_block(i, 0)], send_ref.at[i]) for i in range(send_ref.shape[0])]
    pairs += [(resid_hbm, resid_ref), (basis_hbm, basis_ref), (coarse_hbm, coarse_ref)]
    copies = [pltpu.make_async_copy(source, target, sems.at[i]) for i, (source, target) in enumerate(pairs)]
    for copy in copies:
        copy.start()
    copies[0].wait()
    total = None
    for i, part in enumerate(parts):
        copies[2 + i].wait()
        term = jnp.dot(dir_ref[:, part].astype(BF16), schur_ref[part], preferred_element_type=F32)
        total = term if total is None else total + term
    image_ref[...] = total
    copies[1].wait()
    put_faces(perm_ref, total, (f0, f1, f2, f3))
    for copy in copies[2 + CHUNKS :]:
        copy.wait()


def merge_kernel(k, last, blocks_ref, got_ref, out_ref, *send_ref):
    out_ref[...] = blocks_ref[...]
    for i in range(got_ref.shape[0]):
        out_ref[other_block(i, k)] = got_ref[i]
    if not last:
        for i in range(got_ref.shape[0]):
            send_ref[0][i] = out_ref[other_block(i, k + 1)]


def spread_kernel(k, matrix_ref, blocks_ref, send_ref):
    slabs, rows, _ = blocks_ref.shape
    prim = matrix_ref.shape[0] // slabs
    half = prim // 2
    sectors = matrix_ref.shape[1] // prim
    width = blocks_ref.shape[2] // 2
    depth = width // sectors
    source = lax.broadcasted_iota(jnp.int32, (sectors * prim, 2 * width), 0)
    place = lax.broadcasted_iota(jnp.int32, (sectors * prim, 2 * width), 1)
    later = place // width
    within = place % width
    sector, at = within // depth, within % depth
    chosen = jnp.logical_and(at < half, source == sector * prim + later * half + at)
    spread = jnp.dot(matrix_ref[...], jnp.where(chosen, 1.0, 0.0).astype(BF16), preferred_element_type=F32)
    empty = jnp.zeros((rows - prim, 2 * width), F32)
    for g in range(slabs):
        own = jnp.concatenate([spread[g * prim : (g + 1) * prim], empty], axis=0)
        blocks_ref[g] = own.astype(BF16)
    for i in range(send_ref.shape[0]):
        send_ref[i] = blocks_ref[other_block(i, k)]


def conduct_at(row, sector):
    lane = lax.broadcasted_iota(jnp.int32, row.shape, 1)
    return jnp.sum(jnp.where(lane == sector, row, 0.0), axis=1, keepdims=True)


def early_kernel(perm_ref, conduct_ref, dir_ref, image_ref, resid_ref, basis_ref,
                 weight_ref, rhs_ref, curv_ref, scaled_ref):
    slab, sector = lax.axis_index("gx"), lax.axis_index("col")
    slabs, sectors = lax.axis_size("gx"), lax.axis_size("col")
    row = conduct_ref[pl.ds(slab, 1), :]
    own = conduct_at(row, sector)
    below = conduct_at(conduct_ref[pl.ds(jnp.maximum(slab - 1, 0), 1), :], sector)
    above = conduct_at(conduct_ref[pl.ds(jnp.minimum(slab + 1, slabs - 1), 1), :], sector)
    below = jnp.where(slab > 0, below, 0.0)
    above = jnp.where(slab < slabs - 1, above, 0.0)
    left = conduct_at(row, (sector + sectors - 1) % sectors)
    right = conduct_at(row, (sector + 1) % sectors)
    across = [jnp.broadcast_to(own / (own + other), (1, BLK)) for other in (below, above, left, right)]
    places = [slot_place(perm_ref, slot) for slot in range(8)]
    for b in range(weight_ref.shape[1] // BLK):
        weight = across[0]
        for slot in range(2, 8):
            weight = jnp.where(places[slot] == b, across[slot // 2], weight)
        weight_ref[:, b * BLK : (b + 1) * BLK] = jnp.broadcast_to(weight, (8, BLK))
    scaled = (weight_ref[0:1, :] * resid_ref[...]).astype(BF16)
    scaled_ref[...] = scaled
    rhs_ref[...] = lax.dot_general(
        basis_ref[...], scaled, (((1,), (1,)), ((), ())), preferred_element_type=F32
    )
    curv = to_row(jnp.sum(dir_ref[...] * image_ref[...], axis=1, keepdims=True))
    high = curv.astype(BF16).astype(F32)
    n = curv.shape[1]
    curv_ref[...] = jnp.zeros_like(curv_ref)
    curv_ref[0:1, 0:n] = high
    curv_ref[0:1, n : 2 * n] = curv - high


def coarse_rhs_kernel(rows, sectors, perm_ref, image_ref, r0, r1, r2, r3, weight_ref, basis_ref, rhs_ref, curv_ref,
                      assembled_ref, scaled_ref, out_ref):
    for at, part in received_blocks(perm_ref, (r0, r1, r2, r3), image_ref.shape[1] // BLK):
        assembled_ref[:, at] = image_ref[:, at] + part
    scaled = (weight_ref[0:1, :] * assembled_ref[...]).astype(BF16)
    scaled_ref[...] = scaled
    rhs_q = lax.dot_general(
        basis_ref[...], scaled, (((1,), (1,)), ((), ())), preferred_element_type=F32
    )
    rhs_r = rhs_ref[...]
    half = rhs_r.shape[0] // 2
    packed = jnp.concatenate([rhs_r[:half], rhs_q[:half], rhs_r[half:], rhs_q[half:]], axis=1)
    packed = jnp.concatenate(
        [packed, curv_ref[0:1, :], jnp.zeros((rows - half - 1, BLK), F32)], axis=0
    )
    several = jnp.concatenate([packed] * sectors, axis=0).astype(BF16)
    step = several.shape[0]
    for i in range(out_ref.shape[0] // step):
        out_ref[i * step : (i + 1) * step] = several


def neumann_kernel(scaled_r_ref, scaled_q_ref, neumann_hbm, sol_r_ref, sol_q_ref, neumann_ref, sems):
    rows = neumann_ref.shape[0] // CHUNKS
    parts = [pl.ds(i * rows, rows) for i in range(CHUNKS)]
    copies = [
        pltpu.make_async_copy(neumann_hbm.at[part], neumann_ref.at[part], sems.at[i])
        for i, part in enumerate(parts)
    ]
    for copy in copies:
        copy.start()
    total_r = total_q = None
    for copy, part in zip(copies, parts):
        copy.wait()
        term_r = jnp.dot(scaled_r_ref[:, part], neumann_ref[part], preferred_element_type=F32)
        term_q = jnp.dot(scaled_q_ref[:, part], neumann_ref[part], preferred_element_type=F32)
        total_r = term_r if total_r is None else total_r + term_r
        total_q = term_q if total_q is None else total_q + term_q
    sol_r_ref[...] = total_r
    sol_q_ref[...] = total_q


def solve_kernel(rows, perm_ref, gathered_ref, blocks_ref, rz_ref, resid_ref, assembled_ref, weight_ref,
                 basis_ref, sol_r_ref, sol_q_ref, step_out, weighted_out, rz_out, *faces):
    n = rz_ref.shape[1]
    prim = basis_ref.shape[0]
    slabs, _, width = blocks_ref.shape
    width = width // 2
    total = None
    for h in range(slabs):
        part = gathered_ref[h * width : (h + 1) * width]
        halves = jnp.concatenate([part[:, : 2 * n], part[:, 2 * n :]], axis=0)
        term = jnp.dot(blocks_ref[h], halves, preferred_element_type=F32)
        total = term if total is None else total + term
    everything = gathered_ref[...]
    at = lax.broadcasted_iota(jnp.int32, (16, slabs * width), 1) % rows
    picks = jnp.where(at == prim // 2, 1.0, 0.0).astype(BF16)
    sums = jnp.dot(picks, everything, preferred_element_type=F32)
    step = rz_ref[...] / (sums[0:1, 0:n] + sums[0:1, n : 2 * n])
    coarse_sol = (total[0:prim, 0:n] - step * total[0:prim, n : 2 * n]).astype(BF16)
    correction = lax.dot_general(
        coarse_sol, basis_ref[...], (((0,), (0,)), ((), ())), preferred_element_type=F32
    )
    step_col = to_column(step)
    step_out[...] = jnp.broadcast_to(step_col, step_out.shape)
    resid_new = resid_ref[...] - step_col * assembled_ref[...]
    local = sol_r_ref[...] - step_col * sol_q_ref[...] + correction
    weighted = weight_ref[0:1, :] * local
    weighted_out[...] = weighted
    put_faces(perm_ref, weighted, faces)
    partial = to_row(jnp.sum(resid_new * weighted, axis=1, keepdims=True))
    partial = jnp.concatenate([partial, jnp.zeros((1, BLK - n), F32)], axis=1)
    for i in range(rz_out.shape[0]):
        rz_out[i] = partial


def resid_kernel(step_ref, resid_ref, assembled_ref, out_ref):
    out_ref[...] = resid_ref[...] - step_ref[:, 0:1] * assembled_ref[...]


def direction_kernel(perm_ref, partials_ref, rz_ref, dir_ref, weighted_ref, r0, r1, r2, r3,
                     out_ref, rz_out):
    n = rz_ref.shape[1]
    rz_next = jnp.sum(partials_ref[...], axis=0)[:, 0:n]
    rz_out[...] = rz_next
    factor = to_column(rz_next / rz_ref[...])
    for at, part in received_blocks(perm_ref, (r0, r1, r2, r3), dir_ref.shape[1] // BLK):
        out_ref[:, at] = weighted_ref[:, at] + factor * dir_ref[:, at] + part


def body(resid, direction, rz_prev, schur, neumann, basis, coarse_inv, conduct, face_perm):
    resid, direction, schur, neumann = resid[0, 0], direction[0, 0], schur[0, 0], neumann[0, 0]
    basis_t = basis[0, 0].T
    perm = face_perm[0]
    rhs, width = resid.shape
    prim = basis_t.shape[0]
    slabs, sectors = lax.axis_size("gx"), lax.axis_size("col")
    rows = -(-(prim // 2 + 1) // 4) * 4
    block_rows = -(-prim // 16) * 16
    rounds = slabs.bit_length() - 1
    face = jax.ShapeDtypeStruct((rhs, 2 * BLK), BF16)
    full = jax.ShapeDtypeStruct((rhs, width), F32)
    rz_row = rz_prev[None, :]
    vmem = pl.BlockSpec(memory_space=VMEM)
    hbm = pl.BlockSpec(memory_space=pltpu.HBM)
    flops = 2 * rhs * width * width
    coarse = coarse_inv[0, :, :, 0]
    coarse_type = jax.ShapeDtypeStruct(coarse.shape, BF16)
    send_type = jax.ShapeDtypeStruct((slabs // 2,) + coarse.shape[1:], BF16)
    blocks_type = jax.ShapeDtypeStruct((slabs, block_rows, 2 * sectors * rows), BF16)

    fetched = [pltpu.with_memory_space_constraint(x, pltpu.HBM) for x in (perm, direction, schur, resid, basis_t, coarse)]
    image, f0, f1, f2, f3, send, direction, resid, basis_t, coarse = pl.pallas_call(
        image_kernel,
        out_shape=(full,) + (face,) * 4
        + (send_type, full, full, jax.ShapeDtypeStruct((prim, width), BF16), coarse_type),
        in_specs=[hbm] * 6, out_specs=(vmem,) * 10,
        scratch_shapes=[
            pltpu.VMEM(perm.shape, jnp.int32),
            pltpu.VMEM((width, width), BF16),
            pltpu.SemaphoreType.DMA((CHUNKS + 5 + slabs // 2,)),
        ],
        compiler_params=params(), cost_estimate=cost(flops, 2 * width * width),
    )(*fetched)
    received = swap_faces((f0, f1, f2, f3))
    weight, rhs_r, curv, scaled_r = pl.pallas_call(
        early_kernel,
        out_shape=(
            jax.ShapeDtypeStruct((8, width), F32),
            jax.ShapeDtypeStruct((prim, rhs), F32),
            jax.ShapeDtypeStruct((8, BLK), F32),
            jax.ShapeDtypeStruct((rhs, width), BF16),
        ),
        in_specs=[vmem] * 6, out_specs=(vmem,) * 4, compiler_params=params(),
        cost_estimate=cost(2 * rhs * width * prim, 8 * rhs * width),
    )(perm, conduct, direction, image, resid, basis_t)
    for k in range(rounds - 1):
        got = swap_bit(send, k)
        last = k + 2 == rounds
        coarse, *send = pl.pallas_call(
            functools.partial(merge_kernel, k, last),
            out_shape=(coarse_type,) if last else (coarse_type, send_type),
            in_specs=[vmem] * 2, out_specs=(vmem,) if last else (vmem,) * 2,
            compiler_params=params(), cost_estimate=cost(1 << 10, 1 << 16),
        )(coarse, got)
        send = send[0] if send else None
    blocks, send = pl.pallas_call(
        functools.partial(spread_kernel, rounds - 1),
        out_shape=(blocks_type, jax.ShapeDtypeStruct((slabs // 2,) + blocks_type.shape[1:], BF16)),
        in_specs=[vmem], out_specs=(vmem,) * 2,
        compiler_params=params(), cost_estimate=cost(1 << 20, 1 << 16),
    )(coarse.reshape(slabs * prim, sectors * prim))
    (blocks,) = pl.pallas_call(
        functools.partial(merge_kernel, rounds - 1, True),
        out_shape=(blocks_type,), in_specs=[vmem] * 2, out_specs=(vmem,),
        compiler_params=params(), cost_estimate=cost(1 << 10, 1 << 16),
    )(blocks, swap_bit(send, rounds - 1))
    assembled, scaled_q, packed = pl.pallas_call(
        functools.partial(coarse_rhs_kernel, rows, sectors),
        out_shape=(
            full,
            jax.ShapeDtypeStruct((rhs, width), BF16),
            jax.ShapeDtypeStruct((slabs * sectors * rows, BLK), BF16),
        ),
        in_specs=[vmem] + [vmem] * 9, out_specs=(vmem,) * 3, compiler_params=params(),
        cost_estimate=cost(2 * rhs * width * prim, 8 * rhs * width),
    )(perm, image, *received, weight, basis_t, rhs_r, curv)
    packed = packed.reshape(slabs * sectors, rows // 2, 2, BLK)
    gathered = lax.all_to_all(packed, ("gx", "col"), 0, 0).reshape(slabs * sectors * rows, BLK)
    sol_r, sol_q = pl.pallas_call(
        neumann_kernel, out_shape=(full, full), in_specs=[vmem, vmem, hbm], out_specs=(vmem,) * 2,
        scratch_shapes=[pltpu.VMEM((width, width), BF16), pltpu.SemaphoreType.DMA((CHUNKS,))],
        compiler_params=params(), cost_estimate=cost(1000 * flops, 2 * width * width),
    )(scaled_r, scaled_q, pltpu.with_memory_space_constraint(neumann, pltpu.HBM))
    step, weighted, partial, *faces = pl.pallas_call(
        functools.partial(solve_kernel, rows),
        out_shape=(
            jax.ShapeDtypeStruct((rhs, BLK), F32),
            full,
            jax.ShapeDtypeStruct((slabs * sectors, 1, BLK), F32),
        )
        + (face,) * 4,
        in_specs=[vmem] + [vmem] * 9, out_specs=(vmem,) * 7, compiler_params=params(),
        cost_estimate=cost(2 * rhs * width * prim, 8 * rhs * width),
    )(perm, gathered, blocks, rz_row, resid, assembled, weight, basis_t, sol_r, sol_q)
    partials = lax.all_to_all(partial, ("gx", "col"), 0, 0)
    received = swap_faces(faces)
    resid_new = pl.pallas_call(
        resid_kernel, out_shape=full, in_specs=[vmem] * 3, out_specs=vmem,
        compiler_params=params(), cost_estimate=cost(2 * rhs * width, 12 * rhs * width),
    )(step, resid, assembled)
    direction_new, rz_next = pl.pallas_call(
        direction_kernel, out_shape=(full, jax.ShapeDtypeStruct((1, rhs), F32)),
        in_specs=[vmem] + [vmem] * 8, out_specs=(vmem,) * 2, compiler_params=params(),
        cost_estimate=cost(2 * rhs * width, 8 * rhs * width),
    )(perm, partials, rz_row, direction, weighted, *received)
    return (resid_new[None, None], direction_new[None, None], rz_next[0])


def solution(mesh):
    placed = (
        P("gx", "col", None, None),
        P("gx", "col", None, None),
        P(),
        P("gx", "col", None, None),
        P("gx", "col", None, None),
        P("gx", "col", None, None),
        P("col", None, None, "gx", None, None),
        P(),
        P("gx", "col", None),
    )
    return jax.shard_map(
        body,
        mesh=mesh,
        in_specs=placed,
        out_specs=(P("gx", "col", None, None), P("gx", "col", None, None), P()),
        check_vma=False,
    )
```

```python
import functools

import jax
import jax.numpy as jnp
from jax import lax
from jax.experimental import pallas as pl
from jax.experimental.pallas import tpu as pltpu
from jax.sharding import PartitionSpec as P

F32 = jnp.float32
BF16 = jnp.bfloat16
BLK = 128
EXACT = lax.Precision.HIGHEST
VMEM = pltpu.VMEM


def params(limit=16 * 1024 * 1024):
    return pltpu.CompilerParams(vmem_limit_bytes=limit)


def cost(flops, nbytes):
    return pl.CostEstimate(flops=flops, bytes_accessed=nbytes, transcendentals=0)


def swap(value, axis, offset):
    count = lax.axis_size(axis)
    pairs = []
    for low in range(offset, count, 2):
        high = (low + 1) % count
        pairs += [(low, high), (high, low)]
    return lax.ppermute(value, axis, pairs)


def swap_second(value):
    slabs, sectors = lax.axis_size("gx"), lax.axis_size("col")
    pairs = []
    for slab in range(slabs):
        for sector in range(sectors):
            other = (slab + 1 if slab % 2 else slab - 1, sector)
            if not 0 <= other[0] < slabs:
                other = (slab, sector ^ 1)
            pairs.append((slab * sectors + sector, other[0] * sectors + other[1]))
    return lax.ppermute(value, ("gx", "col"), pairs)


def swap_faces(faces):
    return (
        swap(faces[0], "col", 1),
        swap(faces[1], "col", 0),
        swap_second(faces[2]),
        swap(faces[3], "gx", 0),
    )


def swap_counts():
    slab = lax.axis_index("gx")
    inside = jnp.logical_and(slab > 0, slab < lax.axis_size("gx") - 1)
    return (None, None, inside, None)


def slot_place(perm_ref, slot):
    return jnp.broadcast_to(perm_ref[0:1, slot : slot + 1], (1, BLK))


def swapped_places(perm_ref):
    slab = lax.axis_index("gx") % 2
    sector = lax.axis_index("col") % 2
    places = []
    for parity, even, odd in ((sector, 2, 3), (sector, 3, 2), (slab, 0, 1), (slab, 1, 0)):
        for j in range(2):
            at_even, at_odd = (slot_place(perm_ref, 2 * face + j) for face in (even, odd))
            places.append(jnp.where(parity == 0, at_even, at_odd))
    return places


def put_faces(perm_ref, source, outs):
    blocks = [source[:, b * BLK : (b + 1) * BLK] for b in range(source.shape[1] // BLK)]
    for i, place in enumerate(swapped_places(perm_ref)):
        chosen = blocks[0]
        for b in range(1, len(blocks)):
            chosen = jnp.where(place == b, blocks[b], chosen)
        j = i % 2
        outs[i // 2][:, j * BLK : (j + 1) * BLK] = chosen.astype(BF16)


def received_blocks(perm_ref, received, blocks):
    places = swapped_places(perm_ref)
    parts = []
    for i in range(len(places)):
        j = i % 2
        part = received[i // 2][:, j * BLK : (j + 1) * BLK].astype(F32)
        counts = swap_counts()[i // 2]
        parts.append(part if counts is None else jnp.where(counts, part, 0.0))
    for b in range(blocks):
        chosen = parts[0]
        for place, part in zip(places[1:], parts[1:]):
            chosen = jnp.where(place == b, part, chosen)
        yield slice(b * BLK, (b + 1) * BLK), chosen


def to_column(row):
    n = row.shape[1]
    at = lax.broadcasted_iota(jnp.int32, (n, n), 0) == lax.broadcasted_iota(jnp.int32, (n, n), 1)
    return jnp.sum(jnp.where(at, row, 0.0), axis=1, keepdims=True)


def to_row(column):
    n = column.shape[0]
    at = lax.broadcasted_iota(jnp.int32, (n, n), 0) == lax.broadcasted_iota(jnp.int32, (n, n), 1)
    return jnp.sum(jnp.where(at, column, 0.0), axis=0, keepdims=True)


CHUNKS = 4


def other_block(i, k):
    mine = (lax.axis_index("gx") >> k) % 2
    return ((i >> k) << (k + 1)) + (i & ((1 << k) - 1)) + ((1 - mine) << k)


def swap_bit(value, k):
    count = lax.axis_size("gx")
    return lax.ppermute(value, "gx", [(i, i ^ (1 << k)) for i in range(count)])


def image_kernel(perm_hbm, dir_hbm, schur_hbm, resid_hbm, basis_hbm, coarse_hbm,
                 image_ref, f0, f1, f2, f3, send_ref, dir_ref, resid_ref, basis_ref, coarse_ref, perm_ref,
                 schur_ref, sems):
    rows = schur_ref.shape[0] // CHUNKS
    parts = [pl.ds(i * rows, rows) for i in range(CHUNKS)]
    pairs = [(dir_hbm, dir_ref), (perm_hbm, perm_ref)]
    pairs += [(schur_hbm.at[part], schur_ref.at[part]) for part in parts]
    pairs += [(coarse_hbm.at[other_block(i, 0)], send_ref.at[i]) for i in range(send_ref.shape[0])]
    pairs += [(resid_hbm, resid_ref), (basis_hbm, basis_ref), (coarse_hbm, coarse_ref)]
    copies = [pltpu.make_async_copy(source, target, sems.at[i]) for i, (source, target) in enumerate(pairs)]
    for copy in copies:
        copy.start()
    copies[0].wait()
    total = None
    for i, part in enumerate(parts):
        copies[2 + i].wait()
        term = jnp.dot(dir_ref[:, part].astype(BF16), schur_ref[part], preferred_element_type=F32)
        total = term if total is None else total + term
    image_ref[...] = total
    copies[1].wait()
    put_faces(perm_ref, total, (f0, f1, f2, f3))
    for copy in copies[2 + CHUNKS :]:
        copy.wait()


def merge_kernel(k, last, blocks_ref, got_ref, out_ref, *send_ref):
    out_ref[...] = blocks_ref[...]
    for i in range(got_ref.shape[0]):
        out_ref[other_block(i, k)] = got_ref[i]
    if not last:
        for i in range(got_ref.shape[0]):
            send_ref[0][i] = out_ref[other_block(i, k + 1)]


def join_kernel(k, depth, prim, blocks_ref, got_ref, wide_ref, all_ref):
    all_ref[...] = blocks_ref[...]
    for i in range(got_ref.shape[0]):
        all_ref[other_block(i, k)] = got_ref[i]
    slabs, rows, width = blocks_ref.shape
    width = width // 2
    for half in range(2):
        for h in range(slabs):
            at = (half * slabs + h) * width
            wide_ref[:, at : at + width] = all_ref[h, :, half * width : (half + 1) * width]
    row = lax.broadcasted_iota(jnp.int32, wide_ref.shape, 0)
    lane = lax.broadcasted_iota(jnp.int32, wide_ref.shape, 1)
    picked = jnp.logical_and(lane < slabs * width, lane % depth == prim // 2)
    wide = jnp.where(row == prim, jnp.where(picked, 1.0, 0.0), wide_ref[...].astype(F32))
    wide_ref[...] = wide.astype(BF16)


def spread_kernel(k, matrix_ref, blocks_ref, send_ref):
    slabs, rows, _ = blocks_ref.shape
    prim = matrix_ref.shape[0] // slabs
    half = prim // 2
    sectors = matrix_ref.shape[1] // prim
    width = blocks_ref.shape[2] // 2
    depth = width // sectors
    source = lax.broadcasted_iota(jnp.int32, (sectors * prim, 2 * width), 0)
    place = lax.broadcasted_iota(jnp.int32, (sectors * prim, 2 * width), 1)
    later = place // width
    within = place % width
    sector, at = within // depth, within % depth
    chosen = jnp.logical_and(at < half, source == sector * prim + later * half + at)
    spread = jnp.dot(matrix_ref[...], jnp.where(chosen, 1.0, 0.0).astype(BF16), preferred_element_type=F32)
    empty = jnp.zeros((rows - prim, 2 * width), F32)
    for g in range(slabs):
        own = jnp.concatenate([spread[g * prim : (g + 1) * prim], empty], axis=0)
        blocks_ref[g] = own.astype(BF16)
    for i in range(send_ref.shape[0]):
        send_ref[i] = blocks_ref[other_block(i, k)]


def conduct_at(row, sector):
    lane = lax.broadcasted_iota(jnp.int32, row.shape, 1)
    return jnp.sum(jnp.where(lane == sector, row, 0.0), axis=1, keepdims=True)


def early_kernel(perm_ref, conduct_ref, dir_ref, image_ref, resid_ref, basis_ref,
                 weight_ref, rhs_ref, curv_ref, scaled_ref):
    slab, sector = lax.axis_index("gx"), lax.axis_index("col")
    slabs, sectors = lax.axis_size("gx"), lax.axis_size("col")
    row = conduct_ref[pl.ds(slab, 1), :]
    own = conduct_at(row, sector)
    below = conduct_at(conduct_ref[pl.ds(jnp.maximum(slab - 1, 0), 1), :], sector)
    above = conduct_at(conduct_ref[pl.ds(jnp.minimum(slab + 1, slabs - 1), 1), :], sector)
    below = jnp.where(slab > 0, below, 0.0)
    above = jnp.where(slab < slabs - 1, above, 0.0)
    left = conduct_at(row, (sector + sectors - 1) % sectors)
    right = conduct_at(row, (sector + 1) % sectors)
    across = [jnp.broadcast_to(own / (own + other), (1, BLK)) for other in (below, above, left, right)]
    places = [slot_place(perm_ref, slot) for slot in range(8)]
    for b in range(weight_ref.shape[1] // BLK):
        weight = across[0]
        for slot in range(2, 8):
            weight = jnp.where(places[slot] == b, across[slot // 2], weight)
        weight_ref[:, b * BLK : (b + 1) * BLK] = jnp.broadcast_to(weight, (8, BLK))
    scaled = (weight_ref[0:1, :] * resid_ref[...]).astype(BF16)
    scaled_ref[...] = scaled
    rhs_ref[...] = lax.dot_general(
        basis_ref[...], scaled, (((1,), (1,)), ((), ())), preferred_element_type=F32
    )
    curv = to_row(jnp.sum(dir_ref[...] * image_ref[...], axis=1, keepdims=True))
    high = curv.astype(BF16).astype(F32)
    n = curv.shape[1]
    curv_ref[...] = jnp.zeros_like(curv_ref)
    curv_ref[0:1, 0:n] = high
    curv_ref[0:1, n : 2 * n] = curv - high


def coarse_rhs_kernel(rows, sectors, perm_ref, image_ref, r0, r1, r2, r3, weight_ref, basis_ref, rhs_ref, curv_ref,
                      assembled_ref, scaled_ref, rhs_q_ref, out_ref):
    for at, part in received_blocks(perm_ref, (r0, r1, r2, r3), image_ref.shape[1] // BLK):
        assembled_ref[:, at] = image_ref[:, at] + part
    scaled = (weight_ref[0:1, :] * assembled_ref[...]).astype(BF16)
    scaled_ref[...] = scaled
    rhs_q = lax.dot_general(
        basis_ref[...], scaled, (((1,), (1,)), ((), ())), preferred_element_type=F32
    )
    rhs_q_ref[...] = rhs_q
    rhs_r = rhs_ref[...]
    half = rhs_r.shape[0] // 2
    packed = jnp.concatenate([rhs_r[:half], rhs_q[:half], rhs_r[half:], rhs_q[half:]], axis=1)
    packed = jnp.concatenate(
        [packed, curv_ref[0:1, :], jnp.zeros((rows - half - 1, BLK), F32)], axis=0
    )
    several = jnp.concatenate([packed] * sectors, axis=0).astype(BF16)
    step = several.shape[0]
    for i in range(out_ref.shape[0] // step):
        out_ref[i * step : (i + 1) * step] = several


def neumann_kernel(scaled_r_ref, scaled_q_ref, resid_ref, assembled_ref, weight_ref, neumann_hbm,
                   sol_r_ref, sol_q_ref, sums_ref, neumann_ref, sems):
    rows = neumann_ref.shape[0] // CHUNKS
    parts = [pl.ds(i * rows, rows) for i in range(CHUNKS)]
    copies = [
        pltpu.make_async_copy(neumann_hbm.at[part], neumann_ref.at[part], sems.at[i])
        for i, part in enumerate(parts)
    ]
    for copy in copies:
        copy.start()
    total_r = total_q = None
    for copy, part in zip(copies, parts):
        copy.wait()
        term_r = jnp.dot(scaled_r_ref[:, part], neumann_ref[part], preferred_element_type=F32)
        term_q = jnp.dot(scaled_q_ref[:, part], neumann_ref[part], preferred_element_type=F32)
        total_r = term_r if total_r is None else total_r + term_r
        total_q = term_q if total_q is None else total_q + term_q
    sol_r_ref[...] = total_r
    sol_q_ref[...] = total_q
    weighted_r = weight_ref[0:1, :] * resid_ref[...]
    weighted_q = weight_ref[0:1, :] * assembled_ref[...]
    n = total_r.shape[0]
    sums_ref[...] = jnp.zeros_like(sums_ref)
    for i, product in enumerate(
        (weighted_r * total_r, weighted_r * total_q + weighted_q * total_r, weighted_q * total_q)
    ):
        sums_ref[0:1, i * n : (i + 1) * n] = to_row(jnp.sum(product, axis=1, keepdims=True))


def solve_kernel(perm_ref, gathered_ref, wide_ref, rz_ref, weight_ref, basis_ref, sol_r_ref, sol_q_ref,
                 sums_ref, rhs_r_ref, rhs_q_ref, step_out, weighted_out, rz_hbm, f0, f1, f2, f3, rz_ref_out, sem):
    n = rz_ref.shape[1]
    prim = basis_ref.shape[0]
    halves = jnp.concatenate([gathered_ref[:, : 2 * n], gathered_ref[:, 2 * n :]], axis=0)
    total = jnp.dot(wide_ref[...], halves, preferred_element_type=F32)
    step = rz_ref[...] / (total[prim : prim + 1, 0:n] + total[prim : prim + 1, n : 2 * n])
    coarse_sol = (total[0:prim, 0:n] - step * total[0:prim, n : 2 * n]).astype(BF16)
    coarse_part = coarse_sol.astype(F32) * (rhs_r_ref[...] - step * rhs_q_ref[...])
    partial = (
        sums_ref[0:1, 0:n]
        - step * (sums_ref[0:1, n : 2 * n] - step * sums_ref[0:1, 2 * n : 3 * n])
        + jnp.sum(coarse_part, axis=0, keepdims=True)
    )
    partial = jnp.concatenate([partial, jnp.zeros((1, BLK - n), F32)], axis=1)
    for i in range(rz_ref_out.shape[0]):
        rz_ref_out[i] = partial
    copy = pltpu.make_async_copy(rz_ref_out, rz_hbm, sem)
    copy.start()
    correction = lax.dot_general(
        coarse_sol, basis_ref[...], (((0,), (0,)), ((), ())), preferred_element_type=F32
    )
    step_col = to_column(step)
    step_out[...] = jnp.broadcast_to(step_col, step_out.shape)
    weighted = weight_ref[0:1, :] * (sol_r_ref[...] - step_col * sol_q_ref[...] + correction)
    weighted_out[...] = weighted
    put_faces(perm_ref, weighted, (f0, f1, f2, f3))
    copy.wait()


def resid_kernel(step_ref, resid_ref, assembled_ref, out_ref):
    out_ref[...] = resid_ref[...] - step_ref[:, 0:1] * assembled_ref[...]


def direction_kernel(perm_ref, partials_ref, rz_ref, dir_ref, weighted_ref, r0, r1, r2, r3,
                     out_ref, rz_out):
    n = rz_ref.shape[1]
    rz_next = jnp.sum(partials_ref[...], axis=0)[:, 0:n]
    rz_out[...] = rz_next
    factor = to_column(rz_next / rz_ref[...])
    for at, part in received_blocks(perm_ref, (r0, r1, r2, r3), dir_ref.shape[1] // BLK):
        out_ref[:, at] = weighted_ref[:, at] + factor * dir_ref[:, at] + part


def body(resid, direction, rz_prev, schur, neumann, basis, coarse_inv, conduct, face_perm):
    resid, direction, schur, neumann = resid[0, 0], direction[0, 0], schur[0, 0], neumann[0, 0]
    basis_t = basis[0, 0].T
    perm = face_perm[0]
    rhs, width = resid.shape
    prim = basis_t.shape[0]
    slabs, sectors = lax.axis_size("gx"), lax.axis_size("col")
    rows = -(-(prim // 2 + 1) // 4) * 4
    block_rows = -(-(prim + 1) // 16) * 16
    rounds = slabs.bit_length() - 1
    face = jax.ShapeDtypeStruct((rhs, 2 * BLK), BF16)
    full = jax.ShapeDtypeStruct((rhs, width), F32)
    rz_row = rz_prev[None, :]
    vmem = pl.BlockSpec(memory_space=VMEM)
    hbm = pl.BlockSpec(memory_space=pltpu.HBM)
    flops = 2 * rhs * width * width
    coarse = coarse_inv[0, :, :, 0]
    coarse_type = jax.ShapeDtypeStruct(coarse.shape, BF16)
    send_type = jax.ShapeDtypeStruct((slabs // 2,) + coarse.shape[1:], BF16)
    blocks_type = jax.ShapeDtypeStruct((slabs, block_rows, 2 * sectors * rows), BF16)

    fetched = [pltpu.with_memory_space_constraint(x, pltpu.HBM) for x in (perm, direction, schur, resid, basis_t, coarse)]
    image, f0, f1, f2, f3, send, direction, resid, basis_t, coarse = pl.pallas_call(
        image_kernel,
        out_shape=(full,) + (face,) * 4
        + (send_type, full, full, jax.ShapeDtypeStruct((prim, width), BF16), coarse_type),
        in_specs=[hbm] * 6, out_specs=(vmem,) * 10,
        scratch_shapes=[
            pltpu.VMEM(perm.shape, jnp.int32),
            pltpu.VMEM((width, width), BF16),
            pltpu.SemaphoreType.DMA((CHUNKS + 5 + slabs // 2,)),
        ],
        compiler_params=params(), cost_estimate=cost(flops, 2 * width * width),
    )(*fetched)
    received = swap_faces((f0, f1, f2, f3))
    weight, rhs_r, curv, scaled_r = pl.pallas_call(
        early_kernel,
        out_shape=(
            jax.ShapeDtypeStruct((8, width), F32),
            jax.ShapeDtypeStruct((prim, rhs), F32),
            jax.ShapeDtypeStruct((8, BLK), F32),
            jax.ShapeDtypeStruct((rhs, width), BF16),
        ),
        in_specs=[vmem] * 6, out_specs=(vmem,) * 4, compiler_params=params(),
        cost_estimate=cost(2 * rhs * width * prim, 8 * rhs * width),
    )(perm, conduct, direction, image, resid, basis_t)
    for k in range(rounds - 1):
        got = swap_bit(send, k)
        last = k + 2 == rounds
        coarse, *send = pl.pallas_call(
            functools.partial(merge_kernel, k, last),
            out_shape=(coarse_type,) if last else (coarse_type, send_type),
            in_specs=[vmem] * 2, out_specs=(vmem,) if last else (vmem,) * 2,
            compiler_params=params(), cost_estimate=cost(1 << 10, 1 << 16),
        )(coarse, got)
        send = send[0] if send else None
    blocks, send = pl.pallas_call(
        functools.partial(spread_kernel, rounds - 1),
        out_shape=(blocks_type, jax.ShapeDtypeStruct((slabs // 2,) + blocks_type.shape[1:], BF16)),
        in_specs=[vmem], out_specs=(vmem,) * 2,
        compiler_params=params(), cost_estimate=cost(1 << 20, 1 << 16),
    )(coarse.reshape(slabs * prim, sectors * prim))
    wide = pl.pallas_call(
        functools.partial(join_kernel, rounds - 1, rows, prim),
        out_shape=jax.ShapeDtypeStruct((block_rows, slabs * blocks_type.shape[2]), BF16),
        in_specs=[vmem] * 2, out_specs=vmem,
        scratch_shapes=[pltpu.VMEM(blocks_type.shape, BF16)],
        compiler_params=params(), cost_estimate=cost(1 << 10, 1 << 16),
    )(blocks, swap_bit(send, rounds - 1))
    assembled, scaled_q, rhs_q, packed = pl.pallas_call(
        functools.partial(coarse_rhs_kernel, rows, sectors),
        out_shape=(
            full,
            jax.ShapeDtypeStruct((rhs, width), BF16),
            jax.ShapeDtypeStruct((prim, rhs), F32),
            jax.ShapeDtypeStruct((slabs * sectors * rows, BLK), BF16),
        ),
        in_specs=[vmem] + [vmem] * 9, out_specs=(vmem,) * 4, compiler_params=params(),
        cost_estimate=cost(2 * rhs * width * prim, 8 * rhs * width),
    )(perm, image, *received, weight, basis_t, rhs_r, curv)
    packed = packed.reshape(slabs * sectors, rows // 2, 2, BLK)
    gathered = lax.all_to_all(packed, ("gx", "col"), 0, 0).reshape(slabs * sectors * rows, BLK)
    sol_r, sol_q, sums = pl.pallas_call(
        neumann_kernel,
        out_shape=(full, full, jax.ShapeDtypeStruct((8, BLK), F32)),
        in_specs=[vmem] * 5 + [hbm], out_specs=(vmem,) * 3,
        scratch_shapes=[pltpu.VMEM((width, width), BF16), pltpu.SemaphoreType.DMA((CHUNKS,))],
        compiler_params=params(), cost_estimate=cost(1000 * flops, 2 * width * width),
    )(scaled_r, scaled_q, resid, assembled, weight, pltpu.with_memory_space_constraint(neumann, pltpu.HBM))
    step, weighted, partial, *faces = pl.pallas_call(
        solve_kernel,
        out_shape=(
            jax.ShapeDtypeStruct((rhs, BLK), F32),
            full,
            jax.ShapeDtypeStruct((slabs * sectors, 1, BLK), F32),
        )
        + (face,) * 4,
        in_specs=[vmem] * 11, out_specs=(vmem, vmem, hbm) + (vmem,) * 4,
        scratch_shapes=[pltpu.VMEM((slabs * sectors, 1, BLK), F32), pltpu.SemaphoreType.DMA],
        compiler_params=params(), cost_estimate=cost(2 * rhs * width * prim, 8 * rhs * width),
    )(perm, gathered, wide, rz_row, weight, basis_t, sol_r, sol_q, sums, rhs_r, rhs_q)
    partials = lax.all_to_all(partial, ("gx", "col"), 0, 0)
    received = swap_faces(faces)
    resid_new = pl.pallas_call(
        resid_kernel, out_shape=full, in_specs=[vmem] * 3, out_specs=vmem,
        compiler_params=params(), cost_estimate=cost(2 * rhs * width, 12 * rhs * width),
    )(step, resid, assembled)
    direction_new, rz_next = pl.pallas_call(
        direction_kernel, out_shape=(full, jax.ShapeDtypeStruct((1, rhs), F32)),
        in_specs=[vmem] + [vmem] * 8, out_specs=(vmem,) * 2, compiler_params=params(),
        cost_estimate=cost(2 * rhs * width, 8 * rhs * width),
    )(perm, partials, rz_row, direction, weighted, *received)
    return (resid_new[None, None], direction_new[None, None], rz_next[0])


def solution(mesh):
    placed = (
        P("gx", "col", None, None),
        P("gx", "col", None, None),
        P(),
        P("gx", "col", None, None),
        P("gx", "col", None, None),
        P("gx", "col", None, None),
        P("col", None, None, "gx", None, None),
        P(),
        P("gx", "col", None),
    )
    return jax.shard_map(
        body,
        mesh=mesh,
        in_specs=placed,
        out_specs=(P("gx", "col", None, None), P("gx", "col", None, None), P()),
        check_vma=False,
    )
```

```python
import functools

import jax
import jax.numpy as jnp
from jax import lax
from jax.experimental import pallas as pl
from jax.experimental.pallas import tpu as pltpu
from jax.sharding import PartitionSpec as P

F32 = jnp.float32
BF16 = jnp.bfloat16
BLK = 128
EXACT = lax.Precision.HIGHEST
VMEM = pltpu.VMEM


def params(limit=16 * 1024 * 1024):
    return pltpu.CompilerParams(vmem_limit_bytes=limit)


def cost(flops, nbytes):
    return pl.CostEstimate(flops=flops, bytes_accessed=nbytes, transcendentals=0)


def swap(value, axis, offset):
    count = lax.axis_size(axis)
    pairs = []
    for low in range(offset, count, 2):
        high = (low + 1) % count
        pairs += [(low, high), (high, low)]
    return lax.ppermute(value, axis, pairs)


def swap_second(value):
    slabs, sectors = lax.axis_size("gx"), lax.axis_size("col")
    pairs = []
    for slab in range(slabs):
        for sector in range(sectors):
            other = (slab + 1 if slab % 2 else slab - 1, sector)
            if not 0 <= other[0] < slabs:
                other = (slab, sector ^ 1)
            pairs.append((slab * sectors + sector, other[0] * sectors + other[1]))
    return lax.ppermute(value, ("gx", "col"), pairs)


def swap_faces(faces):
    return (
        swap(faces[0], "col", 1),
        swap(faces[1], "col", 0),
        swap_second(faces[2]),
        swap(faces[3], "gx", 0),
    )


def swap_counts():
    slab = lax.axis_index("gx")
    inside = jnp.logical_and(slab > 0, slab < lax.axis_size("gx") - 1)
    return (None, None, inside, None)


def slot_place(perm_ref, slot):
    return jnp.broadcast_to(perm_ref[0:1, slot : slot + 1], (1, BLK))


def swapped_places(perm_ref):
    slab = lax.axis_index("gx") % 2
    sector = lax.axis_index("col") % 2
    places = []
    for parity, even, odd in ((sector, 2, 3), (sector, 3, 2), (slab, 0, 1), (slab, 1, 0)):
        for j in range(2):
            at_even, at_odd = (slot_place(perm_ref, 2 * face + j) for face in (even, odd))
            places.append(jnp.where(parity == 0, at_even, at_odd))
    return places


def put_faces(perm_ref, source, outs):
    blocks = [source[:, b * BLK : (b + 1) * BLK] for b in range(source.shape[1] // BLK)]
    for i, place in enumerate(swapped_places(perm_ref)):
        chosen = blocks[0]
        for b in range(1, len(blocks)):
            chosen = jnp.where(place == b, blocks[b], chosen)
        j = i % 2
        outs[i // 2][:, j * BLK : (j + 1) * BLK] = chosen.astype(BF16)


def received_blocks(perm_ref, received, blocks):
    places = swapped_places(perm_ref)
    parts = []
    for i in range(len(places)):
        j = i % 2
        part = received[i // 2][:, j * BLK : (j + 1) * BLK].astype(F32)
        counts = swap_counts()[i // 2]
        parts.append(part if counts is None else jnp.where(counts, part, 0.0))
    for b in range(blocks):
        chosen = parts[0]
        for place, part in zip(places[1:], parts[1:]):
            chosen = jnp.where(place == b, part, chosen)
        yield slice(b * BLK, (b + 1) * BLK), chosen


def to_column(row):
    n = row.shape[1]
    at = lax.broadcasted_iota(jnp.int32, (n, n), 0) == lax.broadcasted_iota(jnp.int32, (n, n), 1)
    return jnp.sum(jnp.where(at, row, 0.0), axis=1, keepdims=True)


def to_row(column):
    n = column.shape[0]
    at = lax.broadcasted_iota(jnp.int32, (n, n), 0) == lax.broadcasted_iota(jnp.int32, (n, n), 1)
    return jnp.sum(jnp.where(at, column, 0.0), axis=0, keepdims=True)


CHUNKS = 4


def other_block(i, k):
    mine = (lax.axis_index("gx") >> k) % 2
    return ((i >> k) << (k + 1)) + (i & ((1 << k) - 1)) + ((1 - mine) << k)


def swap_bit(value, k):
    count = lax.axis_size("gx")
    return lax.ppermute(value, "gx", [(i, i ^ (1 << k)) for i in range(count)])


def image_kernel(perm_hbm, dir_hbm, schur_hbm, resid_hbm, basis_hbm, coarse_hbm,
                 image_ref, f0, f1, f2, f3, send_ref, dir_ref, resid_ref, basis_ref, coarse_ref, perm_ref,
                 schur_ref, sems):
    rows = schur_ref.shape[0] // CHUNKS
    parts = [pl.ds(i * rows, rows) for i in range(CHUNKS)]
    pairs = [(dir_hbm, dir_ref), (perm_hbm, perm_ref)]
    pairs += [(schur_hbm.at[part], schur_ref.at[part]) for part in parts]
    pairs += [(coarse_hbm.at[other_block(i, 0)], send_ref.at[i]) for i in range(send_ref.shape[0])]
    pairs += [(resid_hbm, resid_ref), (basis_hbm, basis_ref), (coarse_hbm, coarse_ref)]
    copies = [pltpu.make_async_copy(source, target, sems.at[i]) for i, (source, target) in enumerate(pairs)]
    for copy in copies:
        copy.start()
    copies[0].wait()
    total = None
    for i, part in enumerate(parts):
        copies[2 + i].wait()
        term = jnp.dot(dir_ref[:, part].astype(BF16), schur_ref[part], preferred_element_type=F32)
        total = term if total is None else total + term
    image_ref[...] = total
    copies[1].wait()
    put_faces(perm_ref, total, (f0, f1, f2, f3))
    for copy in copies[2 + CHUNKS :]:
        copy.wait()


def merge_kernel(k, last, blocks_ref, got_ref, out_ref, *send_ref):
    out_ref[...] = blocks_ref[...]
    for i in range(got_ref.shape[0]):
        out_ref[other_block(i, k)] = got_ref[i]
    if not last:
        for i in range(got_ref.shape[0]):
            send_ref[0][i] = out_ref[other_block(i, k + 1)]


def join_kernel(k, depth, prim, blocks_ref, got_ref, wide_ref, all_ref):
    all_ref[...] = blocks_ref[...]
    for i in range(got_ref.shape[0]):
        all_ref[other_block(i, k)] = got_ref[i]
    slabs, rows, width = blocks_ref.shape
    width = width // 2
    for half in range(2):
        for h in range(slabs):
            at = (half * slabs + h) * width
            wide_ref[:, at : at + width] = all_ref[h, :, half * width : (half + 1) * width]
    row = lax.broadcasted_iota(jnp.int32, wide_ref.shape, 0)
    lane = lax.broadcasted_iota(jnp.int32, wide_ref.shape, 1)
    picked = jnp.logical_and(lane < slabs * width, lane % depth == prim // 2)
    wide = jnp.where(row == prim, jnp.where(picked, 1.0, 0.0), wide_ref[...].astype(F32))
    wide_ref[...] = wide.astype(BF16)


def spread_kernel(k, matrix_ref, blocks_ref, send_ref):
    slabs, rows, _ = blocks_ref.shape
    prim = matrix_ref.shape[0] // slabs
    half = prim // 2
    sectors = matrix_ref.shape[1] // prim
    width = blocks_ref.shape[2] // 2
    depth = width // sectors
    source = lax.broadcasted_iota(jnp.int32, (sectors * prim, 2 * width), 0)
    place = lax.broadcasted_iota(jnp.int32, (sectors * prim, 2 * width), 1)
    later = place // width
    within = place % width
    sector, at = within // depth, within % depth
    chosen = jnp.logical_and(at < half, source == sector * prim + later * half + at)
    spread = jnp.dot(matrix_ref[...], jnp.where(chosen, 1.0, 0.0).astype(BF16), preferred_element_type=F32)
    empty = jnp.zeros((rows - prim, 2 * width), F32)
    for g in range(slabs):
        own = jnp.concatenate([spread[g * prim : (g + 1) * prim], empty], axis=0)
        blocks_ref[g] = own.astype(BF16)
    for i in range(send_ref.shape[0]):
        send_ref[i] = blocks_ref[other_block(i, k)]


def conduct_at(row, sector):
    lane = lax.broadcasted_iota(jnp.int32, row.shape, 1)
    return jnp.sum(jnp.where(lane == sector, row, 0.0), axis=1, keepdims=True)


def early_kernel(perm_ref, conduct_ref, dir_ref, image_ref, resid_ref, basis_ref,
                 weight_ref, rhs_ref, curv_ref, scaled_ref):
    slab, sector = lax.axis_index("gx"), lax.axis_index("col")
    slabs, sectors = lax.axis_size("gx"), lax.axis_size("col")
    row = conduct_ref[pl.ds(slab, 1), :]
    own = conduct_at(row, sector)
    below = conduct_at(conduct_ref[pl.ds(jnp.maximum(slab - 1, 0), 1), :], sector)
    above = conduct_at(conduct_ref[pl.ds(jnp.minimum(slab + 1, slabs - 1), 1), :], sector)
    below = jnp.where(slab > 0, below, 0.0)
    above = jnp.where(slab < slabs - 1, above, 0.0)
    left = conduct_at(row, (sector + sectors - 1) % sectors)
    right = conduct_at(row, (sector + 1) % sectors)
    across = [jnp.broadcast_to(own / (own + other), (1, BLK)) for other in (below, above, left, right)]
    places = [slot_place(perm_ref, slot) for slot in range(8)]
    for b in range(weight_ref.shape[1] // BLK):
        weight = across[0]
        for slot in range(2, 8):
            weight = jnp.where(places[slot] == b, across[slot // 2], weight)
        weight_ref[:, b * BLK : (b + 1) * BLK] = jnp.broadcast_to(weight, (8, BLK))
    scaled = (weight_ref[0:1, :] * resid_ref[...]).astype(BF16)
    scaled_ref[...] = scaled
    rhs_ref[...] = lax.dot_general(
        basis_ref[...], scaled, (((1,), (1,)), ((), ())), preferred_element_type=F32
    )
    curv = to_row(jnp.sum(dir_ref[...] * image_ref[...], axis=1, keepdims=True))
    high = curv.astype(BF16).astype(F32)
    n = curv.shape[1]
    curv_ref[...] = jnp.zeros_like(curv_ref)
    curv_ref[0:1, 0:n] = high
    curv_ref[0:1, n : 2 * n] = curv - high


def coarse_rhs_kernel(rows, sectors, perm_ref, image_ref, r0, r1, r2, r3, weight_ref, basis_ref, rhs_ref, curv_ref,
                      assembled_ref, scaled_ref, rhs_q_ref, out_ref):
    for at, part in received_blocks(perm_ref, (r0, r1, r2, r3), image_ref.shape[1] // BLK):
        assembled_ref[:, at] = image_ref[:, at] + part
    scaled = (weight_ref[0:1, :] * assembled_ref[...]).astype(BF16)
    scaled_ref[...] = scaled
    rhs_q = lax.dot_general(
        basis_ref[...], scaled, (((1,), (1,)), ((), ())), preferred_element_type=F32
    )
    rhs_q_ref[...] = rhs_q
    rhs_r = rhs_ref[...]
    half = rhs_r.shape[0] // 2
    packed = jnp.concatenate([rhs_r[:half], rhs_q[:half], rhs_r[half:], rhs_q[half:]], axis=1)
    packed = jnp.concatenate(
        [packed, curv_ref[0:1, :], jnp.zeros((rows - half - 1, BLK), F32)], axis=0
    )
    several = jnp.concatenate([packed] * sectors, axis=0).astype(BF16)
    step = several.shape[0]
    for i in range(out_ref.shape[0] // step):
        out_ref[i * step : (i + 1) * step] = several


def neumann_kernel(scaled_r_ref, scaled_q_ref, resid_ref, assembled_ref, weight_ref, neumann_hbm,
                   sol_r_ref, sol_q_ref, sums_ref, neumann_ref, sems):
    rows = neumann_ref.shape[0] // CHUNKS
    parts = [pl.ds(i * rows, rows) for i in range(CHUNKS)]
    copies = [
        pltpu.make_async_copy(neumann_hbm.at[part], neumann_ref.at[part], sems.at[i])
        for i, part in enumerate(parts)
    ]
    for copy in copies:
        copy.start()
    total_r = total_q = None
    for copy, part in zip(copies, parts):
        copy.wait()
        term_r = jnp.dot(scaled_r_ref[:, part], neumann_ref[part], preferred_element_type=F32)
        term_q = jnp.dot(scaled_q_ref[:, part], neumann_ref[part], preferred_element_type=F32)
        total_r = term_r if total_r is None else total_r + term_r
        total_q = term_q if total_q is None else total_q + term_q
    sol_r_ref[...] = total_r
    sol_q_ref[...] = total_q
    weighted_r = weight_ref[0:1, :] * resid_ref[...]
    weighted_q = weight_ref[0:1, :] * assembled_ref[...]
    n = total_r.shape[0]
    sums_ref[...] = jnp.zeros_like(sums_ref)
    for i, product in enumerate(
        (weighted_r * total_r, weighted_r * total_q + weighted_q * total_r, weighted_q * total_q)
    ):
        sums_ref[0:1, i * n : (i + 1) * n] = to_row(jnp.sum(product, axis=1, keepdims=True))


def solve_kernel(perm_ref, gathered_ref, wide_ref, prev_ref, weight_ref, basis_ref, sol_r_ref, sol_q_ref,
                 sums_ref, rhs_r_ref, rhs_q_ref, step_out, weighted_out, rz_out, f0, f1, f2, f3, rz_ref, sem):
    n = prev_ref.shape[1]
    prim = basis_ref.shape[0]
    halves = jnp.concatenate([gathered_ref[:, : 2 * n], gathered_ref[:, 2 * n :]], axis=0)
    total = jnp.dot(wide_ref[...], halves, preferred_element_type=F32)
    step = prev_ref[...] / (total[prim : prim + 1, 0:n] + total[prim : prim + 1, n : 2 * n])
    coarse_sol = (total[0:prim, 0:n] - step * total[0:prim, n : 2 * n]).astype(BF16)
    coarse_part = coarse_sol.astype(F32) * (rhs_r_ref[...] - step * rhs_q_ref[...])
    partial = (
        sums_ref[0:1, 0:n]
        - step * (sums_ref[0:1, n : 2 * n] - step * sums_ref[0:1, 2 * n : 3 * n])
        + jnp.sum(coarse_part, axis=0, keepdims=True)
    )
    partial = jnp.concatenate([partial, jnp.zeros((1, BLK - n), F32)], axis=1)
    for i in range(rz_ref.shape[0]):
        rz_ref[i] = partial
    copy = pltpu.make_async_copy(rz_ref, rz_out, sem)
    copy.start()
    correction = lax.dot_general(
        coarse_sol, basis_ref[...], (((0,), (0,)), ((), ())), preferred_element_type=F32
    )
    step_col = to_column(step)
    step_out[...] = jnp.broadcast_to(step_col, step_out.shape)
    weighted = weight_ref[0:1, :] * (sol_r_ref[...] - step_col * sol_q_ref[...] + correction)
    weighted_out[...] = weighted
    put_faces(perm_ref, weighted, (f0, f1, f2, f3))
    copy.wait()


def resid_kernel(step_ref, resid_ref, assembled_ref, out_ref):
    out_ref[...] = resid_ref[...] - step_ref[:, 0:1] * assembled_ref[...]


def direction_kernel(perm_ref, partials_ref, rz_ref, dir_ref, weighted_ref, r0, r1, r2, r3,
                     out_ref, rz_out):
    n = rz_ref.shape[1]
    rz_next = jnp.sum(partials_ref[...], axis=0)[:, 0:n]
    rz_out[...] = rz_next
    factor = to_column(rz_next / rz_ref[...])
    for at, part in received_blocks(perm_ref, (r0, r1, r2, r3), dir_ref.shape[1] // BLK):
        out_ref[:, at] = weighted_ref[:, at] + factor * dir_ref[:, at] + part


def body(resid, direction, rz_prev, schur, neumann, basis, coarse_inv, conduct, face_perm):
    resid, direction, schur, neumann = resid[0, 0], direction[0, 0], schur[0, 0], neumann[0, 0]
    basis_t = basis[0, 0].T
    perm = face_perm[0]
    rhs, width = resid.shape
    prim = basis_t.shape[0]
    slabs, sectors = lax.axis_size("gx"), lax.axis_size("col")
    rows = -(-(prim // 2 + 1) // 4) * 4
    block_rows = -(-(prim + 1) // 16) * 16
    rounds = slabs.bit_length() - 1
    face = jax.ShapeDtypeStruct((rhs, 2 * BLK), BF16)
    full = jax.ShapeDtypeStruct((rhs, width), F32)
    rz_row = rz_prev[None, :]
    vmem = pl.BlockSpec(memory_space=VMEM)
    hbm = pl.BlockSpec(memory_space=pltpu.HBM)
    anywhere = pl.BlockSpec(memory_space=pl.ANY)
    flops = 2 * rhs * width * width
    coarse = coarse_inv[0, :, :, 0]
    coarse_type = jax.ShapeDtypeStruct(coarse.shape, BF16)
    send_type = jax.ShapeDtypeStruct((slabs // 2,) + coarse.shape[1:], BF16)
    blocks_type = jax.ShapeDtypeStruct((slabs, block_rows, 2 * sectors * rows), BF16)

    fetched = [pltpu.with_memory_space_constraint(x, pltpu.HBM) for x in (perm, direction, schur, resid, basis_t, coarse)]
    image, f0, f1, f2, f3, send, direction, resid, basis_t, coarse = pl.pallas_call(
        image_kernel,
        out_shape=(full,) + (face,) * 4
        + (send_type, full, full, jax.ShapeDtypeStruct((prim, width), BF16), coarse_type),
        in_specs=[hbm] * 6, out_specs=(vmem,) * 10,
        scratch_shapes=[
            pltpu.VMEM(perm.shape, jnp.int32),
            pltpu.VMEM((width, width), BF16),
            pltpu.SemaphoreType.DMA((CHUNKS + 5 + slabs // 2,)),
        ],
        compiler_params=params(), cost_estimate=cost(flops, 2 * width * width),
    )(*fetched)
    received = swap_faces((f0, f1, f2, f3))
    weight, rhs_r, curv, scaled_r = pl.pallas_call(
        early_kernel,
        out_shape=(
            jax.ShapeDtypeStruct((8, width), F32),
            jax.ShapeDtypeStruct((prim, rhs), F32),
            jax.ShapeDtypeStruct((8, BLK), F32),
            jax.ShapeDtypeStruct((rhs, width), BF16),
        ),
        in_specs=[vmem] * 6, out_specs=(vmem,) * 4, compiler_params=params(),
        cost_estimate=cost(2 * rhs * width * prim, 8 * rhs * width),
    )(perm, conduct, direction, image, resid, basis_t)
    for k in range(rounds - 1):
        got = swap_bit(send, k)
        last = k + 2 == rounds
        coarse, *send = pl.pallas_call(
            functools.partial(merge_kernel, k, last),
            out_shape=(coarse_type,) if last else (coarse_type, send_type),
            in_specs=[vmem] * 2, out_specs=(vmem,) if last else (vmem,) * 2,
            compiler_params=params(), cost_estimate=cost(1 << 10, 1 << 16),
        )(coarse, got)
        send = send[0] if send else None
    blocks, send = pl.pallas_call(
        functools.partial(spread_kernel, rounds - 1),
        out_shape=(blocks_type, jax.ShapeDtypeStruct((slabs // 2,) + blocks_type.shape[1:], BF16)),
        in_specs=[vmem], out_specs=(vmem,) * 2,
        compiler_params=params(), cost_estimate=cost(1 << 20, 1 << 16),
    )(coarse.reshape(slabs * prim, sectors * prim))
    wide = pl.pallas_call(
        functools.partial(join_kernel, rounds - 1, rows, prim),
        out_shape=jax.ShapeDtypeStruct((block_rows, slabs * blocks_type.shape[2]), BF16),
        in_specs=[vmem] * 2, out_specs=vmem,
        scratch_shapes=[pltpu.VMEM(blocks_type.shape, BF16)],
        compiler_params=params(), cost_estimate=cost(1 << 10, 1 << 16),
    )(blocks, swap_bit(send, rounds - 1))
    assembled, scaled_q, rhs_q, packed = pl.pallas_call(
        functools.partial(coarse_rhs_kernel, rows, sectors),
        out_shape=(
            full,
            jax.ShapeDtypeStruct((rhs, width), BF16),
            jax.ShapeDtypeStruct((prim, rhs), F32),
            jax.ShapeDtypeStruct((slabs * sectors * rows, BLK), BF16),
        ),
        in_specs=[vmem] + [vmem] * 9, out_specs=(vmem,) * 4, compiler_params=params(),
        cost_estimate=cost(2 * rhs * width * prim, 8 * rhs * width),
    )(perm, image, *received, weight, basis_t, rhs_r, curv)
    packed = packed.reshape(slabs * sectors, rows // 2, 2, BLK)
    gathered = lax.all_to_all(packed, ("gx", "col"), 0, 0).reshape(slabs * sectors * rows, BLK)
    sol_r, sol_q, sums = pl.pallas_call(
        neumann_kernel,
        out_shape=(full, full, jax.ShapeDtypeStruct((8, BLK), F32)),
        in_specs=[vmem] * 5 + [hbm], out_specs=(vmem,) * 3,
        scratch_shapes=[pltpu.VMEM((width, width), BF16), pltpu.SemaphoreType.DMA((CHUNKS,))],
        compiler_params=params(), cost_estimate=cost(1000 * flops, 2 * width * width),
    )(scaled_r, scaled_q, resid, assembled, weight, pltpu.with_memory_space_constraint(neumann, pltpu.HBM))
    step, weighted, partial, *faces = pl.pallas_call(
        solve_kernel,
        out_shape=(
            jax.ShapeDtypeStruct((rhs, BLK), F32),
            full,
            jax.ShapeDtypeStruct((slabs * sectors, 1, BLK), F32),
        )
        + (face,) * 4,
        in_specs=[vmem] * 11, out_specs=(vmem, vmem, anywhere) + (vmem,) * 4,
        scratch_shapes=[pltpu.VMEM((slabs * sectors, 1, BLK), F32), pltpu.SemaphoreType.DMA],
        compiler_params=params(), cost_estimate=cost(2 * rhs * width * prim, 8 * rhs * width),
    )(perm, gathered, wide, rz_row, weight, basis_t, sol_r, sol_q, sums, rhs_r, rhs_q)
    partials = lax.all_to_all(partial, ("gx", "col"), 0, 0)
    received = swap_faces(faces)
    resid_new = pl.pallas_call(
        resid_kernel, out_shape=full, in_specs=[vmem] * 3, out_specs=vmem,
        compiler_params=params(), cost_estimate=cost(2 * rhs * width, 12 * rhs * width),
    )(step, resid, assembled)
    direction_new, rz_next = pl.pallas_call(
        direction_kernel, out_shape=(full, jax.ShapeDtypeStruct((1, rhs), F32)),
        in_specs=[vmem] + [vmem] * 8, out_specs=(vmem,) * 2, compiler_params=params(),
        cost_estimate=cost(2 * rhs * width, 8 * rhs * width),
    )(perm, partials, rz_row, direction, weighted, *received)
    return (resid_new[None, None], direction_new[None, None], rz_next[0])


def solution(mesh):
    placed = (
        P("gx", "col", None, None),
        P("gx", "col", None, None),
        P(),
        P("gx", "col", None, None),
        P("gx", "col", None, None),
        P("gx", "col", None, None),
        P("col", None, None, "gx", None, None),
        P(),
        P("gx", "col", None),
    )
    return jax.shard_map(
        body,
        mesh=mesh,
        in_specs=placed,
        out_specs=(P("gx", "col", None, None), P("gx", "col", None, None), P()),
        check_vma=False,
    )
```

```python
import functools

import jax
import jax.numpy as jnp
from jax import lax
from jax.experimental import pallas as pl
from jax.experimental.pallas import tpu as pltpu
from jax.sharding import PartitionSpec as P

F32 = jnp.float32
BF16 = jnp.bfloat16
BLK = 128
EXACT = lax.Precision.HIGHEST
VMEM = pltpu.VMEM


def params(limit=16 * 1024 * 1024):
    return pltpu.CompilerParams(vmem_limit_bytes=limit)


def cost(flops, nbytes):
    return pl.CostEstimate(flops=flops, bytes_accessed=nbytes, transcendentals=0)


def swap(value, axis, offset):
    count = lax.axis_size(axis)
    pairs = []
    for low in range(offset, count, 2):
        high = (low + 1) % count
        pairs += [(low, high), (high, low)]
    return lax.ppermute(value, axis, pairs)


def swap_second(value):
    slabs, sectors = lax.axis_size("gx"), lax.axis_size("col")
    pairs = []
    for slab in range(slabs):
        for sector in range(sectors):
            other = (slab + 1 if slab % 2 else slab - 1, sector)
            if not 0 <= other[0] < slabs:
                other = (slab, sector ^ 1)
            pairs.append((slab * sectors + sector, other[0] * sectors + other[1]))
    return lax.ppermute(value, ("gx", "col"), pairs)


def swap_faces(faces):
    return (
        swap(faces[0], "col", 1),
        swap(faces[1], "col", 0),
        swap_second(faces[2]),
        swap(faces[3], "gx", 0),
    )


def swap_counts():
    slab = lax.axis_index("gx")
    inside = jnp.logical_and(slab > 0, slab < lax.axis_size("gx") - 1)
    return (None, None, inside, None)


def slot_place(perm_ref, slot):
    return jnp.broadcast_to(perm_ref[0:1, slot : slot + 1], (1, BLK))


def swapped_places(perm_ref):
    slab = lax.axis_index("gx") % 2
    sector = lax.axis_index("col") % 2
    places = []
    for parity, even, odd in ((sector, 2, 3), (sector, 3, 2), (slab, 0, 1), (slab, 1, 0)):
        for j in range(2):
            at_even, at_odd = (slot_place(perm_ref, 2 * face + j) for face in (even, odd))
            places.append(jnp.where(parity == 0, at_even, at_odd))
    return places


def put_faces(perm_ref, source, outs):
    blocks = [source[:, b * BLK : (b + 1) * BLK] for b in range(source.shape[1] // BLK)]
    for i, place in enumerate(swapped_places(perm_ref)):
        chosen = blocks[0]
        for b in range(1, len(blocks)):
            chosen = jnp.where(place == b, blocks[b], chosen)
        j = i % 2
        outs[i // 2][0 : chosen.shape[0], j * BLK : (j + 1) * BLK] = chosen.astype(BF16)


def received_blocks(perm_ref, received, blocks):
    places = swapped_places(perm_ref)
    parts = []
    for i in range(len(places)):
        j = i % 2
        part = received[i // 2][:, j * BLK : (j + 1) * BLK].astype(F32)
        counts = swap_counts()[i // 2]
        parts.append(part if counts is None else jnp.where(counts, part, 0.0))
    for b in range(blocks):
        chosen = parts[0]
        for place, part in zip(places[1:], parts[1:]):
            chosen = jnp.where(place == b, part, chosen)
        yield slice(b * BLK, (b + 1) * BLK), chosen


def to_column(row):
    n = row.shape[1]
    at = lax.broadcasted_iota(jnp.int32, (n, n), 0) == lax.broadcasted_iota(jnp.int32, (n, n), 1)
    return jnp.sum(jnp.where(at, row, 0.0), axis=1, keepdims=True)


def to_row(column):
    n = column.shape[0]
    at = lax.broadcasted_iota(jnp.int32, (n, n), 0) == lax.broadcasted_iota(jnp.int32, (n, n), 1)
    return jnp.sum(jnp.where(at, column, 0.0), axis=0, keepdims=True)


CHUNKS = 4


def other_block(i, k):
    mine = (lax.axis_index("gx") >> k) % 2
    return ((i >> k) << (k + 1)) + (i & ((1 << k) - 1)) + ((1 - mine) << k)


def swap_bit(value, k):
    count = lax.axis_size("gx")
    return lax.ppermute(value, "gx", [(i, i ^ (1 << k)) for i in range(count)])


def image_kernel(perm_hbm, dir_hbm, schur_hbm, resid_hbm, basis_hbm, coarse_hbm,
                 image_ref, f0, f1, f2, f3, dir_ref, resid_ref, basis_ref, coarse_ref, *rest):
    *send_ref, perm_ref, schur_ref, sems = rest
    rows = schur_ref.shape[0] // CHUNKS
    parts = [pl.ds(i * rows, rows) for i in range(CHUNKS)]
    pairs = [(dir_hbm, dir_ref), (perm_hbm, perm_ref)]
    pairs += [(schur_hbm.at[part], schur_ref.at[part]) for part in parts]
    for ref in send_ref:
        pairs += [(coarse_hbm.at[other_block(i, 0)], ref.at[i]) for i in range(ref.shape[0])]
    pairs += [(resid_hbm, resid_ref), (basis_hbm, basis_ref), (coarse_hbm, coarse_ref)]
    copies = [pltpu.make_async_copy(source, target, sems.at[i]) for i, (source, target) in enumerate(pairs)]
    for copy in copies:
        copy.start()
    copies[0].wait()
    total = None
    for i, part in enumerate(parts):
        copies[2 + i].wait()
        term = jnp.dot(dir_ref[:, part].astype(BF16), schur_ref[part], preferred_element_type=F32)
        total = term if total is None else total + term
    image_ref[...] = total
    copies[1].wait()
    put_faces(perm_ref, total, (f0, f1, f2, f3))
    for copy in copies[2 + CHUNKS :]:
        copy.wait()


def merge_kernel(k, last, blocks_ref, got_ref, out_ref, *send_ref):
    out_ref[...] = blocks_ref[...]
    for i in range(got_ref.shape[0]):
        out_ref[other_block(i, k)] = got_ref[i]
    if not last:
        for i in range(got_ref.shape[0]):
            send_ref[0][i] = out_ref[other_block(i, k + 1)]


def join_kernel(k, depth, prim, blocks_ref, got_ref, wide_ref, all_ref):
    all_ref[...] = blocks_ref[...]
    for i in range(got_ref.shape[0]):
        all_ref[other_block(i, k)] = got_ref[i]
    slabs, rows, width = blocks_ref.shape
    width = width // 2
    for half in range(2):
        for h in range(slabs):
            at = (half * slabs + h) * width
            wide_ref[:, at : at + width] = all_ref[h, :, half * width : (half + 1) * width]
    row = lax.broadcasted_iota(jnp.int32, wide_ref.shape, 0)
    lane = lax.broadcasted_iota(jnp.int32, wide_ref.shape, 1)
    picked = jnp.logical_and(lane < slabs * width, lane % depth == prim // 2)
    wide = jnp.where(row == prim, jnp.where(picked, 1.0, 0.0), wide_ref[...].astype(F32))
    wide_ref[...] = wide.astype(BF16)


def spread_kernel(k, matrix_ref, blocks_ref, send_ref):
    slabs, rows, _ = blocks_ref.shape
    prim = matrix_ref.shape[0] // slabs
    half = prim // 2
    sectors = matrix_ref.shape[1] // prim
    width = blocks_ref.shape[2] // 2
    depth = width // sectors
    source = lax.broadcasted_iota(jnp.int32, (sectors * prim, 2 * width), 0)
    place = lax.broadcasted_iota(jnp.int32, (sectors * prim, 2 * width), 1)
    later = place // width
    within = place % width
    sector, at = within // depth, within % depth
    chosen = jnp.logical_and(at < half, source == sector * prim + later * half + at)
    spread = jnp.dot(matrix_ref[...], jnp.where(chosen, 1.0, 0.0).astype(BF16), preferred_element_type=F32)
    empty = jnp.zeros((rows - prim, 2 * width), F32)
    for g in range(slabs):
        own = jnp.concatenate([spread[g * prim : (g + 1) * prim], empty], axis=0)
        blocks_ref[g] = own.astype(BF16)
    for i in range(send_ref.shape[0]):
        send_ref[i] = blocks_ref[other_block(i, k)]


def conduct_at(row, sector):
    lane = lax.broadcasted_iota(jnp.int32, row.shape, 1)
    return jnp.sum(jnp.where(lane == sector, row, 0.0), axis=1, keepdims=True)


def early_kernel(perm_ref, conduct_ref, dir_ref, image_ref, resid_ref, basis_ref,
                 weight_ref, rhs_ref, curv_ref, scaled_ref):
    slab, sector = lax.axis_index("gx"), lax.axis_index("col")
    slabs, sectors = lax.axis_size("gx"), lax.axis_size("col")
    row = conduct_ref[pl.ds(slab, 1), :]
    own = conduct_at(row, sector)
    below = conduct_at(conduct_ref[pl.ds(jnp.maximum(slab - 1, 0), 1), :], sector)
    above = conduct_at(conduct_ref[pl.ds(jnp.minimum(slab + 1, slabs - 1), 1), :], sector)
    below = jnp.where(slab > 0, below, 0.0)
    above = jnp.where(slab < slabs - 1, above, 0.0)
    left = conduct_at(row, (sector + sectors - 1) % sectors)
    right = conduct_at(row, (sector + 1) % sectors)
    across = [jnp.broadcast_to(own / (own + other), (1, BLK)) for other in (below, above, left, right)]
    places = [slot_place(perm_ref, slot) for slot in range(8)]
    for b in range(weight_ref.shape[1] // BLK):
        weight = across[0]
        for slot in range(2, 8):
            weight = jnp.where(places[slot] == b, across[slot // 2], weight)
        weight_ref[:, b * BLK : (b + 1) * BLK] = jnp.broadcast_to(weight, (8, BLK))
    scaled = (weight_ref[0:1, :] * resid_ref[...]).astype(BF16)
    scaled_ref[...] = scaled
    rhs_ref[...] = lax.dot_general(
        basis_ref[...], scaled, (((1,), (1,)), ((), ())), preferred_element_type=F32
    )
    curv = to_row(jnp.sum(dir_ref[...] * image_ref[...], axis=1, keepdims=True))
    high = curv.astype(BF16).astype(F32)
    n = curv.shape[1]
    curv_ref[...] = jnp.zeros_like(curv_ref)
    curv_ref[0:1, 0:n] = high
    curv_ref[0:1, n : 2 * n] = curv - high


def coarse_rhs_kernel(rows, sectors, perm_ref, image_ref, r0, r1, r2, r3, weight_ref, basis_ref, rhs_ref, curv_ref,
                      assembled_ref, scaled_ref, rhs_q_ref, out_ref):
    for at, part in received_blocks(perm_ref, (r0, r1, r2, r3), image_ref.shape[1] // BLK):
        assembled_ref[:, at] = image_ref[:, at] + part
    scaled = (weight_ref[0:1, :] * assembled_ref[...]).astype(BF16)
    scaled_ref[...] = scaled
    rhs_q = lax.dot_general(
        basis_ref[...], scaled, (((1,), (1,)), ((), ())), preferred_element_type=F32
    )
    rhs_q_ref[...] = rhs_q
    rhs_r = rhs_ref[...]
    half = rhs_r.shape[0] // 2
    packed = jnp.concatenate([rhs_r[:half], rhs_q[:half], rhs_r[half:], rhs_q[half:]], axis=1)
    packed = jnp.concatenate(
        [packed, curv_ref[0:1, :], jnp.zeros((rows - half - 1, BLK), F32)], axis=0
    )
    several = jnp.concatenate([packed] * sectors, axis=0).astype(BF16)
    step = several.shape[0]
    for i in range(out_ref.shape[0] // step):
        out_ref[i * step : (i + 1) * step] = several


def neumann_kernel(scaled_r_ref, scaled_q_ref, resid_ref, assembled_ref, weight_ref, neumann_hbm,
                   sol_r_ref, sol_q_ref, sums_ref, neumann_ref, sems):
    rows = neumann_ref.shape[0] // CHUNKS
    parts = [pl.ds(i * rows, rows) for i in range(CHUNKS)]
    copies = [
        pltpu.make_async_copy(neumann_hbm.at[part], neumann_ref.at[part], sems.at[i])
        for i, part in enumerate(parts)
    ]
    for copy in copies:
        copy.start()
    total_r = total_q = None
    for copy, part in zip(copies, parts):
        copy.wait()
        term_r = jnp.dot(scaled_r_ref[:, part], neumann_ref[part], preferred_element_type=F32)
        term_q = jnp.dot(scaled_q_ref[:, part], neumann_ref[part], preferred_element_type=F32)
        total_r = term_r if total_r is None else total_r + term_r
        total_q = term_q if total_q is None else total_q + term_q
    sol_r_ref[...] = total_r
    sol_q_ref[...] = total_q
    weighted_r = weight_ref[0:1, :] * resid_ref[...]
    weighted_q = weight_ref[0:1, :] * assembled_ref[...]
    n = total_r.shape[0]
    sums_ref[...] = jnp.zeros_like(sums_ref)
    for i, product in enumerate(
        (weighted_r * total_r, weighted_r * total_q + weighted_q * total_r, weighted_q * total_q)
    ):
        sums_ref[0:1, i * n : (i + 1) * n] = to_row(jnp.sum(product, axis=1, keepdims=True))


def solve_kernel(perm_ref, gathered_ref, wide_ref, prev_ref, weight_ref, basis_ref, sol_r_ref, sol_q_ref,
                 sums_ref, rhs_r_ref, rhs_q_ref, step_out, weighted_out, rz_out, f0, f1, f2, f3, rz_ref, sem):
    n = prev_ref.shape[1]
    prim = basis_ref.shape[0]
    halves = jnp.concatenate([gathered_ref[:, : 2 * n], gathered_ref[:, 2 * n :]], axis=0)
    total = jnp.dot(wide_ref[...], halves, preferred_element_type=F32)
    step = prev_ref[...] / (total[prim : prim + 1, 0:n] + total[prim : prim + 1, n : 2 * n])
    coarse_sol = (total[0:prim, 0:n] - step * total[0:prim, n : 2 * n]).astype(BF16)
    coarse_part = coarse_sol.astype(F32) * (rhs_r_ref[...] - step * rhs_q_ref[...])
    partial = (
        sums_ref[0:1, 0:n]
        - step * (sums_ref[0:1, n : 2 * n] - step * sums_ref[0:1, 2 * n : 3 * n])
        + jnp.sum(coarse_part, axis=0, keepdims=True)
    )
    partial = jnp.concatenate([partial, jnp.zeros((1, BLK - n), F32)], axis=1)
    for i in range(rz_ref.shape[0]):
        rz_ref[i] = partial
    copy = pltpu.make_async_copy(rz_ref, rz_out, sem)
    copy.start()
    correction = lax.dot_general(
        coarse_sol, basis_ref[...], (((0,), (0,)), ((), ())), preferred_element_type=F32
    )
    step_col = to_column(step)
    step_out[...] = jnp.broadcast_to(step_col, step_out.shape)
    weighted = weight_ref[0:1, :] * (sol_r_ref[...] - step_col * sol_q_ref[...] + correction)
    weighted_out[...] = weighted
    put_faces(perm_ref, weighted, (f0, f1, f2, f3))
    copy.wait()


def resid_kernel(step_ref, resid_ref, assembled_ref, out_ref):
    out_ref[...] = resid_ref[...] - step_ref[:, 0:1] * assembled_ref[...]


def direction_kernel(perm_ref, partials_ref, rz_ref, dir_ref, weighted_ref, r0, r1, r2, r3,
                     out_ref, rz_out):
    n = rz_ref.shape[1]
    rz_next = jnp.sum(partials_ref[...], axis=0)[:, 0:n]
    rz_out[...] = rz_next
    factor = to_column(rz_next / rz_ref[...])
    for at, part in received_blocks(perm_ref, (r0, r1, r2, r3), dir_ref.shape[1] // BLK):
        out_ref[:, at] = weighted_ref[:, at] + factor * dir_ref[:, at] + part


def split(value):
    high = value.astype(BF16).astype(F32)
    return high, value - high


def spread_pair_kernel(after_ref, own_ref, mate_ref, out_ref):
    slabs = lax.axis_size("gx")
    prim = own_ref.shape[0] // slabs
    half = prim // 2
    sectors = own_ref.shape[1] // prim
    width = out_ref.shape[2] // 2
    depth = width // sectors
    source = lax.broadcasted_iota(jnp.int32, (sectors * prim, 2 * width), 0)
    place = lax.broadcasted_iota(jnp.int32, (sectors * prim, 2 * width), 1)
    later = place // width
    within = place % width
    sector, at = within // depth, within % depth
    chosen = jnp.logical_and(at < half, source == sector * prim + later * half + at)
    chosen = jnp.where(chosen, 1.0, 0.0).astype(BF16)
    mine = lax.axis_index("gx") % 2
    for ref, bit in ((own_ref, mine), (mate_ref, 1 - mine)):
        out_ref[bit] = jnp.dot(ref[...], chosen, preferred_element_type=F32).astype(BF16)


def gather_kernel(k, after_ref, mine_ref, got_ref, out_ref, both_ref):
    bit = (lax.axis_index("gx") >> k) % 2
    n = mine_ref.shape[0]
    for i in range(n):
        both_ref[bit * n + i] = mine_ref[i]
        both_ref[(1 - bit) * n + i] = got_ref[i]
    out_ref[...] = jnp.concatenate([both_ref[i] for i in range(2 * n)], axis=1)


def sector_kernel(prim, depth, width, up, mine_ref, got_ref, wide_ref):
    slabs = lax.axis_size("gx")
    rows = slabs * up
    half = prim // 2
    top = (lax.axis_index("gx") * 2) // slabs
    low = jnp.where(top == 0, mine_ref[...].astype(F32), got_ref[...].astype(F32))
    high = jnp.where(top == 0, got_ref[...].astype(F32), mine_ref[...].astype(F32))
    pieces = []
    for part in range(2):
        for h in range(slabs):
            source = low if h < slabs // 2 else high
            at = h % (slabs // 2) * 2 * width + part * width
            pieces.append(source[:, at : at + width])
    flat = jnp.concatenate(pieces, axis=1)
    empty = jnp.zeros((up - prim, flat.shape[1]), F32)
    parts = []
    for g in range(slabs):
        parts += [flat[g * prim : (g + 1) * prim], empty]
    wide_ref[0:rows, :] = jnp.concatenate(parts, axis=0).astype(BF16)
    shape = (wide_ref.shape[0] - rows, wide_ref.shape[1])
    row = lax.broadcasted_iota(jnp.int32, shape, 0)
    lane = lax.broadcasted_iota(jnp.int32, shape, 1)
    part = lane // (slabs * width)
    at = lane % depth
    slab = lane // width % slabs
    sector = lane % width // depth
    sums = jnp.logical_and(at >= half, row == (at - half) * 2 + part)
    mine = jnp.logical_and(sector == lax.axis_index("col"), at < half)
    own = jnp.logical_and(mine, row == 16 + slab * up + part * half + at)
    wide_ref[rows:, :] = jnp.where(jnp.logical_or(sums, own), 1.0, 0.0).astype(BF16)


def near_rhs_kernel(rows, sectors, perm_ref, image_ref, r0, r1, r2, r3, weight_ref, basis_ref, rhs_ref, curv_ref,
                    scaled_ref, resid_ref, neumann_ref, assembled_ref, sol_r_ref, sol_q_ref, out_ref):
    for at, part in received_blocks(perm_ref, (r0, r1, r2, r3), image_ref.shape[1] // BLK):
        assembled_ref[:, at] = image_ref[:, at] + part
    weighted_r = weight_ref[0:1, :] * resid_ref[...]
    weighted_q = weight_ref[0:1, :] * assembled_ref[...]
    scaled = weighted_q.astype(BF16)
    n = scaled.shape[0]
    both = jnp.concatenate([scaled_ref[...], scaled], axis=0)
    sol = jnp.dot(both, neumann_ref[...], preferred_element_type=F32)
    rhs_q = lax.dot_general(
        basis_ref[...], scaled, (((1,), (1,)), ((), ())), preferred_element_type=F32
    )
    sol_r, sol_q = sol[:n], sol[n:]
    sol_r_ref[...] = sol_r
    sol_q_ref[...] = sol_q
    products = (weighted_r * sol_r, weighted_r * sol_q + weighted_q * sol_r, weighted_q * sol_q)
    sums = [to_row(jnp.sum(product, axis=1, keepdims=True)) for product in products]
    first = jnp.concatenate([curv_ref[0:1, : 2 * n], *split(sums[0])], axis=1)
    second = jnp.concatenate([*split(sums[1]), *split(sums[2])], axis=1)
    rhs_r = rhs_ref[...]
    half = rhs_r.shape[0] // 2
    packed = jnp.concatenate([rhs_r[:half], rhs_q[:half], rhs_r[half:], rhs_q[half:]], axis=1)
    packed = jnp.concatenate([packed, first, second], axis=0)
    several = jnp.concatenate([packed] * sectors, axis=0).astype(BF16)
    step = several.shape[0]
    for i in range(out_ref.shape[0] // step):
        out_ref[i * step : (i + 1) * step] = several


def weigh_kernel(weight_ref, r_ref, q_ref, r_out, q_out):
    r_out[...] = weight_ref[0:1, :] * r_ref[...]
    q_out[...] = weight_ref[0:1, :] * q_ref[...]


def near_solve_kernel(perm_ref, gathered_ref, wide_ref, prev_ref, weight_ref, basis_ref, sol_r_ref, sol_q_ref,
                      step_out, weighted_out, base_out, part_out, f0, f1, f2, f3, sol_ref):
    n = prev_ref.shape[1]
    prim = basis_ref.shape[0]
    slabs = lax.axis_size("gx")
    rows = (wide_ref.shape[0] - 16) // 2
    up = rows // slabs
    halves = jnp.concatenate([gathered_ref[:, : 2 * n], gathered_ref[:, 2 * n :]], axis=0)
    total = jnp.dot(wide_ref[...], halves, preferred_element_type=F32)
    curvature, first, second, third = (
        total[rows + i : rows + i + 1, 0:n] + total[rows + i : rows + i + 1, n : 2 * n] for i in range(4)
    )
    step = prev_ref[...] / curvature
    sol = (total[0:rows, 0:n] - step * total[0:rows, n : 2 * n]).astype(BF16).astype(F32)
    sol_ref[...] = sol
    rhs = total[rows + 16 :, 0:n] - step * total[rows + 16 :, n : 2 * n]
    high, low = split(jnp.sum(sol * rhs, axis=0, keepdims=True))
    own = sol_ref[pl.ds(pl.multiple_of(lax.axis_index("gx") * up, 8), up), :].astype(BF16)
    correction = lax.dot_general(
        own[0:prim], basis_ref[...], (((0,), (0,)), ((), ())), preferred_element_type=F32
    )
    step_col = to_column(step)
    step_out[...] = jnp.broadcast_to(step_col, step_out.shape)
    weighted = sol_r_ref[...] - step_col * sol_q_ref[...] + weight_ref[0:1, :] * correction
    weighted_out[...] = weighted
    blank = jnp.zeros((1, BLK - n), F32)
    low = low.astype(BF16).astype(F32)
    base = first - step * (second - step * third)
    base_out[...] = jnp.broadcast_to(jnp.concatenate([base, blank], axis=1), base_out.shape)
    part_out[...] = jnp.broadcast_to(jnp.concatenate([high + low, blank], axis=1), part_out.shape)
    put_faces(perm_ref, weighted, (f0, f1, f2, f3))
    lines = jnp.concatenate([high, low, jnp.zeros((14, n), F32)], axis=0)
    lines = jnp.concatenate([lines, jnp.zeros((16, 2 * BLK - n), F32)], axis=1).astype(BF16)
    f0[n:, :] = lines
    f1[n:, :] = lines


def near_direction_kernel(perm_ref, rz_ref, dir_ref, weighted_ref, base_ref, part_ref, r0, r1, r2, r3, far_ref,
                          out_ref, rz_out):
    n = rz_ref.shape[1]
    sector = lax.axis_index("col")
    beside = jnp.where(sector % 2 == 1, (sector + 1) % 4, (sector + 3) % 4)
    parts = [(sector, part_ref[0:1, 0:n]), (sector ^ 2, far_ref[0:1, 0:n])]
    for ref, other in ((r0, beside), (r1, sector ^ 1)):
        lines = ref[n : n + 16, 0:n].astype(F32)
        parts.append((other, lines[0:1] + lines[1:2]))
    rz_next = base_ref[0:1, 0:n]
    for at in range(4):
        value = parts[0][1]
        for other, part in parts[1:]:
            value = jnp.where(other == at, part, value)
        rz_next = rz_next + value
    rz_out[...] = rz_next
    factor = to_column(rz_next / rz_ref[...])
    received = (r0[0:n, :], r1[0:n, :], r2[...], r3[...])
    for at, part in received_blocks(perm_ref, received, dir_ref.shape[1] // BLK):
        out_ref[:, at] = weighted_ref[:, at] + factor * dir_ref[:, at] + part


def near_rest(perm, rz_row, neumann, image, received, weight, rhs_r, curv, scaled_r, direction, resid, basis_t,
              coarse, rows):
    rhs, width = resid.shape
    prim = basis_t.shape[0]
    slabs, sectors = lax.axis_size("gx"), lax.axis_size("col")
    up = -(-prim // 8) * 8
    vmem = pl.BlockSpec(memory_space=VMEM)
    full = jax.ShapeDtypeStruct((rhs, width), F32)
    line = jax.ShapeDtypeStruct((8, BLK), F32)
    small = cost(1 << 10, 1 << 16)

    def call(kernel, outs, *args, scratch=(), estimate=small, after=()):
        return pl.pallas_call(
            kernel, out_shape=outs, in_specs=[pl.BlockSpec(memory_space=pl.ANY)] * len(after) + [vmem] * len(args),
            out_specs=(vmem,) * len(outs), scratch_shapes=scratch, compiler_params=params(), cost_estimate=estimate,
        )(*after, *args)

    mate = swap_bit(coarse, 0)
    flat = (slabs * prim, sectors * prim)
    shard = (slabs * prim, 2 * sectors * rows)
    (blocks,) = call(
        spread_pair_kernel, (jax.ShapeDtypeStruct((2,) + shard, BF16),),
        coarse.reshape(flat), mate.reshape(flat), after=(perm,),
    )
    assembled, sol_r, sol_q, packed = call(
        functools.partial(near_rhs_kernel, rows, sectors),
        (full, full, full, jax.ShapeDtypeStruct((slabs * sectors * rows, BLK), BF16)),
        perm, image, *received, weight, basis_t, rhs_r, curv, scaled_r, resid, neumann,
        estimate=cost(2000 * rhs * width * width, 1 << 16),
    )
    (blocks,) = call(
        functools.partial(gather_kernel, 1), (jax.ShapeDtypeStruct((shard[0], 4 * shard[1]), BF16),),
        blocks, swap_bit(blocks, 1), after=(packed,), scratch=[pltpu.VMEM((4,) + shard, BF16)],
        estimate=cost(2000 * rhs * width * width, 1 << 16),
    )
    (wide,) = call(
        functools.partial(sector_kernel, prim, rows, shard[1] // 2, up),
        (jax.ShapeDtypeStruct((2 * slabs * up + 16, slabs * shard[1]), BF16),), blocks, swap_bit(blocks, 2),
    )
    packed = packed.reshape(slabs * sectors, rows // 2, 2, BLK)
    gathered = lax.all_to_all(packed, ("gx", "col"), 0, 0).reshape(slabs * sectors * rows, BLK)
    sol_r, sol_q = call(
        weigh_kernel, (full, full), weight, sol_r, sol_q,
    )
    face = jax.ShapeDtypeStruct((rhs, 2 * BLK), BF16)
    tall = jax.ShapeDtypeStruct((rhs + 16, 2 * BLK), BF16)
    step, weighted, base, part, *faces = call(
        near_solve_kernel,
        (jax.ShapeDtypeStruct((rhs, BLK), F32), full, line, line, tall, tall, face, face),
        perm, gathered, wide, rz_row, weight, basis_t, sol_r, sol_q,
        scratch=[pltpu.VMEM((slabs * up, rhs), F32)],
    )
    received = swap_faces(faces)
    far = lax.ppermute(part, "col", [(i, i ^ 2) for i in range(sectors)])
    (resid_new,) = call(resid_kernel, (full,), step, resid, assembled)
    direction_new, rz_next = call(
        near_direction_kernel, (full, jax.ShapeDtypeStruct((1, rhs), F32)),
        perm, rz_row, direction, weighted, base, part, *received, far,
    )
    return (resid_new[None, None], direction_new[None, None], rz_next[0])


def body(resid, direction, rz_prev, schur, neumann, basis, coarse_inv, conduct, face_perm):
    resid, direction, schur, neumann = resid[0, 0], direction[0, 0], schur[0, 0], neumann[0, 0]
    basis_t = basis[0, 0].T
    perm = face_perm[0]
    rhs, width = resid.shape
    prim = basis_t.shape[0]
    slabs, sectors = lax.axis_size("gx"), lax.axis_size("col")
    rows = -(-(prim // 2 + 1) // 4) * 4
    block_rows = -(-(prim + 1) // 16) * 16
    rounds = slabs.bit_length() - 1
    face = jax.ShapeDtypeStruct((rhs, 2 * BLK), BF16)
    full = jax.ShapeDtypeStruct((rhs, width), F32)
    rz_row = rz_prev[None, :]
    vmem = pl.BlockSpec(memory_space=VMEM)
    hbm = pl.BlockSpec(memory_space=pltpu.HBM)
    anywhere = pl.BlockSpec(memory_space=pl.ANY)
    flops = 2 * rhs * width * width
    coarse = coarse_inv[0, :, :, 0]
    coarse_type = jax.ShapeDtypeStruct(coarse.shape, BF16)
    send_type = jax.ShapeDtypeStruct((slabs // 2,) + coarse.shape[1:], BF16)
    blocks_type = jax.ShapeDtypeStruct((slabs, block_rows, 2 * sectors * rows), BF16)

    near = sectors == 4 and slabs == 8
    sends = () if near else (send_type,)
    fetched = [pltpu.with_memory_space_constraint(x, pltpu.HBM) for x in (perm, direction, schur, resid, basis_t, coarse)]
    image, f0, f1, f2, f3, direction, resid, basis_t, coarse, *send = pl.pallas_call(
        image_kernel,
        out_shape=(full,) + (face,) * 4
        + (full, full, jax.ShapeDtypeStruct((prim, width), BF16), coarse_type) + sends,
        in_specs=[hbm] * 6, out_specs=(vmem,) * (9 + len(sends)),
        scratch_shapes=[
            pltpu.VMEM(perm.shape, jnp.int32),
            pltpu.VMEM((width, width), BF16),
            pltpu.SemaphoreType.DMA((CHUNKS + 5 + len(sends) * (slabs // 2),)),
        ],
        compiler_params=params(), cost_estimate=cost(flops, 2 * width * width),
    )(*fetched)
    received = swap_faces((f0, f1, f2, f3))
    weight, rhs_r, curv, scaled_r = pl.pallas_call(
        early_kernel,
        out_shape=(
            jax.ShapeDtypeStruct((8, width), F32),
            jax.ShapeDtypeStruct((prim, rhs), F32),
            jax.ShapeDtypeStruct((8, BLK), F32),
            jax.ShapeDtypeStruct((rhs, width), BF16),
        ),
        in_specs=[vmem] * 6, out_specs=(vmem,) * 4, compiler_params=params(),
        cost_estimate=cost(1000 * flops, 8 * rhs * width),
    )(perm, conduct, direction, image, resid, basis_t)
    if near:
        return near_rest(perm, rz_row, neumann, image, received, weight, rhs_r, curv, scaled_r, direction, resid,
                         basis_t, coarse, rows)
    send = send[0]
    for k in range(rounds - 1):
        got = swap_bit(send, k)
        last = k + 2 == rounds
        coarse, *send = pl.pallas_call(
            functools.partial(merge_kernel, k, last),
            out_shape=(coarse_type,) if last else (coarse_type, send_type),
            in_specs=[vmem] * 2, out_specs=(vmem,) if last else (vmem,) * 2,
            compiler_params=params(), cost_estimate=cost(1 << 10, 1 << 16),
        )(coarse, got)
        send = send[0] if send else None
    blocks, send = pl.pallas_call(
        functools.partial(spread_kernel, rounds - 1),
        out_shape=(blocks_type, jax.ShapeDtypeStruct((slabs // 2,) + blocks_type.shape[1:], BF16)),
        in_specs=[vmem], out_specs=(vmem,) * 2,
        compiler_params=params(), cost_estimate=cost(1 << 20, 1 << 16),
    )(coarse.reshape(slabs * prim, sectors * prim))
    wide = pl.pallas_call(
        functools.partial(join_kernel, rounds - 1, rows, prim),
        out_shape=jax.ShapeDtypeStruct((block_rows, slabs * blocks_type.shape[2]), BF16),
        in_specs=[vmem] * 2, out_specs=vmem,
        scratch_shapes=[pltpu.VMEM(blocks_type.shape, BF16)],
        compiler_params=params(), cost_estimate=cost(1 << 10, 1 << 16),
    )(blocks, swap_bit(send, rounds - 1))
    assembled, scaled_q, rhs_q, packed = pl.pallas_call(
        functools.partial(coarse_rhs_kernel, rows, sectors),
        out_shape=(
            full,
            jax.ShapeDtypeStruct((rhs, width), BF16),
            jax.ShapeDtypeStruct((prim, rhs), F32),
            jax.ShapeDtypeStruct((slabs * sectors * rows, BLK), BF16),
        ),
        in_specs=[vmem] + [vmem] * 9, out_specs=(vmem,) * 4, compiler_params=params(),
        cost_estimate=cost(2 * rhs * width * prim, 8 * rhs * width),
    )(perm, image, *received, weight, basis_t, rhs_r, curv)
    packed = packed.reshape(slabs * sectors, rows // 2, 2, BLK)
    gathered = lax.all_to_all(packed, ("gx", "col"), 0, 0).reshape(slabs * sectors * rows, BLK)
    sol_r, sol_q, sums = pl.pallas_call(
        neumann_kernel,
        out_shape=(full, full, jax.ShapeDtypeStruct((8, BLK), F32)),
        in_specs=[vmem] * 5 + [hbm], out_specs=(vmem,) * 3,
        scratch_shapes=[pltpu.VMEM((width, width), BF16), pltpu.SemaphoreType.DMA((CHUNKS,))],
        compiler_params=params(), cost_estimate=cost(1000 * flops, 2 * width * width),
    )(scaled_r, scaled_q, resid, assembled, weight, pltpu.with_memory_space_constraint(neumann, pltpu.HBM))
    step, weighted, partial, *faces = pl.pallas_call(
        solve_kernel,
        out_shape=(
            jax.ShapeDtypeStruct((rhs, BLK), F32),
            full,
            jax.ShapeDtypeStruct((slabs * sectors, 1, BLK), F32),
        )
        + (face,) * 4,
        in_specs=[vmem] * 11, out_specs=(vmem, vmem, anywhere) + (vmem,) * 4,
        scratch_shapes=[pltpu.VMEM((slabs * sectors, 1, BLK), F32), pltpu.SemaphoreType.DMA],
        compiler_params=params(), cost_estimate=cost(2 * rhs * width * prim, 8 * rhs * width),
    )(perm, gathered, wide, rz_row, weight, basis_t, sol_r, sol_q, sums, rhs_r, rhs_q)
    partials = lax.all_to_all(partial, ("gx", "col"), 0, 0)
    received = swap_faces(faces)
    resid_new = pl.pallas_call(
        resid_kernel, out_shape=full, in_specs=[vmem] * 3, out_specs=vmem,
        compiler_params=params(), cost_estimate=cost(2 * rhs * width, 12 * rhs * width),
    )(step, resid, assembled)
    direction_new, rz_next = pl.pallas_call(
        direction_kernel, out_shape=(full, jax.ShapeDtypeStruct((1, rhs), F32)),
        in_specs=[vmem] + [vmem] * 8, out_specs=(vmem,) * 2, compiler_params=params(),
        cost_estimate=cost(2 * rhs * width, 8 * rhs * width),
    )(perm, partials, rz_row, direction, weighted, *received)
    return (resid_new[None, None], direction_new[None, None], rz_next[0])


def solution(mesh):
    placed = (
        P("gx", "col", None, None),
        P("gx", "col", None, None),
        P(),
        P("gx", "col", None, None),
        P("gx", "col", None, None),
        P("gx", "col", None, None),
        P("col", None, None, "gx", None, None),
        P(),
        P("gx", "col", None),
    )
    return jax.shard_map(
        body,
        mesh=mesh,
        in_specs=placed,
        out_specs=(P("gx", "col", None, None), P("gx", "col", None, None), P()),
        check_vma=False,
    )
```

```python
import functools

import jax
import jax.numpy as jnp
from jax import lax
from jax.experimental import pallas as pl
from jax.experimental.pallas import tpu as pltpu
from jax.sharding import PartitionSpec as P

F32 = jnp.float32
BF16 = jnp.bfloat16
BLK = 128
EXACT = lax.Precision.HIGHEST
VMEM = pltpu.VMEM


def params(limit=16 * 1024 * 1024):
    return pltpu.CompilerParams(vmem_limit_bytes=limit)


def cost(flops, nbytes):
    return pl.CostEstimate(flops=flops, bytes_accessed=nbytes, transcendentals=0)


def swap(value, axis, offset):
    count = lax.axis_size(axis)
    pairs = []
    for low in range(offset, count, 2):
        high = (low + 1) % count
        pairs += [(low, high), (high, low)]
    return lax.ppermute(value, axis, pairs)


def swap_second(value):
    slabs, sectors = lax.axis_size("gx"), lax.axis_size("col")
    pairs = []
    for slab in range(slabs):
        for sector in range(sectors):
            other = (slab + 1 if slab % 2 else slab - 1, sector)
            if not 0 <= other[0] < slabs:
                other = (slab, sector ^ 1)
            pairs.append((slab * sectors + sector, other[0] * sectors + other[1]))
    return lax.ppermute(value, ("gx", "col"), pairs)


def swap_faces(faces):
    return (
        swap(faces[0], "col", 1),
        swap(faces[1], "col", 0),
        swap_second(faces[2]),
        swap(faces[3], "gx", 0),
    )


def swap_counts():
    slab = lax.axis_index("gx")
    inside = jnp.logical_and(slab > 0, slab < lax.axis_size("gx") - 1)
    return (None, None, inside, None)


def slot_place(perm_ref, slot):
    return jnp.broadcast_to(perm_ref[0:1, slot : slot + 1], (1, BLK))


def swapped_places(perm_ref):
    slab = lax.axis_index("gx") % 2
    sector = lax.axis_index("col") % 2
    places = []
    for parity, even, odd in ((sector, 2, 3), (sector, 3, 2), (slab, 0, 1), (slab, 1, 0)):
        for j in range(2):
            at_even, at_odd = (slot_place(perm_ref, 2 * face + j) for face in (even, odd))
            places.append(jnp.where(parity == 0, at_even, at_odd))
    return places


def put_faces(perm_ref, source, outs):
    blocks = [source[:, b * BLK : (b + 1) * BLK] for b in range(source.shape[1] // BLK)]
    for i, place in enumerate(swapped_places(perm_ref)):
        chosen = blocks[0]
        for b in range(1, len(blocks)):
            chosen = jnp.where(place == b, blocks[b], chosen)
        j = i % 2
        outs[i // 2][0 : chosen.shape[0], j * BLK : (j + 1) * BLK] = chosen.astype(BF16)


def received_blocks(perm_ref, received, blocks):
    places = swapped_places(perm_ref)
    parts = []
    for i in range(len(places)):
        j = i % 2
        part = received[i // 2][:, j * BLK : (j + 1) * BLK].astype(F32)
        counts = swap_counts()[i // 2]
        parts.append(part if counts is None else jnp.where(counts, part, 0.0))
    for b in range(blocks):
        chosen = parts[0]
        for place, part in zip(places[1:], parts[1:]):
            chosen = jnp.where(place == b, part, chosen)
        yield slice(b * BLK, (b + 1) * BLK), chosen


def to_column(row):
    n = row.shape[1]
    at = lax.broadcasted_iota(jnp.int32, (n, n), 0) == lax.broadcasted_iota(jnp.int32, (n, n), 1)
    return jnp.sum(jnp.where(at, row, 0.0), axis=1, keepdims=True)


def to_row(column):
    n = column.shape[0]
    at = lax.broadcasted_iota(jnp.int32, (n, n), 0) == lax.broadcasted_iota(jnp.int32, (n, n), 1)
    return jnp.sum(jnp.where(at, column, 0.0), axis=0, keepdims=True)


CHUNKS = 4


def other_block(i, k):
    mine = (lax.axis_index("gx") >> k) % 2
    return ((i >> k) << (k + 1)) + (i & ((1 << k) - 1)) + ((1 - mine) << k)


def swap_bit(value, k):
    count = lax.axis_size("gx")
    return lax.ppermute(value, "gx", [(i, i ^ (1 << k)) for i in range(count)])


def image_kernel(perm_hbm, dir_hbm, schur_hbm, resid_hbm, basis_hbm, coarse_hbm,
                 image_ref, f0, f1, f2, f3, dir_ref, resid_ref, basis_ref, coarse_ref, *rest):
    *send_ref, perm_ref, schur_ref, sems = rest
    rows = schur_ref.shape[0] // CHUNKS
    parts = [pl.ds(i * rows, rows) for i in range(CHUNKS)]
    pairs = [(dir_hbm, dir_ref), (perm_hbm, perm_ref)]
    pairs += [(schur_hbm.at[part], schur_ref.at[part]) for part in parts]
    for ref in send_ref:
        pairs += [(coarse_hbm.at[other_block(i, 0)], ref.at[i]) for i in range(ref.shape[0])]
    pairs += [(resid_hbm, resid_ref), (basis_hbm, basis_ref), (coarse_hbm, coarse_ref)]
    copies = [pltpu.make_async_copy(source, target, sems.at[i]) for i, (source, target) in enumerate(pairs)]
    for copy in copies:
        copy.start()
    copies[0].wait()
    total = None
    for i, part in enumerate(parts):
        copies[2 + i].wait()
        term = jnp.dot(dir_ref[:, part].astype(BF16), schur_ref[part], preferred_element_type=F32)
        total = term if total is None else total + term
    image_ref[...] = total
    copies[1].wait()
    put_faces(perm_ref, total, (f0, f1, f2, f3))
    for copy in copies[2 + CHUNKS :]:
        copy.wait()


def merge_kernel(k, last, blocks_ref, got_ref, out_ref, *send_ref):
    out_ref[...] = blocks_ref[...]
    for i in range(got_ref.shape[0]):
        out_ref[other_block(i, k)] = got_ref[i]
    if not last:
        for i in range(got_ref.shape[0]):
            send_ref[0][i] = out_ref[other_block(i, k + 1)]


def join_kernel(k, depth, prim, blocks_ref, got_ref, wide_ref, all_ref):
    all_ref[...] = blocks_ref[...]
    for i in range(got_ref.shape[0]):
        all_ref[other_block(i, k)] = got_ref[i]
    slabs, rows, width = blocks_ref.shape
    width = width // 2
    for half in range(2):
        for h in range(slabs):
            at = (half * slabs + h) * width
            wide_ref[:, at : at + width] = all_ref[h, :, half * width : (half + 1) * width]
    row = lax.broadcasted_iota(jnp.int32, wide_ref.shape, 0)
    lane = lax.broadcasted_iota(jnp.int32, wide_ref.shape, 1)
    picked = jnp.logical_and(lane < slabs * width, lane % depth == prim // 2)
    wide = jnp.where(row == prim, jnp.where(picked, 1.0, 0.0), wide_ref[...].astype(F32))
    wide_ref[...] = wide.astype(BF16)


def spread_kernel(k, matrix_ref, blocks_ref, send_ref):
    slabs, rows, _ = blocks_ref.shape
    prim = matrix_ref.shape[0] // slabs
    half = prim // 2
    sectors = matrix_ref.shape[1] // prim
    width = blocks_ref.shape[2] // 2
    depth = width // sectors
    source = lax.broadcasted_iota(jnp.int32, (sectors * prim, 2 * width), 0)
    place = lax.broadcasted_iota(jnp.int32, (sectors * prim, 2 * width), 1)
    later = place // width
    within = place % width
    sector, at = within // depth, within % depth
    chosen = jnp.logical_and(at < half, source == sector * prim + later * half + at)
    spread = jnp.dot(matrix_ref[...], jnp.where(chosen, 1.0, 0.0).astype(BF16), preferred_element_type=F32)
    empty = jnp.zeros((rows - prim, 2 * width), F32)
    for g in range(slabs):
        own = jnp.concatenate([spread[g * prim : (g + 1) * prim], empty], axis=0)
        blocks_ref[g] = own.astype(BF16)
    for i in range(send_ref.shape[0]):
        send_ref[i] = blocks_ref[other_block(i, k)]


def conduct_at(row, sector):
    lane = lax.broadcasted_iota(jnp.int32, row.shape, 1)
    return jnp.sum(jnp.where(lane == sector, row, 0.0), axis=1, keepdims=True)


def early_kernel(perm_ref, conduct_ref, dir_ref, image_ref, resid_ref, basis_ref,
                 weight_ref, rhs_ref, curv_ref, scaled_ref):
    slab, sector = lax.axis_index("gx"), lax.axis_index("col")
    slabs, sectors = lax.axis_size("gx"), lax.axis_size("col")
    row = conduct_ref[pl.ds(slab, 1), :]
    own = conduct_at(row, sector)
    below = conduct_at(conduct_ref[pl.ds(jnp.maximum(slab - 1, 0), 1), :], sector)
    above = conduct_at(conduct_ref[pl.ds(jnp.minimum(slab + 1, slabs - 1), 1), :], sector)
    below = jnp.where(slab > 0, below, 0.0)
    above = jnp.where(slab < slabs - 1, above, 0.0)
    left = conduct_at(row, (sector + sectors - 1) % sectors)
    right = conduct_at(row, (sector + 1) % sectors)
    across = [jnp.broadcast_to(own / (own + other), (1, BLK)) for other in (below, above, left, right)]
    places = [slot_place(perm_ref, slot) for slot in range(8)]
    for b in range(weight_ref.shape[1] // BLK):
        weight = across[0]
        for slot in range(2, 8):
            weight = jnp.where(places[slot] == b, across[slot // 2], weight)
        weight_ref[:, b * BLK : (b + 1) * BLK] = jnp.broadcast_to(weight, (8, BLK))
    scaled = (weight_ref[0:1, :] * resid_ref[...]).astype(BF16)
    scaled_ref[...] = scaled
    rhs_ref[...] = lax.dot_general(
        basis_ref[...], scaled, (((1,), (1,)), ((), ())), preferred_element_type=F32
    )
    curv = to_row(jnp.sum(dir_ref[...] * image_ref[...], axis=1, keepdims=True))
    high = curv.astype(BF16).astype(F32)
    n = curv.shape[1]
    curv_ref[...] = jnp.zeros_like(curv_ref)
    curv_ref[0:1, 0:n] = high
    curv_ref[0:1, n : 2 * n] = curv - high


def coarse_rhs_kernel(rows, sectors, perm_ref, image_ref, r0, r1, r2, r3, weight_ref, basis_ref, rhs_ref, curv_ref,
                      assembled_ref, scaled_ref, rhs_q_ref, out_ref):
    for at, part in received_blocks(perm_ref, (r0, r1, r2, r3), image_ref.shape[1] // BLK):
        assembled_ref[:, at] = image_ref[:, at] + part
    scaled = (weight_ref[0:1, :] * assembled_ref[...]).astype(BF16)
    scaled_ref[...] = scaled
    rhs_q = lax.dot_general(
        basis_ref[...], scaled, (((1,), (1,)), ((), ())), preferred_element_type=F32
    )
    rhs_q_ref[...] = rhs_q
    rhs_r = rhs_ref[...]
    half = rhs_r.shape[0] // 2
    packed = jnp.concatenate([rhs_r[:half], rhs_q[:half], rhs_r[half:], rhs_q[half:]], axis=1)
    packed = jnp.concatenate(
        [packed, curv_ref[0:1, :], jnp.zeros((rows - half - 1, BLK), F32)], axis=0
    )
    several = jnp.concatenate([packed] * sectors, axis=0).astype(BF16)
    step = several.shape[0]
    for i in range(out_ref.shape[0] // step):
        out_ref[i * step : (i + 1) * step] = several


def neumann_kernel(scaled_r_ref, scaled_q_ref, resid_ref, assembled_ref, weight_ref, neumann_hbm,
                   sol_r_ref, sol_q_ref, sums_ref, neumann_ref, sems):
    rows = neumann_ref.shape[0] // CHUNKS
    parts = [pl.ds(i * rows, rows) for i in range(CHUNKS)]
    copies = [
        pltpu.make_async_copy(neumann_hbm.at[part], neumann_ref.at[part], sems.at[i])
        for i, part in enumerate(parts)
    ]
    for copy in copies:
        copy.start()
    total_r = total_q = None
    for copy, part in zip(copies, parts):
        copy.wait()
        term_r = jnp.dot(scaled_r_ref[:, part], neumann_ref[part], preferred_element_type=F32)
        term_q = jnp.dot(scaled_q_ref[:, part], neumann_ref[part], preferred_element_type=F32)
        total_r = term_r if total_r is None else total_r + term_r
        total_q = term_q if total_q is None else total_q + term_q
    sol_r_ref[...] = total_r
    sol_q_ref[...] = total_q
    weighted_r = weight_ref[0:1, :] * resid_ref[...]
    weighted_q = weight_ref[0:1, :] * assembled_ref[...]
    n = total_r.shape[0]
    sums_ref[...] = jnp.zeros_like(sums_ref)
    for i, product in enumerate(
        (weighted_r * total_r, weighted_r * total_q + weighted_q * total_r, weighted_q * total_q)
    ):
        sums_ref[0:1, i * n : (i + 1) * n] = to_row(jnp.sum(product, axis=1, keepdims=True))


def solve_kernel(perm_ref, gathered_ref, wide_ref, prev_ref, weight_ref, basis_ref, sol_r_ref, sol_q_ref,
                 sums_ref, rhs_r_ref, rhs_q_ref, step_out, weighted_out, rz_out, f0, f1, f2, f3, rz_ref, sem):
    n = prev_ref.shape[1]
    prim = basis_ref.shape[0]
    halves = jnp.concatenate([gathered_ref[:, : 2 * n], gathered_ref[:, 2 * n :]], axis=0)
    total = jnp.dot(wide_ref[...], halves, preferred_element_type=F32)
    step = prev_ref[...] / (total[prim : prim + 1, 0:n] + total[prim : prim + 1, n : 2 * n])
    coarse_sol = (total[0:prim, 0:n] - step * total[0:prim, n : 2 * n]).astype(BF16)
    coarse_part = coarse_sol.astype(F32) * (rhs_r_ref[...] - step * rhs_q_ref[...])
    partial = (
        sums_ref[0:1, 0:n]
        - step * (sums_ref[0:1, n : 2 * n] - step * sums_ref[0:1, 2 * n : 3 * n])
        + jnp.sum(coarse_part, axis=0, keepdims=True)
    )
    partial = jnp.concatenate([partial, jnp.zeros((1, BLK - n), F32)], axis=1)
    for i in range(rz_ref.shape[0]):
        rz_ref[i] = partial
    copy = pltpu.make_async_copy(rz_ref, rz_out, sem)
    copy.start()
    correction = lax.dot_general(
        coarse_sol, basis_ref[...], (((0,), (0,)), ((), ())), preferred_element_type=F32
    )
    step_col = to_column(step)
    step_out[...] = jnp.broadcast_to(step_col, step_out.shape)
    weighted = weight_ref[0:1, :] * (sol_r_ref[...] - step_col * sol_q_ref[...] + correction)
    weighted_out[...] = weighted
    put_faces(perm_ref, weighted, (f0, f1, f2, f3))
    copy.wait()


def resid_kernel(step_ref, resid_ref, assembled_ref, out_ref):
    out_ref[...] = resid_ref[...] - step_ref[:, 0:1] * assembled_ref[...]


def direction_kernel(perm_ref, partials_ref, rz_ref, dir_ref, weighted_ref, r0, r1, r2, r3,
                     out_ref, rz_out):
    n = rz_ref.shape[1]
    rz_next = jnp.sum(partials_ref[...], axis=0)[:, 0:n]
    rz_out[...] = rz_next
    factor = to_column(rz_next / rz_ref[...])
    for at, part in received_blocks(perm_ref, (r0, r1, r2, r3), dir_ref.shape[1] // BLK):
        out_ref[:, at] = weighted_ref[:, at] + factor * dir_ref[:, at] + part


def split(value):
    high = value.astype(BF16).astype(F32)
    return high, value - high


def spread_pair_kernel(after_ref, own_ref, mate_ref, out_ref):
    slabs = lax.axis_size("gx")
    prim = own_ref.shape[0] // slabs
    half = prim // 2
    sectors = own_ref.shape[1] // prim
    width = out_ref.shape[2] // 2
    depth = width // sectors
    source = lax.broadcasted_iota(jnp.int32, (sectors * prim, 2 * width), 0)
    place = lax.broadcasted_iota(jnp.int32, (sectors * prim, 2 * width), 1)
    later = place // width
    within = place % width
    sector, at = within // depth, within % depth
    chosen = jnp.logical_and(at < half, source == sector * prim + later * half + at)
    chosen = jnp.where(chosen, 1.0, 0.0).astype(BF16)
    mine = lax.axis_index("gx") % 2
    for ref, bit in ((own_ref, mine), (mate_ref, 1 - mine)):
        out_ref[bit] = jnp.dot(ref[...], chosen, preferred_element_type=F32).astype(BF16)


def gather_kernel(k, after_ref, mine_ref, got_ref, out_ref, both_ref):
    bit = (lax.axis_index("gx") >> k) % 2
    n = mine_ref.shape[0]
    for i in range(n):
        both_ref[bit * n + i] = mine_ref[i]
        both_ref[(1 - bit) * n + i] = got_ref[i]
    out_ref[...] = jnp.concatenate([both_ref[i] for i in range(2 * n)], axis=1)


def near_rhs_kernel(rows, sectors, perm_ref, image_ref, r0, r1, r2, r3, weight_ref, basis_ref, rhs_ref, curv_ref,
                    scaled_ref, resid_ref, neumann_ref, assembled_ref, sol_r_ref, sol_q_ref, out_ref):
    for at, part in received_blocks(perm_ref, (r0, r1, r2, r3), image_ref.shape[1] // BLK):
        assembled_ref[:, at] = image_ref[:, at] + part
    weighted_r = weight_ref[0:1, :] * resid_ref[...]
    weighted_q = weight_ref[0:1, :] * assembled_ref[...]
    scaled = weighted_q.astype(BF16)
    n = scaled.shape[0]
    both = jnp.concatenate([scaled_ref[...], scaled], axis=0)
    sol = jnp.dot(both, neumann_ref[...], preferred_element_type=F32)
    rhs_q = lax.dot_general(
        basis_ref[...], scaled, (((1,), (1,)), ((), ())), preferred_element_type=F32
    )
    sol_r, sol_q = sol[:n], sol[n:]
    sol_r_ref[...] = sol_r
    sol_q_ref[...] = sol_q
    products = (weighted_r * sol_r, weighted_r * sol_q + weighted_q * sol_r, weighted_q * sol_q)
    sums = [to_row(jnp.sum(product, axis=1, keepdims=True)) for product in products]
    first = jnp.concatenate([curv_ref[0:1, : 2 * n], *split(sums[0])], axis=1)
    second = jnp.concatenate([*split(sums[1]), *split(sums[2])], axis=1)
    rhs_r = rhs_ref[...]
    half = rhs_r.shape[0] // 2
    packed = jnp.concatenate([rhs_r[:half], rhs_q[:half], rhs_r[half:], rhs_q[half:]], axis=1)
    packed = jnp.concatenate([packed, first, second], axis=0)
    several = jnp.concatenate([packed] * sectors, axis=0).astype(BF16)
    step = several.shape[0]
    for i in range(out_ref.shape[0] // step):
        out_ref[i * step : (i + 1) * step] = several


def frame_kernel(depth, weight_ref, r_ref, q_ref, basis_ref, r_out, q_out, picks_ref, basis_out):
    r_out[...] = weight_ref[0:1, :] * r_ref[...]
    q_out[...] = weight_ref[0:1, :] * q_ref[...]
    prim = basis_ref.shape[0]
    half = prim // 2
    rows = basis_out.shape[0]
    slabs, sectors = lax.axis_size("gx"), lax.axis_size("col")
    width = sectors * depth
    row = lax.broadcasted_iota(jnp.int32, picks_ref.shape, 0)
    lane = lax.broadcasted_iota(jnp.int32, picks_ref.shape, 1)
    part = lane // width % 2
    at = lane % depth
    sums = jnp.logical_and(at >= half, row == (at - half) * 2 + part)
    mine = jnp.logical_and(lane % width // depth == lax.axis_index("col"), at < half)
    own = jnp.logical_and(mine, row == 16 + lane // (2 * width) * prim + part * half + at)
    picks_ref[...] = jnp.where(jnp.logical_or(sums, own), 1.0, 0.0).astype(BF16)
    row = lax.broadcasted_iota(jnp.int32, (rows, prim), 0)
    lane = lax.broadcasted_iota(jnp.int32, (rows, prim), 1)
    here = jnp.where(row == lax.axis_index("gx") * prim + lane, 1.0, 0.0).astype(BF16)
    basis_out[...] = jnp.dot(here, basis_ref[...], preferred_element_type=F32).astype(BF16)


def near_solve_kernel(perm_ref, gathered_ref, mine_ref, got_ref, picks_ref, prev_ref, weight_ref, basis_ref,
                      sol_r_ref, sol_q_ref, step_out, weighted_out, base_out, part_out, f0, f1, f2, f3, rhs_ref):
    n = prev_ref.shape[1]
    slabs = lax.axis_size("gx")
    width = gathered_ref.shape[0] // slabs
    for h in range(slabs):
        part = gathered_ref[h * width : (h + 1) * width]
        rhs_ref[2 * h * width : (2 * h + 1) * width] = part[:, : 2 * n]
        rhs_ref[(2 * h + 1) * width : (2 * h + 2) * width] = part[:, 2 * n :]
    count = slabs * width
    top = (lax.axis_index("gx") * 2) // slabs
    mine = rhs_ref[pl.ds(pl.multiple_of(top * count, 16), count), :]
    got = rhs_ref[pl.ds(pl.multiple_of((1 - top) * count, 16), count), :]
    picked = jnp.dot(picks_ref[...], rhs_ref[...], preferred_element_type=F32)
    total = jnp.dot(mine_ref[...], mine, preferred_element_type=F32) + jnp.dot(
        got_ref[...], got, preferred_element_type=F32
    )
    curvature, first, second, third = (picked[i : i + 1, 0:n] + picked[i : i + 1, n : 2 * n] for i in range(4))
    step = prev_ref[...] / curvature
    sol = (total[:, 0:n] - step * total[:, n : 2 * n]).astype(BF16)
    rhs = picked[16:, 0:n] - step * picked[16:, n : 2 * n]
    high, low = split(jnp.sum(sol.astype(F32) * rhs, axis=0, keepdims=True))
    correction = lax.dot_general(
        sol, basis_ref[...], (((0,), (0,)), ((), ())), preferred_element_type=F32
    )
    step_col = to_column(step)
    step_out[...] = jnp.broadcast_to(step_col, step_out.shape)
    weighted = sol_r_ref[...] - step_col * sol_q_ref[...] + weight_ref[0:1, :] * correction
    weighted_out[...] = weighted
    blank = jnp.zeros((1, BLK - n), F32)
    low = low.astype(BF16).astype(F32)
    base = first - step * (second - step * third)
    base_out[...] = jnp.broadcast_to(jnp.concatenate([base, blank], axis=1), base_out.shape)
    part_out[...] = jnp.broadcast_to(jnp.concatenate([high + low, blank], axis=1), part_out.shape)
    put_faces(perm_ref, weighted, (f0, f1, f2, f3))
    lines = jnp.concatenate([high, low, jnp.zeros((14, n), F32)], axis=0)
    lines = jnp.concatenate([lines, jnp.zeros((16, 2 * BLK - n), F32)], axis=1).astype(BF16)
    f0[n:, :] = lines
    f1[n:, :] = lines


def near_direction_kernel(perm_ref, rz_ref, dir_ref, weighted_ref, base_ref, part_ref, far_ref, r0, r1, r2, r3,
                          out_ref, rz_out):
    n = rz_ref.shape[1]
    sector = lax.axis_index("col")
    beside = jnp.where(sector % 2 == 1, (sector + 1) % 4, (sector + 3) % 4)
    parts = [(sector, part_ref[0:1, 0:n]), (sector ^ 2, far_ref[0:1, 0:n])]
    for ref, other in ((r0, beside), (r1, sector ^ 1)):
        lines = ref[n : n + 16, 0:n].astype(F32)
        parts.append((other, lines[0:1] + lines[1:2]))
    rz_next = base_ref[0:1, 0:n]
    for at in range(4):
        value = parts[0][1]
        for other, part in parts[1:]:
            value = jnp.where(other == at, part, value)
        rz_next = rz_next + value
    rz_out[...] = rz_next
    factor = to_column(rz_next / rz_ref[...])
    received = (r0[0:n, :], r1[0:n, :], r2[...], r3[...])
    for at, part in received_blocks(perm_ref, received, dir_ref.shape[1] // BLK):
        out_ref[:, at] = weighted_ref[:, at] + factor * dir_ref[:, at] + part


def near_rest(perm, rz_row, neumann, image, received, weight, rhs_r, curv, scaled_r, direction, resid, basis_t,
              coarse, rows):
    rhs, width = resid.shape
    prim = basis_t.shape[0]
    slabs, sectors = lax.axis_size("gx"), lax.axis_size("col")
    vmem = pl.BlockSpec(memory_space=VMEM)
    full = jax.ShapeDtypeStruct((rhs, width), F32)
    line = jax.ShapeDtypeStruct((8, BLK), F32)
    small = cost(1 << 10, 1 << 16)

    def call(kernel, outs, *args, scratch=(), estimate=small, after=()):
        return pl.pallas_call(
            kernel, out_shape=outs, in_specs=[pl.BlockSpec(memory_space=pl.ANY)] * len(after) + [vmem] * len(args),
            out_specs=(vmem,) * len(outs), scratch_shapes=scratch, compiler_params=params(), cost_estimate=estimate,
        )(*after, *args)

    mate = swap_bit(coarse, 0)
    flat = (slabs * prim, sectors * prim)
    shard = (slabs * prim, 2 * sectors * rows)
    (blocks,) = call(
        spread_pair_kernel, (jax.ShapeDtypeStruct((2,) + shard, BF16),),
        coarse.reshape(flat), mate.reshape(flat), after=(perm,),
    )
    assembled, sol_r, sol_q, packed = call(
        functools.partial(near_rhs_kernel, rows, sectors),
        (full, full, full, jax.ShapeDtypeStruct((slabs * sectors * rows, BLK), BF16)),
        perm, image, *received, weight, basis_t, rhs_r, curv, scaled_r, resid, neumann,
        estimate=cost(2000 * rhs * width * width, 1 << 16),
    )
    (blocks,) = call(
        functools.partial(gather_kernel, 1), (jax.ShapeDtypeStruct((shard[0], 4 * shard[1]), BF16),),
        blocks, swap_bit(blocks, 1), after=(packed,), scratch=[pltpu.VMEM((4,) + shard, BF16)],
        estimate=cost(2000 * rhs * width * width, 1 << 16),
    )
    got = swap_bit(blocks, 2)
    packed = packed.reshape(slabs * sectors, rows // 2, 2, BLK)
    gathered = lax.all_to_all(packed, ("gx", "col"), 0, 0).reshape(slabs * sectors * rows, BLK)
    sol_r, sol_q, picks, placed = call(
        functools.partial(frame_kernel, rows),
        (
            full,
            full,
            jax.ShapeDtypeStruct((16 + slabs * prim, slabs * shard[1]), BF16),
            jax.ShapeDtypeStruct((slabs * prim, width), BF16),
        ),
        weight, sol_r, sol_q, basis_t,
    )
    face = jax.ShapeDtypeStruct((rhs, 2 * BLK), BF16)
    tall = jax.ShapeDtypeStruct((rhs + 16, 2 * BLK), BF16)
    step, weighted, base, part, *faces = call(
        near_solve_kernel,
        (jax.ShapeDtypeStruct((rhs, BLK), F32), full, line, jax.ShapeDtypeStruct((64, BLK), F32), tall, tall, face, face),
        perm, gathered, blocks, got, picks, rz_row, weight, placed, sol_r, sol_q,
        scratch=[pltpu.VMEM((slabs * shard[1], 2 * rhs), BF16)],
    )
    far = lax.ppermute(part, "col", [(i, i ^ 2) for i in range(sectors)])
    received = swap_faces(faces)
    (resid_new,) = call(resid_kernel, (full,), step, resid, assembled)
    direction_new, rz_next = call(
        near_direction_kernel, (full, jax.ShapeDtypeStruct((1, rhs), F32)),
        perm, rz_row, direction, weighted, base, part, far, *received,
    )
    return (resid_new[None, None], direction_new[None, None], rz_next[0])


def body(resid, direction, rz_prev, schur, neumann, basis, coarse_inv, conduct, face_perm):
    resid, direction, schur, neumann = resid[0, 0], direction[0, 0], schur[0, 0], neumann[0, 0]
    basis_t = basis[0, 0].T
    perm = face_perm[0]
    rhs, width = resid.shape
    prim = basis_t.shape[0]
    slabs, sectors = lax.axis_size("gx"), lax.axis_size("col")
    rows = -(-(prim // 2 + 1) // 4) * 4
    block_rows = -(-(prim + 1) // 16) * 16
    rounds = slabs.bit_length() - 1
    face = jax.ShapeDtypeStruct((rhs, 2 * BLK), BF16)
    full = jax.ShapeDtypeStruct((rhs, width), F32)
    rz_row = rz_prev[None, :]
    vmem = pl.BlockSpec(memory_space=VMEM)
    hbm = pl.BlockSpec(memory_space=pltpu.HBM)
    anywhere = pl.BlockSpec(memory_space=pl.ANY)
    flops = 2 * rhs * width * width
    coarse = coarse_inv[0, :, :, 0]
    coarse_type = jax.ShapeDtypeStruct(coarse.shape, BF16)
    send_type = jax.ShapeDtypeStruct((slabs // 2,) + coarse.shape[1:], BF16)
    blocks_type = jax.ShapeDtypeStruct((slabs, block_rows, 2 * sectors * rows), BF16)

    near = sectors == 4 and slabs == 8
    sends = () if near else (send_type,)
    fetched = [pltpu.with_memory_space_constraint(x, pltpu.HBM) for x in (perm, direction, schur, resid, basis_t, coarse)]
    image, f0, f1, f2, f3, direction, resid, basis_t, coarse, *send = pl.pallas_call(
        image_kernel,
        out_shape=(full,) + (face,) * 4
        + (full, full, jax.ShapeDtypeStruct((prim, width), BF16), coarse_type) + sends,
        in_specs=[hbm] * 6, out_specs=(vmem,) * (9 + len(sends)),
        scratch_shapes=[
            pltpu.VMEM(perm.shape, jnp.int32),
            pltpu.VMEM((width, width), BF16),
            pltpu.SemaphoreType.DMA((CHUNKS + 5 + len(sends) * (slabs // 2),)),
        ],
        compiler_params=params(), cost_estimate=cost(flops, 2 * width * width),
    )(*fetched)
    received = swap_faces((f0, f1, f2, f3))
    weight, rhs_r, curv, scaled_r = pl.pallas_call(
        early_kernel,
        out_shape=(
            jax.ShapeDtypeStruct((8, width), F32),
            jax.ShapeDtypeStruct((prim, rhs), F32),
            jax.ShapeDtypeStruct((8, BLK), F32),
            jax.ShapeDtypeStruct((rhs, width), BF16),
        ),
        in_specs=[vmem] * 6, out_specs=(vmem,) * 4, compiler_params=params(),
        cost_estimate=cost(1000 * flops, 8 * rhs * width),
    )(perm, conduct, direction, image, resid, basis_t)
    if near:
        return near_rest(perm, rz_row, neumann, image, received, weight, rhs_r, curv, scaled_r, direction, resid,
                         basis_t, coarse, rows)
    send = send[0]
    for k in range(rounds - 1):
        got = swap_bit(send, k)
        last = k + 2 == rounds
        coarse, *send = pl.pallas_call(
            functools.partial(merge_kernel, k, last),
            out_shape=(coarse_type,) if last else (coarse_type, send_type),
            in_specs=[vmem] * 2, out_specs=(vmem,) if last else (vmem,) * 2,
            compiler_params=params(), cost_estimate=cost(1 << 10, 1 << 16),
        )(coarse, got)
        send = send[0] if send else None
    blocks, send = pl.pallas_call(
        functools.partial(spread_kernel, rounds - 1),
        out_shape=(blocks_type, jax.ShapeDtypeStruct((slabs // 2,) + blocks_type.shape[1:], BF16)),
        in_specs=[vmem], out_specs=(vmem,) * 2,
        compiler_params=params(), cost_estimate=cost(1 << 20, 1 << 16),
    )(coarse.reshape(slabs * prim, sectors * prim))
    wide = pl.pallas_call(
        functools.partial(join_kernel, rounds - 1, rows, prim),
        out_shape=jax.ShapeDtypeStruct((block_rows, slabs * blocks_type.shape[2]), BF16),
        in_specs=[vmem] * 2, out_specs=vmem,
        scratch_shapes=[pltpu.VMEM(blocks_type.shape, BF16)],
        compiler_params=params(), cost_estimate=cost(1 << 10, 1 << 16),
    )(blocks, swap_bit(send, rounds - 1))
    assembled, scaled_q, rhs_q, packed = pl.pallas_call(
        functools.partial(coarse_rhs_kernel, rows, sectors),
        out_shape=(
            full,
            jax.ShapeDtypeStruct((rhs, width), BF16),
            jax.ShapeDtypeStruct((prim, rhs), F32),
            jax.ShapeDtypeStruct((slabs * sectors * rows, BLK), BF16),
        ),
        in_specs=[vmem] + [vmem] * 9, out_specs=(vmem,) * 4, compiler_params=params(),
        cost_estimate=cost(2 * rhs * width * prim, 8 * rhs * width),
    )(perm, image, *received, weight, basis_t, rhs_r, curv)
    packed = packed.reshape(slabs * sectors, rows // 2, 2, BLK)
    gathered = lax.all_to_all(packed, ("gx", "col"), 0, 0).reshape(slabs * sectors * rows, BLK)
    sol_r, sol_q, sums = pl.pallas_call(
        neumann_kernel,
        out_shape=(full, full, jax.ShapeDtypeStruct((8, BLK), F32)),
        in_specs=[vmem] * 5 + [hbm], out_specs=(vmem,) * 3,
        scratch_shapes=[pltpu.VMEM((width, width), BF16), pltpu.SemaphoreType.DMA((CHUNKS,))],
        compiler_params=params(), cost_estimate=cost(1000 * flops, 2 * width * width),
    )(scaled_r, scaled_q, resid, assembled, weight, pltpu.with_memory_space_constraint(neumann, pltpu.HBM))
    step, weighted, partial, *faces = pl.pallas_call(
        solve_kernel,
        out_shape=(
            jax.ShapeDtypeStruct((rhs, BLK), F32),
            full,
            jax.ShapeDtypeStruct((slabs * sectors, 1, BLK), F32),
        )
        + (face,) * 4,
        in_specs=[vmem] * 11, out_specs=(vmem, vmem, anywhere) + (vmem,) * 4,
        scratch_shapes=[pltpu.VMEM((slabs * sectors, 1, BLK), F32), pltpu.SemaphoreType.DMA],
        compiler_params=params(), cost_estimate=cost(2 * rhs * width * prim, 8 * rhs * width),
    )(perm, gathered, wide, rz_row, weight, basis_t, sol_r, sol_q, sums, rhs_r, rhs_q)
    partials = lax.all_to_all(partial, ("gx", "col"), 0, 0)
    received = swap_faces(faces)
    resid_new = pl.pallas_call(
        resid_kernel, out_shape=full, in_specs=[vmem] * 3, out_specs=vmem,
        compiler_params=params(), cost_estimate=cost(2 * rhs * width, 12 * rhs * width),
    )(step, resid, assembled)
    direction_new, rz_next = pl.pallas_call(
        direction_kernel, out_shape=(full, jax.ShapeDtypeStruct((1, rhs), F32)),
        in_specs=[vmem] + [vmem] * 8, out_specs=(vmem,) * 2, compiler_params=params(),
        cost_estimate=cost(2 * rhs * width, 8 * rhs * width),
    )(perm, partials, rz_row, direction, weighted, *received)
    return (resid_new[None, None], direction_new[None, None], rz_next[0])


def solution(mesh):
    placed = (
        P("gx", "col", None, None),
        P("gx", "col", None, None),
        P(),
        P("gx", "col", None, None),
        P("gx", "col", None, None),
        P("gx", "col", None, None),
        P("col", None, None, "gx", None, None),
        P(),
        P("gx", "col", None),
    )
    return jax.shard_map(
        body,
        mesh=mesh,
        in_specs=placed,
        out_specs=(P("gx", "col", None, None), P("gx", "col", None, None), P()),
        check_vma=False,
    )
```

```python
import functools

import jax
import jax.numpy as jnp
from jax import lax
from jax.experimental import pallas as pl
from jax.experimental.pallas import tpu as pltpu
from jax.sharding import PartitionSpec as P

F32 = jnp.float32
BF16 = jnp.bfloat16
BLK = 128
EXACT = lax.Precision.HIGHEST
VMEM = pltpu.VMEM


def params(limit=16 * 1024 * 1024):
    return pltpu.CompilerParams(vmem_limit_bytes=limit)


def cost(flops, nbytes):
    return pl.CostEstimate(flops=flops, bytes_accessed=nbytes, transcendentals=0)


def swap(value, axis, offset):
    count = lax.axis_size(axis)
    pairs = []
    for low in range(offset, count, 2):
        high = (low + 1) % count
        pairs += [(low, high), (high, low)]
    return lax.ppermute(value, axis, pairs)


def swap_second(value):
    slabs, sectors = lax.axis_size("gx"), lax.axis_size("col")
    pairs = []
    for slab in range(slabs):
        for sector in range(sectors):
            other = (slab + 1 if slab % 2 else slab - 1, sector)
            if not 0 <= other[0] < slabs:
                other = (slab, sector ^ 1)
            pairs.append((slab * sectors + sector, other[0] * sectors + other[1]))
    return lax.ppermute(value, ("gx", "col"), pairs)


def swap_faces(faces, first=0):
    swaps = (
        lambda face: swap(face, "col", 1),
        lambda face: swap(face, "col", 0),
        swap_second,
        lambda face: swap(face, "gx", 0),
    )
    return [swaps[first + i](face) for i, face in enumerate(faces)]


def swap_counts():
    slab = lax.axis_index("gx")
    inside = jnp.logical_and(slab > 0, slab < lax.axis_size("gx") - 1)
    return (None, None, inside, None)


def slot_place(perm_ref, slot):
    return jnp.broadcast_to(perm_ref[0:1, slot : slot + 1], (1, BLK))


def swapped_places(perm_ref):
    slab = lax.axis_index("gx") % 2
    sector = lax.axis_index("col") % 2
    places = []
    for parity, even, odd in ((sector, 2, 3), (sector, 3, 2), (slab, 0, 1), (slab, 1, 0)):
        for j in range(2):
            at_even, at_odd = (slot_place(perm_ref, 2 * face + j) for face in (even, odd))
            places.append(jnp.where(parity == 0, at_even, at_odd))
    return places


def put_faces(perm_ref, source, outs, first=0):
    blocks = [source[:, b * BLK : (b + 1) * BLK] for b in range(source.shape[1] // BLK)]
    for i, place in enumerate(swapped_places(perm_ref)[2 * first : 2 * (first + len(outs))]):
        chosen = blocks[0]
        for b in range(1, len(blocks)):
            chosen = jnp.where(place == b, blocks[b], chosen)
        j = i % 2
        outs[i // 2][0 : chosen.shape[0], j * BLK : (j + 1) * BLK] = chosen.astype(BF16)


def received_blocks(perm_ref, received, blocks):
    places = swapped_places(perm_ref)
    parts = []
    for i in range(len(places)):
        j = i % 2
        part = received[i // 2][:, j * BLK : (j + 1) * BLK].astype(F32)
        counts = swap_counts()[i // 2]
        parts.append(part if counts is None else jnp.where(counts, part, 0.0))
    for b in range(blocks):
        chosen = parts[0]
        for place, part in zip(places[1:], parts[1:]):
            chosen = jnp.where(place == b, part, chosen)
        yield slice(b * BLK, (b + 1) * BLK), chosen


def some_received_blocks(perm_ref, received, blocks, first):
    places = swapped_places(perm_ref)[2 * first :]
    parts = []
    for i, got in enumerate(received):
        counts = swap_counts()[first + i]
        for j in range(2):
            part = got[:, j * BLK : (j + 1) * BLK].astype(F32)
            parts.append(part if counts is None else jnp.where(counts, part, 0.0))
    for b in range(blocks):
        chosen = jnp.zeros_like(parts[0])
        for place, part in zip(places, parts):
            chosen = jnp.where(place == b, part, chosen)
        yield slice(b * BLK, (b + 1) * BLK), chosen


def to_column(row):
    n = row.shape[1]
    at = lax.broadcasted_iota(jnp.int32, (n, n), 0) == lax.broadcasted_iota(jnp.int32, (n, n), 1)
    return jnp.sum(jnp.where(at, row, 0.0), axis=1, keepdims=True)


def to_row(column):
    n = column.shape[0]
    at = lax.broadcasted_iota(jnp.int32, (n, n), 0) == lax.broadcasted_iota(jnp.int32, (n, n), 1)
    return jnp.sum(jnp.where(at, column, 0.0), axis=0, keepdims=True)


CHUNKS = 4


def other_block(i, k):
    mine = (lax.axis_index("gx") >> k) % 2
    return ((i >> k) << (k + 1)) + (i & ((1 << k) - 1)) + ((1 - mine) << k)


def swap_bit(value, k):
    count = lax.axis_size("gx")
    return lax.ppermute(value, "gx", [(i, i ^ (1 << k)) for i in range(count)])


def image_kernel(perm_hbm, dir_hbm, schur_hbm, resid_hbm, basis_hbm, coarse_hbm,
                 image_ref, f0, f1, f2, f3, dir_ref, resid_ref, basis_ref, coarse_ref, *rest):
    *send_ref, perm_ref, schur_ref, sems = rest
    rows = schur_ref.shape[0] // CHUNKS
    parts = [pl.ds(i * rows, rows) for i in range(CHUNKS)]
    pairs = [(dir_hbm, dir_ref), (perm_hbm, perm_ref)]
    pairs += [(schur_hbm.at[part], schur_ref.at[part]) for part in parts]
    for ref in send_ref:
        pairs += [(coarse_hbm.at[other_block(i, 0)], ref.at[i]) for i in range(ref.shape[0])]
    pairs += [(resid_hbm, resid_ref), (basis_hbm, basis_ref), (coarse_hbm, coarse_ref)]
    copies = [pltpu.make_async_copy(source, target, sems.at[i]) for i, (source, target) in enumerate(pairs)]
    for copy in copies:
        copy.start()
    copies[0].wait()
    total = None
    for i, part in enumerate(parts):
        copies[2 + i].wait()
        term = jnp.dot(dir_ref[:, part].astype(BF16), schur_ref[part], preferred_element_type=F32)
        total = term if total is None else total + term
    image_ref[...] = total
    copies[1].wait()
    put_faces(perm_ref, total, (f0, f1, f2, f3))
    for copy in copies[2 + CHUNKS :]:
        copy.wait()


def merge_kernel(k, last, blocks_ref, got_ref, out_ref, *send_ref):
    out_ref[...] = blocks_ref[...]
    for i in range(got_ref.shape[0]):
        out_ref[other_block(i, k)] = got_ref[i]
    if not last:
        for i in range(got_ref.shape[0]):
            send_ref[0][i] = out_ref[other_block(i, k + 1)]


def join_kernel(k, depth, prim, blocks_ref, got_ref, wide_ref, all_ref):
    all_ref[...] = blocks_ref[...]
    for i in range(got_ref.shape[0]):
        all_ref[other_block(i, k)] = got_ref[i]
    slabs, rows, width = blocks_ref.shape
    width = width // 2
    for half in range(2):
        for h in range(slabs):
            at = (half * slabs + h) * width
            wide_ref[:, at : at + width] = all_ref[h, :, half * width : (half + 1) * width]
    row = lax.broadcasted_iota(jnp.int32, wide_ref.shape, 0)
    lane = lax.broadcasted_iota(jnp.int32, wide_ref.shape, 1)
    picked = jnp.logical_and(lane < slabs * width, lane % depth == prim // 2)
    wide = jnp.where(row == prim, jnp.where(picked, 1.0, 0.0), wide_ref[...].astype(F32))
    wide_ref[...] = wide.astype(BF16)


def spread_kernel(k, matrix_ref, blocks_ref, send_ref):
    slabs, rows, _ = blocks_ref.shape
    prim = matrix_ref.shape[0] // slabs
    half = prim // 2
    sectors = matrix_ref.shape[1] // prim
    width = blocks_ref.shape[2] // 2
    depth = width // sectors
    source = lax.broadcasted_iota(jnp.int32, (sectors * prim, 2 * width), 0)
    place = lax.broadcasted_iota(jnp.int32, (sectors * prim, 2 * width), 1)
    later = place // width
    within = place % width
    sector, at = within // depth, within % depth
    chosen = jnp.logical_and(at < half, source == sector * prim + later * half + at)
    spread = jnp.dot(matrix_ref[...], jnp.where(chosen, 1.0, 0.0).astype(BF16), preferred_element_type=F32)
    empty = jnp.zeros((rows - prim, 2 * width), F32)
    for g in range(slabs):
        own = jnp.concatenate([spread[g * prim : (g + 1) * prim], empty], axis=0)
        blocks_ref[g] = own.astype(BF16)
    for i in range(send_ref.shape[0]):
        send_ref[i] = blocks_ref[other_block(i, k)]


def conduct_at(row, sector):
    lane = lax.broadcasted_iota(jnp.int32, row.shape, 1)
    return jnp.sum(jnp.where(lane == sector, row, 0.0), axis=1, keepdims=True)


def early_kernel(perm_ref, conduct_ref, dir_ref, image_ref, resid_ref, basis_ref,
                 weight_ref, rhs_ref, curv_ref, scaled_ref):
    slab, sector = lax.axis_index("gx"), lax.axis_index("col")
    slabs, sectors = lax.axis_size("gx"), lax.axis_size("col")
    row = conduct_ref[pl.ds(slab, 1), :]
    own = conduct_at(row, sector)
    below = conduct_at(conduct_ref[pl.ds(jnp.maximum(slab - 1, 0), 1), :], sector)
    above = conduct_at(conduct_ref[pl.ds(jnp.minimum(slab + 1, slabs - 1), 1), :], sector)
    below = jnp.where(slab > 0, below, 0.0)
    above = jnp.where(slab < slabs - 1, above, 0.0)
    left = conduct_at(row, (sector + sectors - 1) % sectors)
    right = conduct_at(row, (sector + 1) % sectors)
    across = [jnp.broadcast_to(own / (own + other), (1, BLK)) for other in (below, above, left, right)]
    places = [slot_place(perm_ref, slot) for slot in range(8)]
    for b in range(weight_ref.shape[1] // BLK):
        weight = across[0]
        for slot in range(2, 8):
            weight = jnp.where(places[slot] == b, across[slot // 2], weight)
        weight_ref[:, b * BLK : (b + 1) * BLK] = jnp.broadcast_to(weight, (8, BLK))
    scaled = (weight_ref[0:1, :] * resid_ref[...]).astype(BF16)
    scaled_ref[...] = scaled
    rhs_ref[...] = lax.dot_general(
        basis_ref[...], scaled, (((1,), (1,)), ((), ())), preferred_element_type=F32
    )
    curv = to_row(jnp.sum(dir_ref[...] * image_ref[...], axis=1, keepdims=True))
    high = curv.astype(BF16).astype(F32)
    n = curv.shape[1]
    curv_ref[...] = jnp.zeros_like(curv_ref)
    curv_ref[0:1, 0:n] = high
    curv_ref[0:1, n : 2 * n] = curv - high


def coarse_rhs_kernel(rows, sectors, perm_ref, image_ref, r0, r1, r2, r3, weight_ref, basis_ref, rhs_ref, curv_ref,
                      assembled_ref, scaled_ref, rhs_q_ref, out_ref):
    for at, part in received_blocks(perm_ref, (r0, r1, r2, r3), image_ref.shape[1] // BLK):
        assembled_ref[:, at] = image_ref[:, at] + part
    scaled = (weight_ref[0:1, :] * assembled_ref[...]).astype(BF16)
    scaled_ref[...] = scaled
    rhs_q = lax.dot_general(
        basis_ref[...], scaled, (((1,), (1,)), ((), ())), preferred_element_type=F32
    )
    rhs_q_ref[...] = rhs_q
    rhs_r = rhs_ref[...]
    half = rhs_r.shape[0] // 2
    packed = jnp.concatenate([rhs_r[:half], rhs_q[:half], rhs_r[half:], rhs_q[half:]], axis=1)
    packed = jnp.concatenate(
        [packed, curv_ref[0:1, :], jnp.zeros((rows - half - 1, BLK), F32)], axis=0
    )
    several = jnp.concatenate([packed] * sectors, axis=0).astype(BF16)
    step = several.shape[0]
    for i in range(out_ref.shape[0] // step):
        out_ref[i * step : (i + 1) * step] = several


def neumann_kernel(scaled_r_ref, scaled_q_ref, resid_ref, assembled_ref, weight_ref, neumann_hbm,
                   sol_r_ref, sol_q_ref, sums_ref, neumann_ref, sems):
    rows = neumann_ref.shape[0] // CHUNKS
    parts = [pl.ds(i * rows, rows) for i in range(CHUNKS)]
    copies = [
        pltpu.make_async_copy(neumann_hbm.at[part], neumann_ref.at[part], sems.at[i])
        for i, part in enumerate(parts)
    ]
    for copy in copies:
        copy.start()
    total_r = total_q = None
    for copy, part in zip(copies, parts):
        copy.wait()
        term_r = jnp.dot(scaled_r_ref[:, part], neumann_ref[part], preferred_element_type=F32)
        term_q = jnp.dot(scaled_q_ref[:, part], neumann_ref[part], preferred_element_type=F32)
        total_r = term_r if total_r is None else total_r + term_r
        total_q = term_q if total_q is None else total_q + term_q
    sol_r_ref[...] = total_r
    sol_q_ref[...] = total_q
    weighted_r = weight_ref[0:1, :] * resid_ref[...]
    weighted_q = weight_ref[0:1, :] * assembled_ref[...]
    n = total_r.shape[0]
    sums_ref[...] = jnp.zeros_like(sums_ref)
    for i, product in enumerate(
        (weighted_r * total_r, weighted_r * total_q + weighted_q * total_r, weighted_q * total_q)
    ):
        sums_ref[0:1, i * n : (i + 1) * n] = to_row(jnp.sum(product, axis=1, keepdims=True))


def solve_kernel(perm_ref, gathered_ref, wide_ref, prev_ref, weight_ref, basis_ref, sol_r_ref, sol_q_ref,
                 sums_ref, rhs_r_ref, rhs_q_ref, step_out, weighted_out, rz_out, f0, f1, f2, f3, rz_ref, sem):
    n = prev_ref.shape[1]
    prim = basis_ref.shape[0]
    halves = jnp.concatenate([gathered_ref[:, : 2 * n], gathered_ref[:, 2 * n :]], axis=0)
    total = jnp.dot(wide_ref[...], halves, preferred_element_type=F32)
    step = prev_ref[...] / (total[prim : prim + 1, 0:n] + total[prim : prim + 1, n : 2 * n])
    coarse_sol = (total[0:prim, 0:n] - step * total[0:prim, n : 2 * n]).astype(BF16)
    coarse_part = coarse_sol.astype(F32) * (rhs_r_ref[...] - step * rhs_q_ref[...])
    partial = (
        sums_ref[0:1, 0:n]
        - step * (sums_ref[0:1, n : 2 * n] - step * sums_ref[0:1, 2 * n : 3 * n])
        + jnp.sum(coarse_part, axis=0, keepdims=True)
    )
    partial = jnp.concatenate([partial, jnp.zeros((1, BLK - n), F32)], axis=1)
    for i in range(rz_ref.shape[0]):
        rz_ref[i] = partial
    copy = pltpu.make_async_copy(rz_ref, rz_out, sem)
    copy.start()
    correction = lax.dot_general(
        coarse_sol, basis_ref[...], (((0,), (0,)), ((), ())), preferred_element_type=F32
    )
    step_col = to_column(step)
    step_out[...] = jnp.broadcast_to(step_col, step_out.shape)
    weighted = weight_ref[0:1, :] * (sol_r_ref[...] - step_col * sol_q_ref[...] + correction)
    weighted_out[...] = weighted
    put_faces(perm_ref, weighted, (f0, f1, f2, f3))
    copy.wait()


def resid_kernel(step_ref, resid_ref, assembled_ref, out_ref):
    out_ref[...] = resid_ref[...] - step_ref[:, 0:1] * assembled_ref[...]


def direction_kernel(perm_ref, partials_ref, rz_ref, dir_ref, weighted_ref, r0, r1, r2, r3,
                     out_ref, rz_out):
    n = rz_ref.shape[1]
    rz_next = jnp.sum(partials_ref[...], axis=0)[:, 0:n]
    rz_out[...] = rz_next
    factor = to_column(rz_next / rz_ref[...])
    for at, part in received_blocks(perm_ref, (r0, r1, r2, r3), dir_ref.shape[1] // BLK):
        out_ref[:, at] = weighted_ref[:, at] + factor * dir_ref[:, at] + part


def split(value):
    high = value.astype(BF16).astype(F32)
    return high, value - high


def spread_pair_kernel(after_ref, own_ref, mate_ref, out_ref):
    slabs = lax.axis_size("gx")
    prim = own_ref.shape[0] // slabs
    half = prim // 2
    sectors = own_ref.shape[1] // prim
    width = out_ref.shape[2] // 2
    depth = width // sectors
    source = lax.broadcasted_iota(jnp.int32, (sectors * prim, 2 * width), 0)
    place = lax.broadcasted_iota(jnp.int32, (sectors * prim, 2 * width), 1)
    later = place // width
    within = place % width
    sector, at = within // depth, within % depth
    chosen = jnp.logical_and(at < half, source == sector * prim + later * half + at)
    chosen = jnp.where(chosen, 1.0, 0.0).astype(BF16)
    mine = lax.axis_index("gx") % 2
    for ref, bit in ((own_ref, mine), (mate_ref, 1 - mine)):
        out_ref[bit] = jnp.dot(ref[...], chosen, preferred_element_type=F32).astype(BF16)


def gather_kernel(k, after_ref, mine_ref, got_ref, out_ref, both_ref):
    bit = (lax.axis_index("gx") >> k) % 2
    n = mine_ref.shape[0]
    for i in range(n):
        both_ref[bit * n + i] = mine_ref[i]
        both_ref[(1 - bit) * n + i] = got_ref[i]
    out_ref[...] = jnp.concatenate([both_ref[i] for i in range(2 * n)], axis=1)


def near_rhs_kernel(rows, sectors, perm_ref, image_ref, r0, r1, r2, r3, weight_ref, basis_ref, rhs_ref, curv_ref,
                    scaled_ref, resid_ref, neumann_ref, assembled_ref, sol_r_ref, sol_q_ref, out_ref):
    for at, part in received_blocks(perm_ref, (r0, r1, r2, r3), image_ref.shape[1] // BLK):
        assembled_ref[:, at] = image_ref[:, at] + part
    weighted_r = weight_ref[0:1, :] * resid_ref[...]
    weighted_q = weight_ref[0:1, :] * assembled_ref[...]
    scaled = weighted_q.astype(BF16)
    n = scaled.shape[0]
    both = jnp.concatenate([scaled_ref[...], scaled], axis=0)
    sol = jnp.dot(both, neumann_ref[...], preferred_element_type=F32)
    rhs_q = lax.dot_general(
        basis_ref[...], scaled, (((1,), (1,)), ((), ())), preferred_element_type=F32
    )
    sol_r, sol_q = sol[:n], sol[n:]
    sol_r_ref[...] = sol_r
    sol_q_ref[...] = sol_q
    products = (weighted_r * sol_r, weighted_r * sol_q + weighted_q * sol_r, weighted_q * sol_q)
    sums = [to_row(jnp.sum(product, axis=1, keepdims=True)) for product in products]
    first = jnp.concatenate([curv_ref[0:1, : 2 * n], *split(sums[0])], axis=1)
    second = jnp.concatenate([*split(sums[1]), *split(sums[2])], axis=1)
    rhs_r = rhs_ref[...]
    half = rhs_r.shape[0] // 2
    packed = jnp.concatenate([rhs_r[:half], rhs_q[:half], rhs_r[half:], rhs_q[half:]], axis=1)
    packed = jnp.concatenate([packed, first, second], axis=0)
    several = jnp.concatenate([packed] * sectors, axis=0).astype(BF16)
    step = several.shape[0]
    for i in range(out_ref.shape[0] // step):
        out_ref[i * step : (i + 1) * step] = several


def frame_kernel(depth, perm_ref, weight_ref, r_ref, q_ref, basis_ref, r_out, q_out, picks_ref, basis_out, f2, f3):
    weighted_r = weight_ref[0:1, :] * r_ref[...]
    weighted_q = weight_ref[0:1, :] * q_ref[...]
    r_out[...] = weighted_r
    q_out[...] = weighted_q
    prim = basis_ref.shape[0]
    n = r_ref.shape[0]
    weighted_basis = weight_ref[0:1, :] * basis_ref[...].astype(F32)
    blank = jnp.zeros((f2.shape[0] - 2 * n - prim, r_ref.shape[1]), F32)
    put_faces(perm_ref, jnp.concatenate([weighted_r, weighted_q, weighted_basis, blank], axis=0), (f2, f3), 2)
    half = prim // 2
    rows = basis_out.shape[0]
    slabs, sectors = lax.axis_size("gx"), lax.axis_size("col")
    width = sectors * depth
    row = lax.broadcasted_iota(jnp.int32, picks_ref.shape, 0)
    lane = lax.broadcasted_iota(jnp.int32, picks_ref.shape, 1)
    part = lane // width % 2
    at = lane % depth
    sums = jnp.logical_and(at >= half, row == (at - half) * 2 + part)
    mine = jnp.logical_and(lane % width // depth == lax.axis_index("col"), at < half)
    own = jnp.logical_and(mine, row == 16 + lane // (2 * width) * prim + part * half + at)
    picks_ref[...] = jnp.where(jnp.logical_or(sums, own), 1.0, 0.0).astype(BF16)
    row = lax.broadcasted_iota(jnp.int32, (rows, prim), 0)
    lane = lax.broadcasted_iota(jnp.int32, (rows, prim), 1)
    here = jnp.where(row == lax.axis_index("gx") * prim + lane, 1.0, 0.0).astype(BF16)
    basis_out[...] = jnp.dot(here, basis_ref[...], preferred_element_type=F32).astype(BF16)


def near_solve_kernel(r2, r3, perm_ref, gathered_ref, mine_ref, got_ref, picks_ref, prev_ref, weight_ref, basis_ref,
                      sol_r_ref, sol_q_ref, step_out, weighted_out, base_out, part_out, sol_out, f0, f1, rhs_ref):
    n = prev_ref.shape[1]
    slabs = lax.axis_size("gx")
    width = gathered_ref.shape[0] // slabs
    for h in range(slabs):
        part = gathered_ref[h * width : (h + 1) * width]
        rhs_ref[2 * h * width : (2 * h + 1) * width] = part[:, : 2 * n]
        rhs_ref[(2 * h + 1) * width : (2 * h + 2) * width] = part[:, 2 * n :]
    count = slabs * width
    top = (lax.axis_index("gx") * 2) // slabs
    mine = rhs_ref[pl.ds(pl.multiple_of(top * count, 16), count), :]
    got = rhs_ref[pl.ds(pl.multiple_of((1 - top) * count, 16), count), :]
    picked = jnp.dot(picks_ref[...], rhs_ref[...], preferred_element_type=F32)
    total = jnp.dot(mine_ref[...], mine, preferred_element_type=F32) + jnp.dot(
        got_ref[...], got, preferred_element_type=F32
    )
    curvature, first, second, third = (picked[i : i + 1, 0:n] + picked[i : i + 1, n : 2 * n] for i in range(4))
    step = prev_ref[...] / curvature
    sol = (total[:, 0:n] - step * total[:, n : 2 * n]).astype(BF16)
    rhs = picked[16:, 0:n] - step * picked[16:, n : 2 * n]
    sol_out[...] = sol
    high, low = split(jnp.sum(sol.astype(F32) * rhs, axis=0, keepdims=True))
    correction = lax.dot_general(
        sol, basis_ref[...], (((0,), (0,)), ((), ())), preferred_element_type=F32
    )
    step_col = to_column(step)
    step_out[...] = jnp.broadcast_to(step_col, step_out.shape)
    weighted = sol_r_ref[...] - step_col * sol_q_ref[...] + weight_ref[0:1, :] * correction
    weighted_out[...] = weighted
    blank = jnp.zeros((1, BLK - n), F32)
    low = low.astype(BF16).astype(F32)
    base = first - step * (second - step * third)
    base_out[...] = jnp.broadcast_to(jnp.concatenate([base, blank], axis=1), base_out.shape)
    part_out[...] = jnp.broadcast_to(jnp.concatenate([high + low, blank], axis=1), part_out.shape)
    put_faces(perm_ref, weighted, (f0, f1))
    lines = jnp.concatenate([high, low, jnp.zeros((14, n), F32)], axis=0)
    lines = jnp.concatenate([lines, jnp.zeros((16, 2 * BLK - n), F32)], axis=1).astype(BF16)
    f0[n : n + 16, :] = lines
    f1[n : n + 16, :] = lines


def beside_kernel(perm_ref, sol_ref, step_ref, weighted_ref, r2, r3, out_ref):
    n = weighted_ref.shape[0]
    slab, slabs = lax.axis_index("gx"), lax.axis_size("gx")
    prim = sol_ref.shape[0] // slabs
    received = []
    for got, other in ((r2, jnp.where(slab % 2 == 1, slab + 1, slab - 1)), (r3, slab + 1 - 2 * (slab % 2))):
        rows = got.shape[0] - 2 * n
        row = lax.broadcasted_iota(jnp.int32, (rows, sol_ref.shape[0]), 0)
        lane = lax.broadcasted_iota(jnp.int32, (rows, sol_ref.shape[0]), 1)
        chosen = jnp.logical_and(row < prim, lane == other * prim + row)
        sol = jnp.dot(jnp.where(chosen, 1.0, 0.0).astype(BF16), sol_ref[...], preferred_element_type=F32)
        correction = lax.dot_general(
            sol.astype(BF16), got[2 * n :, :], (((0,), (0,)), ((), ())), preferred_element_type=F32
        )
        step = step_ref[:, 0:1]
        received.append(got[0:n, :].astype(F32) - step * got[n : 2 * n, :].astype(F32) + correction)
    for at, part in some_received_blocks(perm_ref, received, weighted_ref.shape[1] // BLK, 2):
        out_ref[:, at] = weighted_ref[:, at] + part


def near_direction_kernel(perm_ref, rz_ref, dir_ref, weighted_ref, base_ref, part_ref, far_ref, r0, r1,
                          out_ref, rz_out):
    n = rz_ref.shape[1]
    sector = lax.axis_index("col")
    beside = jnp.where(sector % 2 == 1, (sector + 1) % 4, (sector + 3) % 4)
    parts = [(sector, part_ref[0:1, 0:n]), (sector ^ 2, far_ref[0:1, 0:n])]
    for ref, other in ((r0, beside), (r1, sector ^ 1)):
        lines = ref[n : n + 16, 0:n].astype(F32)
        parts.append((other, lines[0:1] + lines[1:2]))
    rz_next = base_ref[0:1, 0:n]
    for at in range(4):
        value = parts[0][1]
        for other, part in parts[1:]:
            value = jnp.where(other == at, part, value)
        rz_next = rz_next + value
    rz_out[...] = rz_next
    factor = to_column(rz_next / rz_ref[...])
    received = (r0[0:n, :], r1[0:n, :])
    for at, part in some_received_blocks(perm_ref, received, dir_ref.shape[1] // BLK, 0):
        out_ref[:, at] = weighted_ref[:, at] + factor * dir_ref[:, at] + part


def near_rest(perm, rz_row, neumann, image, received, weight, rhs_r, curv, scaled_r, direction, resid, basis_t,
              coarse, rows):
    rhs, width = resid.shape
    prim = basis_t.shape[0]
    slabs, sectors = lax.axis_size("gx"), lax.axis_size("col")
    vmem = pl.BlockSpec(memory_space=VMEM)
    full = jax.ShapeDtypeStruct((rhs, width), F32)
    line = jax.ShapeDtypeStruct((8, BLK), F32)
    small = cost(1 << 10, 1 << 16)

    def call(kernel, outs, *args, scratch=(), estimate=small, after=()):
        return pl.pallas_call(
            kernel, out_shape=outs, in_specs=[pl.BlockSpec(memory_space=pl.ANY)] * len(after) + [vmem] * len(args),
            out_specs=(vmem,) * len(outs), scratch_shapes=scratch, compiler_params=params(), cost_estimate=estimate,
        )(*after, *args)

    mate = swap_bit(coarse, 0)
    flat = (slabs * prim, sectors * prim)
    shard = (slabs * prim, 2 * sectors * rows)
    (blocks,) = call(
        spread_pair_kernel, (jax.ShapeDtypeStruct((2,) + shard, BF16),),
        coarse.reshape(flat), mate.reshape(flat), after=(perm,),
    )
    assembled, sol_r, sol_q, packed = call(
        functools.partial(near_rhs_kernel, rows, sectors),
        (full, full, full, jax.ShapeDtypeStruct((slabs * sectors * rows, BLK), BF16)),
        perm, image, *received, weight, basis_t, rhs_r, curv, scaled_r, resid, neumann,
        estimate=cost(2000 * rhs * width * width, 1 << 16),
    )
    (blocks,) = call(
        functools.partial(gather_kernel, 1), (jax.ShapeDtypeStruct((shard[0], 4 * shard[1]), BF16),),
        blocks, swap_bit(blocks, 1), after=(packed,), scratch=[pltpu.VMEM((4,) + shard, BF16)],
        estimate=cost(2000 * rhs * width * width, 1 << 16),
    )
    got = swap_bit(blocks, 2)
    packed = packed.reshape(slabs * sectors, rows // 2, 2, BLK)
    gathered = lax.all_to_all(packed, ("gx", "col"), 0, 0).reshape(slabs * sectors * rows, BLK)
    face = jax.ShapeDtypeStruct((-(-(2 * rhs + prim) // 16) * 16, 2 * BLK), BF16)
    sol_r, sol_q, picks, placed, f2, f3 = call(
        functools.partial(frame_kernel, rows),
        (
            full,
            full,
            jax.ShapeDtypeStruct((16 + slabs * prim, slabs * shard[1]), BF16),
            jax.ShapeDtypeStruct((slabs * prim, width), BF16),
            face,
            face,
        ),
        perm, weight, sol_r, sol_q, basis_t,
    )
    r2, r3 = swap_faces((f2, f3), 2)
    tall = jax.ShapeDtypeStruct((rhs + 16, 2 * BLK), BF16)
    step, weighted, base, part, sol, f0, f1 = call(
        near_solve_kernel,
        (
            jax.ShapeDtypeStruct((rhs, BLK), F32),
            full,
            line,
            jax.ShapeDtypeStruct((8, BLK), F32),
            jax.ShapeDtypeStruct((slabs * prim, rhs), BF16),
            jax.ShapeDtypeStruct((64, 2 * BLK), BF16),
            jax.ShapeDtypeStruct((48, 2 * BLK), BF16),
        ),
        perm, gathered, blocks, got, picks, rz_row, weight, placed, sol_r, sol_q,
        scratch=[pltpu.VMEM((slabs * shard[1], 2 * rhs), BF16)], after=(r2, r3),
    )
    far = lax.ppermute(part, "col", [(i, i ^ 2) for i in range(sectors)])
    r0, r1 = swap_faces((f0, f1))
    (weighted,) = call(beside_kernel, (full,), perm, sol, step, weighted, r2, r3)
    (resid_new,) = call(resid_kernel, (full,), step, resid, assembled)
    direction_new, rz_next = call(
        near_direction_kernel, (full, jax.ShapeDtypeStruct((1, rhs), F32)),
        perm, rz_row, direction, weighted, base, part, far, r0, r1,
    )
    return (resid_new[None, None], direction_new[None, None], rz_next[0])


def body(resid, direction, rz_prev, schur, neumann, basis, coarse_inv, conduct, face_perm):
    resid, direction, schur, neumann = resid[0, 0], direction[0, 0], schur[0, 0], neumann[0, 0]
    basis_t = basis[0, 0].T
    perm = face_perm[0]
    rhs, width = resid.shape
    prim = basis_t.shape[0]
    slabs, sectors = lax.axis_size("gx"), lax.axis_size("col")
    rows = -(-(prim // 2 + 1) // 4) * 4
    block_rows = -(-(prim + 1) // 16) * 16
    rounds = slabs.bit_length() - 1
    face = jax.ShapeDtypeStruct((rhs, 2 * BLK), BF16)
    full = jax.ShapeDtypeStruct((rhs, width), F32)
    rz_row = rz_prev[None, :]
    vmem = pl.BlockSpec(memory_space=VMEM)
    hbm = pl.BlockSpec(memory_space=pltpu.HBM)
    anywhere = pl.BlockSpec(memory_space=pl.ANY)
    flops = 2 * rhs * width * width
    coarse = coarse_inv[0, :, :, 0]
    coarse_type = jax.ShapeDtypeStruct(coarse.shape, BF16)
    send_type = jax.ShapeDtypeStruct((slabs // 2,) + coarse.shape[1:], BF16)
    blocks_type = jax.ShapeDtypeStruct((slabs, block_rows, 2 * sectors * rows), BF16)

    near = sectors == 4 and slabs == 8
    sends = () if near else (send_type,)
    fetched = [pltpu.with_memory_space_constraint(x, pltpu.HBM) for x in (perm, direction, schur, resid, basis_t, coarse)]
    image, f0, f1, f2, f3, direction, resid, basis_t, coarse, *send = pl.pallas_call(
        image_kernel,
        out_shape=(full,) + (face,) * 4
        + (full, full, jax.ShapeDtypeStruct((prim, width), BF16), coarse_type) + sends,
        in_specs=[hbm] * 6, out_specs=(vmem,) * (9 + len(sends)),
        scratch_shapes=[
            pltpu.VMEM(perm.shape, jnp.int32),
            pltpu.VMEM((width, width), BF16),
            pltpu.SemaphoreType.DMA((CHUNKS + 5 + len(sends) * (slabs // 2),)),
        ],
        compiler_params=params(), cost_estimate=cost(flops, 2 * width * width),
    )(*fetched)
    received = swap_faces((f0, f1, f2, f3))
    weight, rhs_r, curv, scaled_r = pl.pallas_call(
        early_kernel,
        out_shape=(
            jax.ShapeDtypeStruct((8, width), F32),
            jax.ShapeDtypeStruct((prim, rhs), F32),
            jax.ShapeDtypeStruct((8, BLK), F32),
            jax.ShapeDtypeStruct((rhs, width), BF16),
        ),
        in_specs=[vmem] * 6, out_specs=(vmem,) * 4, compiler_params=params(),
        cost_estimate=cost(1000 * flops, 8 * rhs * width),
    )(perm, conduct, direction, image, resid, basis_t)
    if near:
        return near_rest(perm, rz_row, neumann, image, received, weight, rhs_r, curv, scaled_r, direction, resid,
                         basis_t, coarse, rows)
    send = send[0]
    for k in range(rounds - 1):
        got = swap_bit(send, k)
        last = k + 2 == rounds
        coarse, *send = pl.pallas_call(
            functools.partial(merge_kernel, k, last),
            out_shape=(coarse_type,) if last else (coarse_type, send_type),
            in_specs=[vmem] * 2, out_specs=(vmem,) if last else (vmem,) * 2,
            compiler_params=params(), cost_estimate=cost(1 << 10, 1 << 16),
        )(coarse, got)
        send = send[0] if send else None
    blocks, send = pl.pallas_call(
        functools.partial(spread_kernel, rounds - 1),
        out_shape=(blocks_type, jax.ShapeDtypeStruct((slabs // 2,) + blocks_type.shape[1:], BF16)),
        in_specs=[vmem], out_specs=(vmem,) * 2,
        compiler_params=params(), cost_estimate=cost(1 << 20, 1 << 16),
    )(coarse.reshape(slabs * prim, sectors * prim))
    wide = pl.pallas_call(
        functools.partial(join_kernel, rounds - 1, rows, prim),
        out_shape=jax.ShapeDtypeStruct((block_rows, slabs * blocks_type.shape[2]), BF16),
        in_specs=[vmem] * 2, out_specs=vmem,
        scratch_shapes=[pltpu.VMEM(blocks_type.shape, BF16)],
        compiler_params=params(), cost_estimate=cost(1 << 10, 1 << 16),
    )(blocks, swap_bit(send, rounds - 1))
    assembled, scaled_q, rhs_q, packed = pl.pallas_call(
        functools.partial(coarse_rhs_kernel, rows, sectors),
        out_shape=(
            full,
            jax.ShapeDtypeStruct((rhs, width), BF16),
            jax.ShapeDtypeStruct((prim, rhs), F32),
            jax.ShapeDtypeStruct((slabs * sectors * rows, BLK), BF16),
        ),
        in_specs=[vmem] + [vmem] * 9, out_specs=(vmem,) * 4, compiler_params=params(),
        cost_estimate=cost(2 * rhs * width * prim, 8 * rhs * width),
    )(perm, image, *received, weight, basis_t, rhs_r, curv)
    packed = packed.reshape(slabs * sectors, rows // 2, 2, BLK)
    gathered = lax.all_to_all(packed, ("gx", "col"), 0, 0).reshape(slabs * sectors * rows, BLK)
    sol_r, sol_q, sums = pl.pallas_call(
        neumann_kernel,
        out_shape=(full, full, jax.ShapeDtypeStruct((8, BLK), F32)),
        in_specs=[vmem] * 5 + [hbm], out_specs=(vmem,) * 3,
        scratch_shapes=[pltpu.VMEM((width, width), BF16), pltpu.SemaphoreType.DMA((CHUNKS,))],
        compiler_params=params(), cost_estimate=cost(1000 * flops, 2 * width * width),
    )(scaled_r, scaled_q, resid, assembled, weight, pltpu.with_memory_space_constraint(neumann, pltpu.HBM))
    step, weighted, partial, *faces = pl.pallas_call(
        solve_kernel,
        out_shape=(
            jax.ShapeDtypeStruct((rhs, BLK), F32),
            full,
            jax.ShapeDtypeStruct((slabs * sectors, 1, BLK), F32),
        )
        + (face,) * 4,
        in_specs=[vmem] * 11, out_specs=(vmem, vmem, anywhere) + (vmem,) * 4,
        scratch_shapes=[pltpu.VMEM((slabs * sectors, 1, BLK), F32), pltpu.SemaphoreType.DMA],
        compiler_params=params(), cost_estimate=cost(2 * rhs * width * prim, 8 * rhs * width),
    )(perm, gathered, wide, rz_row, weight, basis_t, sol_r, sol_q, sums, rhs_r, rhs_q)
    partials = lax.all_to_all(partial, ("gx", "col"), 0, 0)
    received = swap_faces(faces)
    resid_new = pl.pallas_call(
        resid_kernel, out_shape=full, in_specs=[vmem] * 3, out_specs=vmem,
        compiler_params=params(), cost_estimate=cost(2 * rhs * width, 12 * rhs * width),
    )(step, resid, assembled)
    direction_new, rz_next = pl.pallas_call(
        direction_kernel, out_shape=(full, jax.ShapeDtypeStruct((1, rhs), F32)),
        in_specs=[vmem] + [vmem] * 8, out_specs=(vmem,) * 2, compiler_params=params(),
        cost_estimate=cost(2 * rhs * width, 8 * rhs * width),
    )(perm, partials, rz_row, direction, weighted, *received)
    return (resid_new[None, None], direction_new[None, None], rz_next[0])


def solution(mesh):
    placed = (
        P("gx", "col", None, None),
        P("gx", "col", None, None),
        P(),
        P("gx", "col", None, None),
        P("gx", "col", None, None),
        P("gx", "col", None, None),
        P("col", None, None, "gx", None, None),
        P(),
        P("gx", "col", None),
    )
    return jax.shard_map(
        body,
        mesh=mesh,
        in_specs=placed,
        out_specs=(P("gx", "col", None, None), P("gx", "col", None, None), P()),
        check_vma=False,
    )
```

```python
import functools

import jax
import jax.numpy as jnp
from jax import lax
from jax.experimental import pallas as pl
from jax.experimental.pallas import tpu as pltpu
from jax.sharding import PartitionSpec as P

F32 = jnp.float32
BF16 = jnp.bfloat16
BLK = 128
EXACT = lax.Precision.HIGHEST
VMEM = pltpu.VMEM


def params(limit=16 * 1024 * 1024):
    return pltpu.CompilerParams(vmem_limit_bytes=limit)


def cost(flops, nbytes):
    return pl.CostEstimate(flops=flops, bytes_accessed=nbytes, transcendentals=0)


def swap(value, axis, offset):
    count = lax.axis_size(axis)
    pairs = []
    for low in range(offset, count, 2):
        high = (low + 1) % count
        pairs += [(low, high), (high, low)]
    return lax.ppermute(value, axis, pairs)


def swap_second(value):
    slabs, sectors = lax.axis_size("gx"), lax.axis_size("col")
    pairs = []
    for slab in range(slabs):
        for sector in range(sectors):
            other = (slab + 1 if slab % 2 else slab - 1, sector)
            if not 0 <= other[0] < slabs:
                other = (slab, sector ^ 1)
            pairs.append((slab * sectors + sector, other[0] * sectors + other[1]))
    return lax.ppermute(value, ("gx", "col"), pairs)


def swap_faces(faces, first=0):
    swaps = (
        lambda face: swap(face, "col", 1),
        lambda face: swap(face, "col", 0),
        swap_second,
        lambda face: swap(face, "gx", 0),
    )
    return [swaps[first + i](face) for i, face in enumerate(faces)]


def swap_counts():
    slab = lax.axis_index("gx")
    inside = jnp.logical_and(slab > 0, slab < lax.axis_size("gx") - 1)
    return (None, None, inside, None)


def slot_place(perm_ref, slot):
    return jnp.broadcast_to(perm_ref[0:1, slot : slot + 1], (1, BLK))


def swapped_places(perm_ref):
    slab = lax.axis_index("gx") % 2
    sector = lax.axis_index("col") % 2
    places = []
    for parity, even, odd in ((sector, 2, 3), (sector, 3, 2), (slab, 0, 1), (slab, 1, 0)):
        for j in range(2):
            at_even, at_odd = (slot_place(perm_ref, 2 * face + j) for face in (even, odd))
            places.append(jnp.where(parity == 0, at_even, at_odd))
    return places


def put_faces(perm_ref, source, outs, first=0):
    blocks = [source[:, b * BLK : (b + 1) * BLK] for b in range(source.shape[1] // BLK)]
    for i, place in enumerate(swapped_places(perm_ref)[2 * first : 2 * (first + len(outs))]):
        chosen = blocks[0]
        for b in range(1, len(blocks)):
            chosen = jnp.where(place == b, blocks[b], chosen)
        j = i % 2
        outs[i // 2][0 : chosen.shape[0], j * BLK : (j + 1) * BLK] = chosen.astype(BF16)


def received_blocks(perm_ref, received, blocks):
    places = swapped_places(perm_ref)
    parts = []
    for i in range(len(places)):
        j = i % 2
        part = received[i // 2][:, j * BLK : (j + 1) * BLK].astype(F32)
        counts = swap_counts()[i // 2]
        parts.append(part if counts is None else jnp.where(counts, part, 0.0))
    for b in range(blocks):
        chosen = parts[0]
        for place, part in zip(places[1:], parts[1:]):
            chosen = jnp.where(place == b, part, chosen)
        yield slice(b * BLK, (b + 1) * BLK), chosen


def some_received_blocks(perm_ref, received, blocks, first):
    places = swapped_places(perm_ref)[2 * first :]
    parts = []
    for i, got in enumerate(received):
        counts = swap_counts()[first + i]
        for j in range(2):
            part = got[:, j * BLK : (j + 1) * BLK].astype(F32)
            parts.append(part if counts is None else jnp.where(counts, part, 0.0))
    for b in range(blocks):
        chosen = jnp.zeros_like(parts[0])
        for place, part in zip(places, parts):
            chosen = jnp.where(place == b, part, chosen)
        yield slice(b * BLK, (b + 1) * BLK), chosen


def to_column(row):
    n = row.shape[1]
    at = lax.broadcasted_iota(jnp.int32, (n, n), 0) == lax.broadcasted_iota(jnp.int32, (n, n), 1)
    return jnp.sum(jnp.where(at, row, 0.0), axis=1, keepdims=True)


def to_row(column):
    n = column.shape[0]
    at = lax.broadcasted_iota(jnp.int32, (n, n), 0) == lax.broadcasted_iota(jnp.int32, (n, n), 1)
    return jnp.sum(jnp.where(at, column, 0.0), axis=0, keepdims=True)


CHUNKS = 4


def other_block(i, k):
    mine = (lax.axis_index("gx") >> k) % 2
    return ((i >> k) << (k + 1)) + (i & ((1 << k) - 1)) + ((1 - mine) << k)


def swap_bit(value, k):
    count = lax.axis_size("gx")
    return lax.ppermute(value, "gx", [(i, i ^ (1 << k)) for i in range(count)])


def image_kernel(perm_hbm, dir_hbm, schur_hbm, resid_hbm, basis_hbm, coarse_hbm, conduct_hbm,
                 image_ref, f0, f1, f2, f3, dir_ref, resid_ref, basis_ref, coarse_ref, weight_ref, rhs_ref,
                 scaled_ref, *rest):
    *send_ref, perm_ref, conduct_ref, schur_ref, sems = rest
    rows = schur_ref.shape[0] // CHUNKS
    parts = [pl.ds(i * rows, rows) for i in range(CHUNKS)]
    pairs = [(dir_hbm, dir_ref), (perm_hbm, perm_ref), (conduct_hbm, conduct_ref)]
    pairs += [(resid_hbm, resid_ref), (basis_hbm, basis_ref)]
    small = len(pairs)
    pairs += [(schur_hbm.at[part], schur_ref.at[part]) for part in parts]
    for ref in send_ref:
        pairs += [(coarse_hbm.at[other_block(i, 0)], ref.at[i]) for i in range(ref.shape[0])]
    pairs += [(coarse_hbm, coarse_ref)]
    copies = [pltpu.make_async_copy(source, target, sems.at[i]) for i, (source, target) in enumerate(pairs)]
    for copy in copies:
        copy.start()
    for copy in copies[:small]:
        copy.wait()
    early_part(perm_ref, conduct_ref, resid_ref, basis_ref, weight_ref, rhs_ref, scaled_ref)
    total = None
    for i, part in enumerate(parts):
        copies[small + i].wait()
        term = jnp.dot(dir_ref[:, part].astype(BF16), schur_ref[part], preferred_element_type=F32)
        total = term if total is None else total + term
    image_ref[...] = total
    put_faces(perm_ref, total, (f0, f1, f2, f3))
    for copy in copies[small + CHUNKS :]:
        copy.wait()


def merge_kernel(k, last, blocks_ref, got_ref, out_ref, *send_ref):
    out_ref[...] = blocks_ref[...]
    for i in range(got_ref.shape[0]):
        out_ref[other_block(i, k)] = got_ref[i]
    if not last:
        for i in range(got_ref.shape[0]):
            send_ref[0][i] = out_ref[other_block(i, k + 1)]


def join_kernel(k, depth, prim, blocks_ref, got_ref, wide_ref, all_ref):
    all_ref[...] = blocks_ref[...]
    for i in range(got_ref.shape[0]):
        all_ref[other_block(i, k)] = got_ref[i]
    slabs, rows, width = blocks_ref.shape
    width = width // 2
    for half in range(2):
        for h in range(slabs):
            at = (half * slabs + h) * width
            wide_ref[:, at : at + width] = all_ref[h, :, half * width : (half + 1) * width]
    row = lax.broadcasted_iota(jnp.int32, wide_ref.shape, 0)
    lane = lax.broadcasted_iota(jnp.int32, wide_ref.shape, 1)
    picked = jnp.logical_and(lane < slabs * width, lane % depth == prim // 2)
    wide = jnp.where(row == prim, jnp.where(picked, 1.0, 0.0), wide_ref[...].astype(F32))
    wide_ref[...] = wide.astype(BF16)


def spread_kernel(k, matrix_ref, blocks_ref, send_ref):
    slabs, rows, _ = blocks_ref.shape
    prim = matrix_ref.shape[0] // slabs
    half = prim // 2
    sectors = matrix_ref.shape[1] // prim
    width = blocks_ref.shape[2] // 2
    depth = width // sectors
    source = lax.broadcasted_iota(jnp.int32, (sectors * prim, 2 * width), 0)
    place = lax.broadcasted_iota(jnp.int32, (sectors * prim, 2 * width), 1)
    later = place // width
    within = place % width
    sector, at = within // depth, within % depth
    chosen = jnp.logical_and(at < half, source == sector * prim + later * half + at)
    spread = jnp.dot(matrix_ref[...], jnp.where(chosen, 1.0, 0.0).astype(BF16), preferred_element_type=F32)
    empty = jnp.zeros((rows - prim, 2 * width), F32)
    for g in range(slabs):
        own = jnp.concatenate([spread[g * prim : (g + 1) * prim], empty], axis=0)
        blocks_ref[g] = own.astype(BF16)
    for i in range(send_ref.shape[0]):
        send_ref[i] = blocks_ref[other_block(i, k)]


def conduct_at(row, slab):
    lane = lax.broadcasted_iota(jnp.int32, row.shape, 1)
    return jnp.sum(jnp.where(lane == slab, row, 0.0), axis=1, keepdims=True)


def early_part(perm_ref, conduct_ref, resid_ref, basis_ref, weight_ref, rhs_ref, scaled_ref):
    slab, sector = lax.axis_index("gx"), lax.axis_index("col")
    slabs, sectors = lax.axis_size("gx"), lax.axis_size("col")
    row = conduct_ref[pl.ds(sector, 1), :]
    own = conduct_at(row, slab)
    below = jnp.where(slab > 0, conduct_at(row, slab - 1), 0.0)
    above = jnp.where(slab < slabs - 1, conduct_at(row, slab + 1), 0.0)
    left = conduct_at(conduct_ref[pl.ds((sector + sectors - 1) % sectors, 1), :], slab)
    right = conduct_at(conduct_ref[pl.ds((sector + 1) % sectors, 1), :], slab)
    across = [jnp.broadcast_to(own / (own + other), (1, BLK)) for other in (below, above, left, right)]
    places = [slot_place(perm_ref, slot) for slot in range(8)]
    for b in range(weight_ref.shape[1] // BLK):
        weight = across[0]
        for slot in range(2, 8):
            weight = jnp.where(places[slot] == b, across[slot // 2], weight)
        weight_ref[:, b * BLK : (b + 1) * BLK] = jnp.broadcast_to(weight, (8, BLK))
    scaled = (weight_ref[0:1, :] * resid_ref[...]).astype(BF16)
    scaled_ref[...] = scaled
    rhs_ref[...] = lax.dot_general(
        basis_ref[...], scaled, (((1,), (1,)), ((), ())), preferred_element_type=F32
    )


def curvature_part(dir_ref, image_ref):
    curv = to_row(jnp.sum(dir_ref[...] * image_ref[...], axis=1, keepdims=True))
    high = curv.astype(BF16).astype(F32)
    return high, curv - high


def coarse_rhs_kernel(rows, sectors, perm_ref, image_ref, r0, r1, r2, r3, weight_ref, basis_ref, rhs_ref, dir_ref,
                      assembled_ref, scaled_ref, rhs_q_ref, out_ref):
    for at, part in received_blocks(perm_ref, (r0, r1, r2, r3), image_ref.shape[1] // BLK):
        assembled_ref[:, at] = image_ref[:, at] + part
    scaled = (weight_ref[0:1, :] * assembled_ref[...]).astype(BF16)
    scaled_ref[...] = scaled
    rhs_q = lax.dot_general(
        basis_ref[...], scaled, (((1,), (1,)), ((), ())), preferred_element_type=F32
    )
    rhs_q_ref[...] = rhs_q
    rhs_r = rhs_ref[...]
    half = rhs_r.shape[0] // 2
    packed = jnp.concatenate([rhs_r[:half], rhs_q[:half], rhs_r[half:], rhs_q[half:]], axis=1)
    high, low = curvature_part(dir_ref, image_ref)
    line = jnp.concatenate([high, low, jnp.zeros_like(high), jnp.zeros_like(high)], axis=1)
    packed = jnp.concatenate(
        [packed, line, jnp.zeros((rows - half - 1, BLK), F32)], axis=0
    )
    several = jnp.concatenate([packed] * sectors, axis=0).astype(BF16)
    step = several.shape[0]
    for i in range(out_ref.shape[0] // step):
        out_ref[i * step : (i + 1) * step] = several


def neumann_kernel(scaled_r_ref, scaled_q_ref, resid_ref, assembled_ref, weight_ref, neumann_hbm,
                   sol_r_ref, sol_q_ref, sums_ref, neumann_ref, sems):
    rows = neumann_ref.shape[0] // CHUNKS
    parts = [pl.ds(i * rows, rows) for i in range(CHUNKS)]
    copies = [
        pltpu.make_async_copy(neumann_hbm.at[part], neumann_ref.at[part], sems.at[i])
        for i, part in enumerate(parts)
    ]
    for copy in copies:
        copy.start()
    total_r = total_q = None
    for copy, part in zip(copies, parts):
        copy.wait()
        term_r = jnp.dot(scaled_r_ref[:, part], neumann_ref[part], preferred_element_type=F32)
        term_q = jnp.dot(scaled_q_ref[:, part], neumann_ref[part], preferred_element_type=F32)
        total_r = term_r if total_r is None else total_r + term_r
        total_q = term_q if total_q is None else total_q + term_q
    sol_r_ref[...] = total_r
    sol_q_ref[...] = total_q
    weighted_r = weight_ref[0:1, :] * resid_ref[...]
    weighted_q = weight_ref[0:1, :] * assembled_ref[...]
    n = total_r.shape[0]
    sums_ref[...] = jnp.zeros_like(sums_ref)
    for i, product in enumerate(
        (weighted_r * total_r, weighted_r * total_q + weighted_q * total_r, weighted_q * total_q)
    ):
        sums_ref[0:1, i * n : (i + 1) * n] = to_row(jnp.sum(product, axis=1, keepdims=True))


def solve_kernel(perm_ref, gathered_ref, wide_ref, prev_ref, weight_ref, basis_ref, sol_r_ref, sol_q_ref,
                 sums_ref, rhs_r_ref, rhs_q_ref, step_out, weighted_out, rz_out, f0, f1, f2, f3, rz_ref, sem):
    n = prev_ref.shape[1]
    prim = basis_ref.shape[0]
    halves = jnp.concatenate([gathered_ref[:, : 2 * n], gathered_ref[:, 2 * n :]], axis=0)
    total = jnp.dot(wide_ref[...], halves, preferred_element_type=F32)
    step = prev_ref[...] / (total[prim : prim + 1, 0:n] + total[prim : prim + 1, n : 2 * n])
    coarse_sol = (total[0:prim, 0:n] - step * total[0:prim, n : 2 * n]).astype(BF16)
    coarse_part = coarse_sol.astype(F32) * (rhs_r_ref[...] - step * rhs_q_ref[...])
    partial = (
        sums_ref[0:1, 0:n]
        - step * (sums_ref[0:1, n : 2 * n] - step * sums_ref[0:1, 2 * n : 3 * n])
        + jnp.sum(coarse_part, axis=0, keepdims=True)
    )
    partial = jnp.concatenate([partial, jnp.zeros((1, BLK - n), F32)], axis=1)
    for i in range(rz_ref.shape[0]):
        rz_ref[i] = partial
    copy = pltpu.make_async_copy(rz_ref, rz_out, sem)
    copy.start()
    correction = lax.dot_general(
        coarse_sol, basis_ref[...], (((0,), (0,)), ((), ())), preferred_element_type=F32
    )
    step_col = to_column(step)
    step_out[...] = jnp.broadcast_to(step_col, step_out.shape)
    weighted = weight_ref[0:1, :] * (sol_r_ref[...] - step_col * sol_q_ref[...] + correction)
    weighted_out[...] = weighted
    put_faces(perm_ref, weighted, (f0, f1, f2, f3))
    copy.wait()


def resid_kernel(step_ref, resid_ref, assembled_ref, out_ref):
    out_ref[...] = resid_ref[...] - step_ref[:, 0:1] * assembled_ref[...]


def direction_kernel(perm_ref, partials_ref, rz_ref, dir_ref, weighted_ref, r0, r1, r2, r3,
                     out_ref, rz_out):
    n = rz_ref.shape[1]
    rz_next = jnp.sum(partials_ref[...], axis=0)[:, 0:n]
    rz_out[...] = rz_next
    factor = to_column(rz_next / rz_ref[...])
    for at, part in received_blocks(perm_ref, (r0, r1, r2, r3), dir_ref.shape[1] // BLK):
        out_ref[:, at] = weighted_ref[:, at] + factor * dir_ref[:, at] + part


def split(value):
    high = value.astype(BF16).astype(F32)
    return high, value - high


def spread_pair_kernel(after_ref, own_ref, mate_ref, out_ref):
    slabs = lax.axis_size("gx")
    prim = own_ref.shape[0] // slabs
    half = prim // 2
    sectors = own_ref.shape[1] // prim
    width = out_ref.shape[2] // 2
    depth = width // sectors
    source = lax.broadcasted_iota(jnp.int32, (sectors * prim, 2 * width), 0)
    place = lax.broadcasted_iota(jnp.int32, (sectors * prim, 2 * width), 1)
    later = place // width
    within = place % width
    sector, at = within // depth, within % depth
    chosen = jnp.logical_and(at < half, source == sector * prim + later * half + at)
    chosen = jnp.where(chosen, 1.0, 0.0).astype(BF16)
    mine = lax.axis_index("gx") % 2
    for ref, bit in ((own_ref, mine), (mate_ref, 1 - mine)):
        out_ref[bit] = jnp.dot(ref[...], chosen, preferred_element_type=F32).astype(BF16)


def gather_kernel(k, after_ref, mine_ref, got_ref, out_ref, both_ref):
    bit = (lax.axis_index("gx") >> k) % 2
    n = mine_ref.shape[0]
    for i in range(n):
        both_ref[bit * n + i] = mine_ref[i]
        both_ref[(1 - bit) * n + i] = got_ref[i]
    out_ref[...] = jnp.concatenate([both_ref[i] for i in range(2 * n)], axis=1)


def near_rhs_kernel(rows, sectors, perm_ref, image_ref, r0, r1, r2, r3, weight_ref, basis_ref, rhs_ref, dir_ref,
                    scaled_ref, resid_ref, neumann_ref, assembled_ref, sol_r_ref, sol_q_ref, out_ref):
    for at, part in received_blocks(perm_ref, (r0, r1, r2, r3), image_ref.shape[1] // BLK):
        assembled_ref[:, at] = image_ref[:, at] + part
    weighted_r = weight_ref[0:1, :] * resid_ref[...]
    weighted_q = weight_ref[0:1, :] * assembled_ref[...]
    scaled = weighted_q.astype(BF16)
    n = scaled.shape[0]
    both = jnp.concatenate([scaled_ref[...], scaled], axis=0)
    sol = jnp.dot(both, neumann_ref[...], preferred_element_type=F32)
    rhs_q = lax.dot_general(
        basis_ref[...], scaled, (((1,), (1,)), ((), ())), preferred_element_type=F32
    )
    sol_r, sol_q = sol[:n], sol[n:]
    sol_r_ref[...] = sol_r
    sol_q_ref[...] = sol_q
    products = (weighted_r * sol_r, weighted_r * sol_q + weighted_q * sol_r, weighted_q * sol_q)
    sums = [to_row(jnp.sum(product, axis=1, keepdims=True)) for product in products]
    first = jnp.concatenate([*curvature_part(dir_ref, image_ref), *split(sums[0])], axis=1)
    second = jnp.concatenate([*split(sums[1]), *split(sums[2])], axis=1)
    rhs_r = rhs_ref[...]
    half = rhs_r.shape[0] // 2
    packed = jnp.concatenate([rhs_r[:half], rhs_q[:half], rhs_r[half:], rhs_q[half:]], axis=1)
    packed = jnp.concatenate([packed, first, second], axis=0)
    several = jnp.concatenate([packed] * sectors, axis=0).astype(BF16)
    step = several.shape[0]
    for i in range(out_ref.shape[0] // step):
        out_ref[i * step : (i + 1) * step] = several


def frame_kernel(depth, perm_ref, weight_ref, r_ref, q_ref, basis_ref, r_out, q_out, picks_ref, basis_out, f2, f3):
    weighted_r = weight_ref[0:1, :] * r_ref[...]
    weighted_q = weight_ref[0:1, :] * q_ref[...]
    r_out[...] = weighted_r
    q_out[...] = weighted_q
    prim = basis_ref.shape[0]
    n = r_ref.shape[0]
    weighted_basis = weight_ref[0:1, :] * basis_ref[...].astype(F32)
    blank = jnp.zeros((f2.shape[0] - 2 * n - prim, r_ref.shape[1]), F32)
    put_faces(perm_ref, jnp.concatenate([weighted_r, weighted_q, weighted_basis, blank], axis=0), (f2, f3), 2)
    half = prim // 2
    rows = basis_out.shape[0]
    slabs, sectors = lax.axis_size("gx"), lax.axis_size("col")
    width = sectors * depth
    row = lax.broadcasted_iota(jnp.int32, picks_ref.shape, 0)
    lane = lax.broadcasted_iota(jnp.int32, picks_ref.shape, 1)
    part = lane // width % 2
    at = lane % depth
    sums = jnp.logical_and(at >= half, row == (at - half) * 2 + part)
    mine = jnp.logical_and(lane % width // depth == lax.axis_index("col"), at < half)
    own = jnp.logical_and(mine, row == 16 + lane // (2 * width) * prim + part * half + at)
    picks_ref[...] = jnp.where(jnp.logical_or(sums, own), 1.0, 0.0).astype(BF16)
    row = lax.broadcasted_iota(jnp.int32, (rows, prim), 0)
    lane = lax.broadcasted_iota(jnp.int32, (rows, prim), 1)
    here = jnp.where(row == lax.axis_index("gx") * prim + lane, 1.0, 0.0).astype(BF16)
    basis_out[...] = jnp.dot(here, basis_ref[...], preferred_element_type=F32).astype(BF16)


def near_solve_kernel(r2, r3, perm_ref, gathered_ref, mine_ref, got_ref, picks_ref, prev_ref, weight_ref, basis_ref,
                      sol_r_ref, sol_q_ref, step_out, weighted_out, base_out, part_out, sol_out, f0, f1, rhs_ref):
    n = prev_ref.shape[1]
    slabs = lax.axis_size("gx")
    width = gathered_ref.shape[0] // slabs
    for h in range(slabs):
        part = gathered_ref[h * width : (h + 1) * width]
        rhs_ref[2 * h * width : (2 * h + 1) * width] = part[:, : 2 * n]
        rhs_ref[(2 * h + 1) * width : (2 * h + 2) * width] = part[:, 2 * n :]
    count = slabs * width
    top = (lax.axis_index("gx") * 2) // slabs
    mine = rhs_ref[pl.ds(pl.multiple_of(top * count, 16), count), :]
    got = rhs_ref[pl.ds(pl.multiple_of((1 - top) * count, 16), count), :]
    picked = jnp.dot(picks_ref[...], rhs_ref[...], preferred_element_type=F32)
    total = jnp.dot(mine_ref[...], mine, preferred_element_type=F32) + jnp.dot(
        got_ref[...], got, preferred_element_type=F32
    )
    curvature, first, second, third = (picked[i : i + 1, 0:n] + picked[i : i + 1, n : 2 * n] for i in range(4))
    step = prev_ref[...] / curvature
    sol = (total[:, 0:n] - step * total[:, n : 2 * n]).astype(BF16)
    rhs = picked[16:, 0:n] - step * picked[16:, n : 2 * n]
    sol_out[...] = sol
    high, low = split(jnp.sum(sol.astype(F32) * rhs, axis=0, keepdims=True))
    correction = lax.dot_general(
        sol, basis_ref[...], (((0,), (0,)), ((), ())), preferred_element_type=F32
    )
    step_col = to_column(step)
    step_out[...] = jnp.broadcast_to(step_col, step_out.shape)
    weighted = sol_r_ref[...] - step_col * sol_q_ref[...] + weight_ref[0:1, :] * correction
    weighted_out[...] = weighted
    blank = jnp.zeros((1, BLK - n), F32)
    low = low.astype(BF16).astype(F32)
    base = first - step * (second - step * third)
    base_out[...] = jnp.broadcast_to(jnp.concatenate([base, blank], axis=1), base_out.shape)
    part_out[...] = jnp.broadcast_to(jnp.concatenate([high + low, blank], axis=1), part_out.shape)
    put_faces(perm_ref, weighted, (f0, f1))
    lines = jnp.concatenate([high, low, jnp.zeros((14, n), F32)], axis=0)
    lines = jnp.concatenate([lines, jnp.zeros((16, 2 * BLK - n), F32)], axis=1).astype(BF16)
    f0[n : n + 16, :] = lines
    f1[n : n + 16, :] = lines


def beside_kernel(perm_ref, sol_ref, step_ref, weighted_ref, r2, r3, out_ref):
    n = weighted_ref.shape[0]
    slab, slabs = lax.axis_index("gx"), lax.axis_size("gx")
    prim = sol_ref.shape[0] // slabs
    received = []
    for got, other in ((r2, jnp.where(slab % 2 == 1, slab + 1, slab - 1)), (r3, slab + 1 - 2 * (slab % 2))):
        rows = got.shape[0] - 2 * n
        row = lax.broadcasted_iota(jnp.int32, (rows, sol_ref.shape[0]), 0)
        lane = lax.broadcasted_iota(jnp.int32, (rows, sol_ref.shape[0]), 1)
        chosen = jnp.logical_and(row < prim, lane == other * prim + row)
        sol = jnp.dot(jnp.where(chosen, 1.0, 0.0).astype(BF16), sol_ref[...], preferred_element_type=F32)
        correction = lax.dot_general(
            sol.astype(BF16), got[2 * n :, :], (((0,), (0,)), ((), ())), preferred_element_type=F32
        )
        step = step_ref[:, 0:1]
        received.append(got[0:n, :].astype(F32) - step * got[n : 2 * n, :].astype(F32) + correction)
    for at, part in some_received_blocks(perm_ref, received, weighted_ref.shape[1] // BLK, 2):
        out_ref[:, at] = weighted_ref[:, at] + part


def near_direction_kernel(perm_ref, rz_ref, dir_ref, weighted_ref, base_ref, part_ref, far_ref, r0, r1,
                          out_ref, rz_out):
    n = rz_ref.shape[1]
    sector = lax.axis_index("col")
    beside = jnp.where(sector % 2 == 1, (sector + 1) % 4, (sector + 3) % 4)
    parts = [(sector, part_ref[0:1, 0:n]), (sector ^ 2, far_ref[0:1, 0:n])]
    for ref, other in ((r0, beside), (r1, sector ^ 1)):
        lines = ref[n : n + 16, 0:n].astype(F32)
        parts.append((other, lines[0:1] + lines[1:2]))
    rz_next = base_ref[0:1, 0:n]
    for at in range(4):
        value = parts[0][1]
        for other, part in parts[1:]:
            value = jnp.where(other == at, part, value)
        rz_next = rz_next + value
    rz_out[...] = rz_next
    factor = to_column(rz_next / rz_ref[...])
    received = (r0[0:n, :], r1[0:n, :])
    for at, part in some_received_blocks(perm_ref, received, dir_ref.shape[1] // BLK, 0):
        out_ref[:, at] = weighted_ref[:, at] + factor * dir_ref[:, at] + part


def near_rest(perm, rz_row, neumann, image, received, weight, rhs_r, scaled_r, direction, resid, basis_t,
              coarse, rows):
    rhs, width = resid.shape
    prim = basis_t.shape[0]
    slabs, sectors = lax.axis_size("gx"), lax.axis_size("col")
    vmem = pl.BlockSpec(memory_space=VMEM)
    full = jax.ShapeDtypeStruct((rhs, width), F32)
    line = jax.ShapeDtypeStruct((8, BLK), F32)
    small = cost(1 << 10, 1 << 16)

    def call(kernel, outs, *args, scratch=(), estimate=small, after=()):
        return pl.pallas_call(
            kernel, out_shape=outs, in_specs=[pl.BlockSpec(memory_space=pl.ANY)] * len(after) + [vmem] * len(args),
            out_specs=(vmem,) * len(outs), scratch_shapes=scratch, compiler_params=params(), cost_estimate=estimate,
        )(*after, *args)

    mate = swap_bit(coarse, 0)
    flat = (slabs * prim, sectors * prim)
    shard = (slabs * prim, 2 * sectors * rows)
    (blocks,) = call(
        spread_pair_kernel, (jax.ShapeDtypeStruct((2,) + shard, BF16),),
        coarse.reshape(flat), mate.reshape(flat), after=(perm,),
        estimate=cost(2000 * rhs * width * width, 1 << 16),
    )
    assembled, sol_r, sol_q, packed = call(
        functools.partial(near_rhs_kernel, rows, sectors),
        (full, full, full, jax.ShapeDtypeStruct((slabs * sectors * rows, BLK), BF16)),
        perm, image, *received, weight, basis_t, rhs_r, direction, scaled_r, resid, neumann,
        estimate=cost(2000 * rhs * width * width, 1 << 16),
    )
    (blocks,) = call(
        functools.partial(gather_kernel, 1), (jax.ShapeDtypeStruct((shard[0], 4 * shard[1]), BF16),),
        blocks, swap_bit(blocks, 1), after=(packed,), scratch=[pltpu.VMEM((4,) + shard, BF16)],
        estimate=cost(2000 * rhs * width * width, 1 << 16),
    )
    got = swap_bit(blocks, 2)
    packed = packed.reshape(slabs * sectors, rows // 2, 2, BLK)
    gathered = lax.all_to_all(packed, ("gx", "col"), 0, 0).reshape(slabs * sectors * rows, BLK)
    face = jax.ShapeDtypeStruct((-(-(2 * rhs + prim) // 16) * 16, 2 * BLK), BF16)
    sol_r, sol_q, picks, placed, f2, f3 = call(
        functools.partial(frame_kernel, rows),
        (
            full,
            full,
            jax.ShapeDtypeStruct((16 + slabs * prim, slabs * shard[1]), BF16),
            jax.ShapeDtypeStruct((slabs * prim, width), BF16),
            face,
            face,
        ),
        perm, weight, sol_r, sol_q, basis_t,
    )
    r2, r3 = swap_faces((f2, f3), 2)
    tall = jax.ShapeDtypeStruct((rhs + 16, 2 * BLK), BF16)
    step, weighted, base, part, sol, f0, f1 = call(
        near_solve_kernel,
        (
            jax.ShapeDtypeStruct((rhs, BLK), F32),
            full,
            line,
            jax.ShapeDtypeStruct((8, BLK), F32),
            jax.ShapeDtypeStruct((slabs * prim, rhs), BF16),
            jax.ShapeDtypeStruct((64, 2 * BLK), BF16),
            jax.ShapeDtypeStruct((48, 2 * BLK), BF16),
        ),
        perm, gathered, blocks, got, picks, rz_row, weight, placed, sol_r, sol_q,
        scratch=[pltpu.VMEM((slabs * shard[1], 2 * rhs), BF16)], after=(r2, r3),
    )
    far = lax.ppermute(part, "col", [(i, i ^ 2) for i in range(sectors)])
    r0, r1 = swap_faces((f0, f1))
    (weighted,) = call(beside_kernel, (full,), perm, sol, step, weighted, r2, r3)
    (resid_new,) = call(resid_kernel, (full,), step, resid, assembled)
    direction_new, rz_next = call(
        near_direction_kernel, (full, jax.ShapeDtypeStruct((1, rhs), F32)),
        perm, rz_row, direction, weighted, base, part, far, r0, r1,
    )
    return (resid_new[None, None], direction_new[None, None], rz_next[0])


def body(resid, direction, rz_prev, schur, neumann, basis, coarse_inv, conduct, face_perm):
    resid, direction, schur, neumann = resid[0, 0], direction[0, 0], schur[0, 0], neumann[0, 0]
    basis_t = basis[0, 0].T
    perm = face_perm[0]
    rhs, width = resid.shape
    prim = basis_t.shape[0]
    slabs, sectors = lax.axis_size("gx"), lax.axis_size("col")
    rows = -(-(prim // 2 + 1) // 4) * 4
    block_rows = -(-(prim + 1) // 16) * 16
    rounds = slabs.bit_length() - 1
    face = jax.ShapeDtypeStruct((rhs, 2 * BLK), BF16)
    full = jax.ShapeDtypeStruct((rhs, width), F32)
    rz_row = rz_prev[None, :]
    vmem = pl.BlockSpec(memory_space=VMEM)
    hbm = pl.BlockSpec(memory_space=pltpu.HBM)
    anywhere = pl.BlockSpec(memory_space=pl.ANY)
    flops = 2 * rhs * width * width
    coarse = coarse_inv[0, :, :, 0]
    coarse_type = jax.ShapeDtypeStruct(coarse.shape, BF16)
    send_type = jax.ShapeDtypeStruct((slabs // 2,) + coarse.shape[1:], BF16)
    blocks_type = jax.ShapeDtypeStruct((slabs, block_rows, 2 * sectors * rows), BF16)

    near = sectors == 4 and slabs == 8
    sends = () if near else (send_type,)
    fetched = [pltpu.with_memory_space_constraint(x, pltpu.HBM) for x in (perm, direction, schur, resid, basis_t, coarse, conduct.T)]
    image, f0, f1, f2, f3, direction, resid, basis_t, coarse, weight, rhs_r, scaled_r, *send = pl.pallas_call(
        image_kernel,
        out_shape=(full,) + (face,) * 4
        + (full, full, jax.ShapeDtypeStruct((prim, width), BF16), coarse_type)
        + (
            jax.ShapeDtypeStruct((8, width), F32),
            jax.ShapeDtypeStruct((prim, rhs), F32),
            jax.ShapeDtypeStruct((rhs, width), BF16),
        )
        + sends,
        in_specs=[hbm] * 7, out_specs=(vmem,) * (12 + len(sends)),
        scratch_shapes=[
            pltpu.VMEM(perm.shape, jnp.int32),
            pltpu.VMEM((sectors, slabs), F32),
            pltpu.VMEM((width, width), BF16),
            pltpu.SemaphoreType.DMA((CHUNKS + 6 + len(sends) * (slabs // 2),)),
        ],
        compiler_params=params(), cost_estimate=cost(flops, 2 * width * width),
    )(*fetched)
    received = swap_faces((f0, f1, f2, f3))
    if near:
        return near_rest(perm, rz_row, neumann, image, received, weight, rhs_r, scaled_r, direction, resid,
                         basis_t, coarse, rows)
    send = send[0]
    for k in range(rounds - 1):
        got = swap_bit(send, k)
        last = k + 2 == rounds
        coarse, *send = pl.pallas_call(
            functools.partial(merge_kernel, k, last),
            out_shape=(coarse_type,) if last else (coarse_type, send_type),
            in_specs=[vmem] * 2, out_specs=(vmem,) if last else (vmem,) * 2,
            compiler_params=params(), cost_estimate=cost(1 << 10, 1 << 16),
        )(coarse, got)
        send = send[0] if send else None
    blocks, send = pl.pallas_call(
        functools.partial(spread_kernel, rounds - 1),
        out_shape=(blocks_type, jax.ShapeDtypeStruct((slabs // 2,) + blocks_type.shape[1:], BF16)),
        in_specs=[vmem], out_specs=(vmem,) * 2,
        compiler_params=params(), cost_estimate=cost(1 << 20, 1 << 16),
    )(coarse.reshape(slabs * prim, sectors * prim))
    wide = pl.pallas_call(
        functools.partial(join_kernel, rounds - 1, rows, prim),
        out_shape=jax.ShapeDtypeStruct((block_rows, slabs * blocks_type.shape[2]), BF16),
        in_specs=[vmem] * 2, out_specs=vmem,
        scratch_shapes=[pltpu.VMEM(blocks_type.shape, BF16)],
        compiler_params=params(), cost_estimate=cost(1 << 10, 1 << 16),
    )(blocks, swap_bit(send, rounds - 1))
    assembled, scaled_q, rhs_q, packed = pl.pallas_call(
        functools.partial(coarse_rhs_kernel, rows, sectors),
        out_shape=(
            full,
            jax.ShapeDtypeStruct((rhs, width), BF16),
            jax.ShapeDtypeStruct((prim, rhs), F32),
            jax.ShapeDtypeStruct((slabs * sectors * rows, BLK), BF16),
        ),
        in_specs=[vmem] + [vmem] * 9, out_specs=(vmem,) * 4, compiler_params=params(),
        cost_estimate=cost(2 * rhs * width * prim, 8 * rhs * width),
    )(perm, image, *received, weight, basis_t, rhs_r, direction)
    packed = packed.reshape(slabs * sectors, rows // 2, 2, BLK)
    gathered = lax.all_to_all(packed, ("gx", "col"), 0, 0).reshape(slabs * sectors * rows, BLK)
    sol_r, sol_q, sums = pl.pallas_call(
        neumann_kernel,
        out_shape=(full, full, jax.ShapeDtypeStruct((8, BLK), F32)),
        in_specs=[vmem] * 5 + [hbm], out_specs=(vmem,) * 3,
        scratch_shapes=[pltpu.VMEM((width, width), BF16), pltpu.SemaphoreType.DMA((CHUNKS,))],
        compiler_params=params(), cost_estimate=cost(1000 * flops, 2 * width * width),
    )(scaled_r, scaled_q, resid, assembled, weight, pltpu.with_memory_space_constraint(neumann, pltpu.HBM))
    step, weighted, partial, *faces = pl.pallas_call(
        solve_kernel,
        out_shape=(
            jax.ShapeDtypeStruct((rhs, BLK), F32),
            full,
            jax.ShapeDtypeStruct((slabs * sectors, 1, BLK), F32),
        )
        + (face,) * 4,
        in_specs=[vmem] * 11, out_specs=(vmem, vmem, anywhere) + (vmem,) * 4,
        scratch_shapes=[pltpu.VMEM((slabs * sectors, 1, BLK), F32), pltpu.SemaphoreType.DMA],
        compiler_params=params(), cost_estimate=cost(2 * rhs * width * prim, 8 * rhs * width),
    )(perm, gathered, wide, rz_row, weight, basis_t, sol_r, sol_q, sums, rhs_r, rhs_q)
    partials = lax.all_to_all(partial, ("gx", "col"), 0, 0)
    received = swap_faces(faces)
    resid_new = pl.pallas_call(
        resid_kernel, out_shape=full, in_specs=[vmem] * 3, out_specs=vmem,
        compiler_params=params(), cost_estimate=cost(2 * rhs * width, 12 * rhs * width),
    )(step, resid, assembled)
    direction_new, rz_next = pl.pallas_call(
        direction_kernel, out_shape=(full, jax.ShapeDtypeStruct((1, rhs), F32)),
        in_specs=[vmem] + [vmem] * 8, out_specs=(vmem,) * 2, compiler_params=params(),
        cost_estimate=cost(2 * rhs * width, 8 * rhs * width),
    )(perm, partials, rz_row, direction, weighted, *received)
    return (resid_new[None, None], direction_new[None, None], rz_next[0])


def solution(mesh):
    placed = (
        P("gx", "col", None, None),
        P("gx", "col", None, None),
        P(),
        P("gx", "col", None, None),
        P("gx", "col", None, None),
        P("gx", "col", None, None),
        P("col", None, None, "gx", None, None),
        P(),
        P("gx", "col", None),
    )
    return jax.shard_map(
        body,
        mesh=mesh,
        in_specs=placed,
        out_specs=(P("gx", "col", None, None), P("gx", "col", None, None), P()),
        check_vma=False,
    )
```
